128 devices in a mesh: row: 8 (over z_lo, x), col: 16 (over y, z_hi, core).
Axes of the slice: x: 4, y: 4, z: 4 (z_hi: 2, z_lo: 2; z = z_hi * 2 + z_lo), core: 2. Of those that a mesh axis runs over, the one named last changes fastest.
Arguments:
- three_centre: bfloat16 [64, 2048, 2048], P('row', 'col'), may hold values from -6 to 6
- green_virt: bfloat16 [2048, 2048], P(('row', 'col')), may hold values from -0.25 to 0.25
- green_occ: bfloat16 [2048, 2048], P(('row', 'col')), may hold values from -0.25 to 0.25
- pattern: int32 [64, 64], replicated, may hold values 0 or 1
- block_sizes: int32 [64], replicated, may hold values from 8 to 32
- atom_order: int32 [64], replicated, may hold values from 0 to 63, each once
Outputs:
- projected: bfloat16 [2048, 64, 2048], P('row', None, 'col')
The draws below stay inside these ranges and needn't reach their ends.
Inputs may be any that keep to these rules, and one draw needn't show every extreme that they name: `atom_order`: each atom index appears exactly once.
All inputs are finite; a program needn't handle non-finite values.
Results may differ from the reference program's by a relative error of at most 0.0049.
Values may be sent and summed in bfloat16 or wider, within the bound.
A program may use at most 128 MiB of HBM per device.

```python
import jax
import jax.numpy as jnp
from jax import lax

BLK = 32
ATOMS = 64
ORB = 2048
NP = 64


def with_ends(entries, rng, least, largest):
    extent = entries.shape
    place = [jax.random.randint(jax.random.fold_in(rng, axis), (), 0, extent[axis]) for axis in range(len(extent))]
    entries = entries.at[tuple(place)].set(least)
    longest = extent.index(max(extent))
    place[longest] = (place[longest] + 1) % extent[longest]
    return entries.at[tuple(place)].set(largest)


def steps_of(rng, extent, shards, low, largest):
    gain = 1.0
    for dim, parts in shards:
        draws = jax.random.uniform(jax.random.fold_in(jax.random.fold_in(rng, 6), dim), (parts,), jnp.float32, low / len(shards), largest / len(shards))
        gain = gain * jnp.repeat(jnp.exp(draws), extent[dim] // parts).reshape((-1,) + (1,) * (len(extent) - 1 - dim))
    return gain


def bell_draw(own_key, dims, deviation, reach, pieces=(), kind=jnp.bfloat16):
    drawn = deviation * jax.random.normal(own_key, dims, jnp.float32)
    if pieces:
        drawn = drawn * steps_of(own_key, dims, pieces, -0.22, 0.18)
    return jnp.clip(drawn, -reach, reach).astype(kind)


def setup_inputs(seed: int = 0) -> dict:
    key_list = jax.random.split(jax.random.key(seed), 7)
    return {
        "three_centre": bell_draw(key_list[0], (NP, ORB, ORB), 1.0, 6.0, ((0, 8), (1, 16))),
        "green_virt": bell_draw(key_list[1], (ORB, ORB), (ORB // 4) ** -0.5, 0.25, ((0, 128),)),
        "green_occ": bell_draw(key_list[2], (ORB, ORB), (ORB // 4) ** -0.5, 0.25, ((0, 128),)),
        "pattern": with_ends((jax.random.randint(key_list[3], (ATOMS, ATOMS), 0, 3) < 2).astype(jnp.int32), jax.random.fold_in(key_list[3], 1), 0, 1),
        "block_sizes": with_ends(jax.random.randint(key_list[4], (ATOMS,), BLK // 4, BLK + 1), jax.random.fold_in(key_list[4], 1), BLK // 4, BLK).astype(jnp.int32),
        "atom_order": jax.random.permutation(key_list[5], ATOMS).astype(jnp.int32),
    }


def reference(three_centre, green_virt, green_occ, pattern, block_sizes, atom_order):
    usable = (lax.broadcasted_iota(jnp.int32, (ATOMS, BLK), 1) < block_sizes[:, None]).reshape(-1)
    paired = jnp.repeat(jnp.repeat(pattern > 0, BLK, axis=0), BLK, axis=1)
    kept_mask = paired & usable[:, None] & usable[None, :]
    slot_ids = jnp.arange(BLK, dtype=jnp.int32)
    columns_order = (atom_order[:, None] * BLK + slot_ids[None, :]).reshape(-1).astype(jnp.int32)
    permuted = jnp.take(green_virt, columns_order, axis=1)
    occ_turned = green_occ.T

    def one_slab(tensor_rows):
        filtered = jnp.where(kept_mask, tensor_rows, jnp.zeros((), tensor_rows.dtype))
        half_done = jnp.dot(filtered, permuted, preferred_element_type=jnp.float32).astype(jnp.bfloat16)
        return jnp.dot(occ_turned, half_done, preferred_element_type=jnp.float32).astype(jnp.bfloat16)

    stacked = lax.map(one_slab, three_centre)
    return jnp.transpose(stacked, (1, 0, 2))
```

```python
import jax
import jax.numpy as jnp
from jax import lax
from jax.experimental import pallas as pl
from jax.experimental.pallas import tpu as pltpu
from jax.sharding import PartitionSpec as P

MESH = pl.DeviceIdType.MESH
BF = jnp.bfloat16
F32 = jnp.float32
NC = 4
PARTS = ((0, 3), (3, 3), (6, 2))
ORDERS = ("xyz", "yzx", "zxy")


def me():
    r = lax.axis_index("row")
    c = lax.axis_index("col")
    return {
        "x": lax.rem(r, 4),
        "y": c // 4,
        "z": lax.rem(c // 2, 2) * 2 + r // 4,
        "k": lax.rem(c, 2),
    }


def device(p):
    return {"row": lax.rem(p["z"], 2) * 4 + p["x"], "col": (p["y"] * 2 + p["z"] // 2) * 2 + p["k"]}


def moved(p, **by):
    q = dict(p)
    for axis, d in by.items():
        q[axis] = lax.rem(p[axis] + d, 2) if axis == "k" else lax.rem(p[axis] + d + 4, 4)
    return q


def flip(p, axis):
    q = dict(p)
    q[axis] = p[axis] + 1 - 2 * lax.rem(p[axis], 2)
    return q


def partners(p):
    found = []
    for axis in "xyz":
        for d in (1, 2, 3):
            for e in (0, 1):
                found.append(moved(p, **{axis: d, "k": e}))
    found.append(moved(p, k=1))
    for d in (1, 2, 3):
        found.append(moved(p, y=d, z=2))
        found.append(flip(moved(p, x=d), "z"))
    found.append(flip(moved(p, z=2, k=1), "y"))
    found.append(flip(moved(p, y=2), "z"))
    return found


def kernel(gv, go, order, sizes, pattern, t_hbm, out,
           turned, gp, gvb, t2, mask, hs, hr, gst, got, ss,
           t_sem, own_sem, ts_sem, tr_sem, v1s, v1r, v2s, v2r, v3s, v3r,
           o1s, o1r, o2s, o2r, o3s, o3r, o4s, o4r, hss, hrs, hl, sss, srs, sl):
    p = me()
    x, y, z, k = p["x"], p["y"], p["z"], p["k"]
    zl, zh, yl, yh = lax.rem(z, 2), z // 2, lax.rem(y, 2), y // 2
    row, col = lax.axis_index("row"), lax.axis_index("col")

    def remote(src, dst, send, recv, to):
        return pltpu.make_async_remote_copy(
            src_ref=src, dst_ref=dst, send_sem=send, recv_sem=recv, device_id=device(to), device_id_type=MESH
        )

    def t_load(c):
        two = pl.ds(c * 2, 2)
        return pltpu.make_async_copy(t_hbm.at[two], t2.at[two, k], t_sem.at[c])

    for c in range(NC):
        t_load(c).start()

    barrier = pltpu.get_barrier_semaphore()
    peers = partners(p)
    for q in peers:
        pl.semaphore_signal(barrier, inc=1, device_id=device(q), device_id_type=MESH)

    lane_slot = lax.broadcasted_iota(jnp.int32, (16, 128), 1) // 32
    for b in range(16):
        source = gv[:, b * 128:(b + 1) * 128].astype(F32)
        for t in range(4):
            turned[t, b] = pltpu.roll(source, t * 32, 1) if t else source

    def permute(j, carry):
        wanted = jnp.zeros((16, 128), jnp.int32)
        for s in range(4):
            wanted = jnp.where(lane_slot == s, order[4 * j + s], wanted)
        block = jnp.zeros((16, 128), F32)
        for t in range(4):
            first_atom = wanted - lax.rem(lane_slot - t + 4, 4)
            for b in range(16):
                block = jnp.where(first_atom == 4 * b, turned[t, b], block)
        gp[lax.rem(j, 2), j // 2] = block.astype(BF)
        return carry

    lax.fori_loop(0, 16, permute, 0)

    def rows16(core):
        return pl.ds(pl.multiple_of(core * 16, 16), 16)

    own = pltpu.make_async_copy(gp.at[k], gvb.at[:, zl, x, y, zh, rows16(k)], own_sem.at[0])
    own.start()
    own_o = pltpu.make_async_copy(
        go.at[:, pl.ds(pl.multiple_of(k * 1024, 1024), 1024)], gst.at[yl * 4 + zh * 2 + k], own_sem.at[1]
    )
    own_o.start()

    pl.semaphore_wait(barrier, len(peers))

    def v1(part, d, e, mine):
        k0, nk = PARTS[part]
        axis = ORDERS[part][0]
        to = moved(p, **{axis: d, "k": e})
        frm = p if mine else moved(p, **{axis: -d, "k": e})
        dst = gvb.at[pl.ds(k0, nk), lax.rem(frm["z"], 2), frm["x"], frm["y"], frm["z"] // 2, rows16(frm["k"])]
        return remote(gp.at[to["k"], pl.ds(k0, nk)], dst, v1s.at[part, d - 1, e], v1r.at[part, d - 1, e], to)

    def v1_sibling(mine):
        frm = p if mine else moved(p, k=1)
        return remote(
            gp.at[1 - k], gvb.at[:, zl, x, y, zh, rows16(frm["k"])], v1s.at[3, 0, 0], v1r.at[3, 0, 0], moved(p, k=1)
        )

    v1_sibling(True).start()
    for d in (1, 3, 2):
        for part in range(3):
            for e in (0, 1):
                v1(part, d, e, True).start()

    def o1(a, b, e, mine):
        to = moved(p, z=2 * b, k=e)
        if a:
            to = flip(to, "y")
        frm = p if mine else to
        half = pl.ds(pl.multiple_of(to["k"] * 1024, 1024), 1024)
        slot = lax.rem(frm["y"], 2) * 4 + (frm["z"] // 2) * 2 + frm["k"]
        return remote(go.at[:, half], gst.at[slot], o1s.at[a, b, e], o1r.at[a, b, e], to)

    group = [(a, b, e) for a in (0, 1) for b in (0, 1) for e in (0, 1) if a or b or e]
    for abe in group:
        o1(*abe, True).start()

    atom_of_row = lax.broadcasted_iota(jnp.int32, (128, 64), 0) // 32 + col * 4
    pick = (lax.broadcasted_iota(jnp.int32, (128, 64), 1) == atom_of_row).astype(F32)
    spread = (
        lax.broadcasted_iota(jnp.int32, (64, 2048), 1) // 32 == lax.broadcasted_iota(jnp.int32, (64, 2048), 0)
    ).astype(BF)
    size_row = sizes[...].astype(F32)
    own_size = jnp.sum(pick * size_row, axis=1, keepdims=True)
    row_ok = lax.rem(lax.broadcasted_iota(jnp.int32, (128, 1), 0), 32).astype(F32) < own_size
    paired = jnp.dot(pick.astype(BF), pattern[...].astype(F32).astype(BF), preferred_element_type=F32)
    paired = jnp.where(row_ok, paired, 0.0)
    paired = jnp.dot(paired.astype(BF), spread, preferred_element_type=F32)
    all_sizes = jnp.dot(jnp.broadcast_to(size_row, (8, 64)).astype(BF), spread, preferred_element_type=F32)[0:1]
    column_ok = lax.rem(lax.broadcasted_iota(jnp.int32, (1, 2048), 1), 32).astype(F32) < all_sizes
    mask[...] = jnp.where(column_ok, paired, 0.0).astype(BF)

    def t_share(c, mine):
        part = t2.at[pl.ds(c * 2, 2), k if mine else 1 - k]
        return remote(part, part, ts_sem.at[c], tr_sem.at[c], moved(p, k=1))

    def filter_chunk(c, carry):
        t_load(c).wait()

        def strip(i, inner):
            rows = pl.ds(pl.multiple_of(i * 16, 16), 16)
            m = mask[rows, :]
            for q in range(2):
                t2[c * 2 + q, k, rows, :] = t2[c * 2 + q, k, rows, :] * m
            return inner

        lax.fori_loop(0, 8, strip, 0)
        t_share(c, True).start()
        return carry

    lax.fori_loop(0, NC, filter_chunk, 0)

    def v_slot(part, at, full):
        k0, nk = PARTS[part]
        every = slice(None)
        return gvb.at[
            pl.ds(k0, nk),
            every if "z" in full else lax.rem(at["z"], 2),
            every if "x" in full else at["x"],
            every if "y" in full else at["y"],
            every if "z" in full else at["z"] // 2,
        ]

    def v23(step, part, d, mine):
        axis = ORDERS[part][step]
        slot = v_slot(part, p if mine else moved(p, **{axis: -d}), ORDERS[part][:step])
        s, r = ((v2s, v2r), (v3s, v3r))[step - 1]
        return remote(slot, slot, s.at[part, d - 1], r.at[part, d - 1], moved(p, **{axis: d}))

    own.wait()
    v1_sibling(False).wait_recv()
    for part in range(3):
        for d in (1, 2, 3):
            for e in (0, 1):
                v1(part, d, e, False).wait_recv()
        for d in (1, 3, 2):
            v23(1, part, d, True).start()

    own_o.wait()
    for abe in group:
        o1(*abe, False).wait_recv()
    got[zl, x, yh, k] = gst[...].reshape(128, 1024).T

    def o2(a, b, mine):
        to = moved(p, y=2 * a)
        if b:
            to = flip(to, "z")
        frm = p if mine else to
        slot = got.at[lax.rem(frm["z"], 2), x, frm["y"] // 2, k]
        return remote(slot, slot, o2s.at[a, b], o2r.at[a, b], to)

    for part in range(3):
        for d in (1, 2, 3):
            v23(1, part, d, False).wait_recv()
        for d in (1, 3, 2):
            v23(2, part, d, True).start()

    trio = ((0, 1), (1, 0), (1, 1))
    for ab in trio:
        o2(*ab, True).start()

    def o3(d, mine):
        slot = got.at[:, x if mine else moved(p, x=-d)["x"], :, k]
        return remote(slot, slot, o3s.at[d - 1], o3r.at[d - 1], moved(p, x=d))

    def o4(d, mine):
        slot = got.at[:, moved(p, x=-d)["x"], :, k if mine else 1 - k]
        return remote(slot, slot, o4s.at[d], o4r.at[d], moved(p, k=1))

    for ab in trio:
        o2(*ab, False).wait_recv()
    for d in (1, 3, 2):
        o3(d, True).start()
    o4(0, True).start()

    for c in range(NC):
        t_share(c, False).wait_recv()
    for part in range(3):
        for d in (1, 2, 3):
            v23(2, part, d, False).wait_recv()

    def h_copy(c, s, e, mine):
        to = moved(p, y=s, z=2 * e)
        frm = p if mine else moved(p, y=-s, z=2 * e)
        return remote(
            hs.at[c, to["y"] * 2 + to["z"] // 2],
            hr.at[c, :, frm["y"] * 2 + frm["z"] // 2],
            hss.at[c, s, e], hrs.at[c, s, e], to,
        )

    def h_own(c):
        chip = y * 2 + zh
        return pltpu.make_async_copy(hs.at[c, chip], hr.at[c, :, chip], hl.at[c])

    def first(i, carry):
        c, s = i // 4, lax.rem(i, 4)
        pair = lax.rem(y + s, 4) * 2
        rhs = jnp.concatenate([gvb[pair + q].reshape(2048, 128) for q in range(2)], axis=1)
        lhs = t2[pl.ds(c * 2, 2)].reshape(512, 2048)
        h = jnp.dot(lhs, rhs, preferred_element_type=F32).astype(BF)
        for q in range(2):
            hs[c, pair + q] = h[:, q * 128:(q + 1) * 128].reshape(2, 256, 128)
        h_copy(c, s, 1, True).start()

        @pl.when(s == 0)
        def _():
            h_own(c).start()

        @pl.when(s > 0)
        def _():
            h_copy(c, s, 0, True).start()

        return carry

    lax.fori_loop(0, NC * 4, first, 0)

    for d in (1, 3, 2):
        o3(d, False).wait_recv()
        o4(d, True).start()
    for d in range(4):
        o4(d, False).wait_recv()

    def s_copy(c, d, e, mine):
        to = moved(p, x=d)
        frm = p if mine else moved(p, x=-d)
        if e:
            to = flip(to, "z")
            if not mine:
                frm = flip(frm, "z")
        frm_row = lax.rem(frm["z"], 2) * 4 + frm["x"]
        return remote(ss.at[c, d, e], out.at[pl.ds(frm_row * 8 + c * 2, 2)], sss.at[c, d, e], srs.at[c, d, e], to)

    def s_own(c):
        return pltpu.make_async_copy(ss.at[c, 0, 0], out.at[pl.ds(row * 8 + c * 2, 2)], sl.at[c])

    def second(c, carry):
        h_own(c).wait()
        h_copy(c, 0, 1, False).wait_recv()
        for s in (1, 2, 3):
            for e in (0, 1):
                h_copy(c, s, e, False).wait_recv()

        def tile(d, inner):
            rows = pl.ds(pl.multiple_of(lax.rem(x + d, 4) * 256, 256), 256)
            lhs = jnp.concatenate(
                [
                    jnp.concatenate(
                        [
                            got[b // 8, lax.rem(b // 2, 4), lax.rem(b, 2), zl if e == 0 else 1 - zl, rows, :]
                            for b in range(16)
                        ],
                        axis=1,
                    )
                    for e in (0, 1)
                ],
                axis=0,
            )
            rhs = jnp.concatenate([hr[c, q].reshape(2048, 128) for q in range(2)], axis=1)
            r = jnp.dot(lhs, rhs, preferred_element_type=F32).astype(BF)
            for e in (0, 1):
                for q in range(2):
                    ss[c, d, e, q] = r[e * 256:(e + 1) * 256, q * 128:(q + 1) * 128]
            s_copy(c, d, 1, True).start()

            @pl.when(d == 0)
            def _():
                s_own(c).start()

            @pl.when(d > 0)
            def _():
                s_copy(c, d, 0, True).start()

            return inner

        lax.fori_loop(0, 4, tile, 0)
        return carry

    lax.fori_loop(0, NC, second, 0)

    v1_sibling(True).wait_send()
    for part in range(3):
        for d in (1, 2, 3):
            for e in (0, 1):
                v1(part, d, e, True).wait_send()
            v23(1, part, d, True).wait_send()
            v23(2, part, d, True).wait_send()
    for abe in group:
        o1(*abe, True).wait_send()
    for ab in trio:
        o2(*ab, True).wait_send()
    for d in (1, 2, 3):
        o3(d, True).wait_send()
    for d in range(4):
        o4(d, True).wait_send()

    def drain(c, carry):
        t_share(c, True).wait_send()
        s_own(c).wait()
        for s in range(4):
            for e in (0, 1):
                if s or e:
                    h_copy(c, s, e, True).wait_send()
                    s_copy(c, s, e, True).wait_send()
                    s_copy(c, s, e, False).wait_recv()
        return carry

    lax.fori_loop(0, NC, drain, 0)


def per_device(three_centre, green_virt, green_occ, pattern, block_sizes, atom_order):
    vmem = pl.BlockSpec(memory_space=pltpu.VMEM)
    dma = pltpu.SemaphoreType.DMA
    blocks = pl.pallas_call(
        kernel,
        out_shape=jax.ShapeDtypeStruct((64, 256, 128), BF),
        in_specs=[vmem, vmem, pl.BlockSpec(memory_space=pltpu.SMEM), vmem, vmem, pl.BlockSpec(memory_space=pl.ANY)],
        out_specs=pl.BlockSpec(memory_space=pl.ANY),
        scratch_shapes=[
            pltpu.VMEM((4, 16, 16, 128), F32),
            pltpu.VMEM((2, 8, 16, 128), BF),
            pltpu.VMEM((8, 2, 4, 4, 2, 32, 128), BF),
            pltpu.VMEM((8, 2, 128, 2048), BF),
            pltpu.VMEM((128, 2048), BF),
            pltpu.VMEM((NC, 8, 2, 256, 128), BF),
            pltpu.VMEM((NC, 2, 8, 256, 128), BF),
            pltpu.VMEM((8, 16, 1024), BF),
            pltpu.VMEM((2, 4, 2, 2, 1024, 128), BF),
            pltpu.VMEM((NC, 4, 2, 2, 256, 128), BF),
            dma((NC,)), dma((2,)), dma((NC,)), dma((NC,)),
            dma((4, 3, 2)), dma((4, 3, 2)), dma((3, 3)), dma((3, 3)), dma((3, 3)), dma((3, 3)),
            dma((2, 2, 2)), dma((2, 2, 2)), dma((2, 2)), dma((2, 2)), dma((3,)), dma((3,)), dma((4,)), dma((4,)),
            dma((NC, 4, 2)), dma((NC, 4, 2)), dma((NC,)), dma((NC, 4, 2)), dma((NC, 4, 2)), dma((NC,)),
        ],
        compiler_params=pltpu.CompilerParams(
            collective_id=0, has_side_effects=True, vmem_limit_bytes=56 * 2**20
        ),
        name="contract",
    )(green_virt, green_occ, atom_order, block_sizes.reshape(1, -1), pattern, three_centre)
    return jnp.transpose(blocks, (1, 0, 2))


def solution(mesh):
    in_specs = (P("row", "col", None), P(("row", "col"), None), P(("row", "col"), None), P(), P(), P())
    return jax.shard_map(
        per_device, mesh=mesh, in_specs=in_specs, out_specs=P("row", None, "col"), check_vma=False
    )
```

```python
import jax
import jax.numpy as jnp
from jax import lax
from jax.experimental import pallas as pl
from jax.experimental.pallas import tpu as pltpu
from jax.sharding import PartitionSpec as P

MESH = pl.DeviceIdType.MESH
BF = jnp.bfloat16
F32 = jnp.float32
NC = 4
ORDERS = ("yzx", "zxy")


def me():
    r = lax.axis_index("row")
    c = lax.axis_index("col")
    return {
        "x": lax.rem(r, 4),
        "y": c // 4,
        "z": lax.rem(c // 2, 2) * 2 + r // 4,
        "k": lax.rem(c, 2),
    }


def turn(i):
    return i + (i // 2) * (5 - 2 * i)


def device(p):
    return {"row": lax.rem(p["z"], 2) * 4 + p["x"], "col": (p["y"] * 2 + p["z"] // 2) * 2 + p["k"]}


def moved(p, **by):
    q = dict(p)
    for axis, d in by.items():
        q[axis] = lax.rem(p[axis] + d, 2) if axis == "k" else lax.rem(p[axis] + d + 4, 4)
    return q


def flip(p, axis):
    q = dict(p)
    q[axis] = p[axis] + 1 - 2 * lax.rem(p[axis], 2)
    return q


def partners(p):
    found = [moved(p, k=1)]
    for d in (1, 2, 3):
        for e in (0, 1):
            found.append(moved(p, y=d, k=e))
            found.append(moved(p, z=d, k=e))
        found.append(moved(p, x=d))
        found.append(moved(p, y=d, z=2))
        found.append(flip(moved(p, x=d), "z"))
    return found


def kernel(gv, go, order, sizes, pattern, t_hbm, out,
           turned, gp, gvb, t2, mask, hs, hr, gst, got, ss,
           t_sem, own_sem, ts_sem, tr_sem, v1s, v1r, v2s, v2r, vys, vyr, vxs, vxr,
           o1s, o1r, o2s, o2r, o3s, o3r, o4s, o4r, hss, hrs, hl, sss, srs, sl):
    p = me()
    x, y, z, k = p["x"], p["y"], p["z"], p["k"]
    zl, zh, yl, yh = lax.rem(z, 2), z // 2, lax.rem(y, 2), y // 2
    row, col = lax.axis_index("row"), lax.axis_index("col")

    def remote(src, dst, send, recv, to):
        return pltpu.make_async_remote_copy(
            src_ref=src, dst_ref=dst, send_sem=send, recv_sem=recv, device_id=device(to), device_id_type=MESH
        )

    def t_load(c):
        two = pl.ds(c * 2, 2)
        return pltpu.make_async_copy(t_hbm.at[two], t2.at[two, k], t_sem.at[c])

    for c in range(NC):
        t_load(c).start()

    barrier = pltpu.get_barrier_semaphore()
    peers = partners(p)
    for q in peers:
        pl.semaphore_signal(barrier, inc=1, device_id=device(q), device_id_type=MESH)

    lane_slot = lax.broadcasted_iota(jnp.int32, (16, 128), 1) // 32
    for b in range(16):
        source = gv[:, b * 128:(b + 1) * 128].astype(F32)
        for t in range(4):
            turned[t, b] = pltpu.roll(source, t * 32, 1) if t else source

    def permute(j, carry):
        wanted = jnp.zeros((16, 128), jnp.int32)
        for s in range(4):
            wanted = jnp.where(lane_slot == s, order[4 * j + s], wanted)
        block = jnp.zeros((16, 128), F32)
        for t in range(4):
            first_atom = wanted - lax.rem(lane_slot - t + 4, 4)
            for b in range(16):
                block = jnp.where(first_atom == 4 * b, turned[t, b], block)
        gp[lax.rem(j, 2), lax.rem(j // 2, 2), j // 4] = block.astype(BF)
        return carry

    lax.fori_loop(0, 16, permute, 0)

    def rows16(core):
        return pl.ds(pl.multiple_of(core * 16, 16), 16)

    own = pltpu.make_async_copy(gp.at[k], gvb.at[:, :, zl, x, y, zh, rows16(k)], own_sem.at[0])
    own.start()
    own_o = pltpu.make_async_copy(
        go.at[:, pl.ds(pl.multiple_of(k * 1024, 1024), 1024)], gst.at[y * 2 + k], own_sem.at[1]
    )
    own_o.start()

    pl.semaphore_wait(barrier, len(peers))

    def v1(part, d, e, mine):
        axis = ORDERS[part][0]
        to = moved(p, **{axis: d, "k": e})
        frm = p if mine else moved(p, **{axis: -d, "k": e})
        dst = gvb.at[part, :, lax.rem(frm["z"], 2), frm["x"], frm["y"], frm["z"] // 2, rows16(frm["k"])]
        return remote(gp.at[to["k"], part], dst, v1s.at[part, d - 1, e], v1r.at[part, d - 1, e], to)

    def v1_sibling(mine):
        frm = p if mine else moved(p, k=1)
        return remote(
            gp.at[1 - k], gvb.at[:, :, zl, x, y, zh, rows16(frm["k"])], v1s.at[2, 0, 0], v1r.at[2, 0, 0], moved(p, k=1)
        )

    v1_sibling(True).start()
    for d in (1, 3, 2):
        for part in (0, 1):
            for e in (0, 1):
                v1(part, d, e, True).start()

    def o1(d, e, mine):
        to = moved(p, y=d, k=e)
        frm = p if mine else moved(p, y=-d, k=e)
        half = pl.ds(pl.multiple_of(to["k"] * 1024, 1024), 1024)
        return remote(go.at[:, half], gst.at[frm["y"] * 2 + frm["k"]], o1s.at[d, e], o1r.at[d, e], to)

    group = [(d, e) for d in range(4) for e in (0, 1) if d or e]
    for de in group:
        o1(*de, True).start()

    atom_of_row = lax.broadcasted_iota(jnp.int32, (128, 64), 0) // 32 + col * 4
    pick = (lax.broadcasted_iota(jnp.int32, (128, 64), 1) == atom_of_row).astype(F32)
    spread = (
        lax.broadcasted_iota(jnp.int32, (64, 2048), 1) // 32 == lax.broadcasted_iota(jnp.int32, (64, 2048), 0)
    ).astype(BF)
    size_row = sizes[...].astype(F32)
    own_size = jnp.sum(pick * size_row, axis=1, keepdims=True)
    row_ok = lax.rem(lax.broadcasted_iota(jnp.int32, (128, 1), 0), 32).astype(F32) < own_size
    paired = jnp.dot(pick.astype(BF), pattern[...].astype(F32).astype(BF), preferred_element_type=F32)
    paired = jnp.where(row_ok, paired, 0.0)
    paired = jnp.dot(paired.astype(BF), spread, preferred_element_type=F32)
    all_sizes = jnp.dot(jnp.broadcast_to(size_row, (8, 64)).astype(BF), spread, preferred_element_type=F32)[0:1]
    column_ok = lax.rem(lax.broadcasted_iota(jnp.int32, (1, 2048), 1), 32).astype(F32) < all_sizes
    mask[...] = jnp.where(column_ok, paired, 0.0).astype(BF)

    def t_share(c, mine):
        part = t2.at[pl.ds(c * 2, 2), k if mine else 1 - k]
        return remote(part, part, ts_sem.at[c], tr_sem.at[c], moved(p, k=1))

    def filter_chunk(c, carry):
        t_load(c).wait()

        def strip(i, inner):
            rows = pl.ds(pl.multiple_of(i * 16, 16), 16)
            m = mask[rows, :]
            for q in range(2):
                t2[c * 2 + q, k, rows, :] = t2[c * 2 + q, k, rows, :] * m
            return inner

        lax.fori_loop(0, 8, strip, 0)
        t_share(c, True).start()
        return carry

    lax.fori_loop(0, NC, filter_chunk, 0)

    def v2(part, d, mine):
        axis = ORDERS[part][1]
        at = p if mine else moved(p, **{axis: -d})
        azl, azh = lax.rem(at["z"], 2), at["z"] // 2
        slot = gvb.at[0, :, azl, x, :, azh] if part == 0 else gvb.at[1, :, :, at["x"], y, :]
        return remote(slot, slot, v2s.at[part, d - 1], v2r.at[part, d - 1], moved(p, **{axis: d}))

    own.wait()
    v1_sibling(False).wait_recv()
    for part in (0, 1):
        for d in (1, 2, 3):
            for e in (0, 1):
                v1(part, d, e, False).wait_recv()
        for d in (1, 3, 2):
            v2(part, d, True).start()

    own_o.wait()
    for de in group:
        o1(*de, False).wait_recv()
    got[zl, x, zh, k] = gst[...].reshape(128, 1024).T

    def o2(d, mine):
        at = p if mine else moved(p, z=-d)
        slot = got.at[lax.rem(at["z"], 2), x, at["z"] // 2, k]
        return remote(slot, slot, o2s.at[d - 1], o2r.at[d - 1], moved(p, z=d))

    for d in (1, 3, 2):
        o2(d, True).start()

    def vy(s, d, mine):
        pair = lax.rem((y + d if mine else y) + turn(s), 4)
        slot = gvb.at[1, pair, :, :, y if mine else moved(p, y=-d)["y"], :]
        return remote(slot, slot, vys.at[s, d - 1], vyr.at[s, d - 1], moved(p, y=d))

    def along_x(ref_of, send, recv, side, n, mine):
        step = 1 - 2 * side
        origin = (x if n < 2 else moved(p, x=-step)["x"]) if mine else moved(p, x=-step if n < 2 else 2)["x"]
        slot = ref_of(side if n == 2 else n, origin)
        return remote(slot, slot, send.at[side, n], recv.at[side, n], moved(p, x=step))

    def vx(s, side, n, mine):
        pair = lax.rem(y + turn(s), 4)
        return along_x(lambda half, at: gvb.at[0, pair, half, at], vxs.at[s], vxr.at[s], side, n, mine)

    def o3(t, side, n, mine):
        rows = pl.ds(t * 256, 256)
        return along_x(lambda half, at: got.at[half, at, :, k, rows], o3s.at[t], o3r.at[t], side, n, mine)

    def own_out(copy, i):
        for n in (0, 1):
            for side in (0, 1):
                copy(i, side, n if side == 0 else 1 - n, True).start()

    def pass_on(copy, i):
        for side in (0, 1):
            copy(i, side, side, False).wait_recv()
            copy(i, side, 2, True).start()

    def rest_in(copy, i):
        for side in (0, 1):
            copy(i, side, 1 - side, False).wait_recv()
            copy(i, side, 2, False).wait_recv()

    def o4(t, mine):
        slot = got.at[:, :, :, k if mine else 1 - k, pl.ds(t * 256, 256)]
        return remote(slot, slot, o4s.at[t], o4r.at[t], moved(p, k=1))

    for part in (0, 1):
        for d in (1, 2, 3):
            v2(part, d, False).wait_recv()

    own_out(vx, 0)
    own_out(vx, 1)

    def vy_start(s, carry):
        for d in (1, 3, 2):
            vy(s, d, True).start()
        return carry

    lax.fori_loop(0, 4, vy_start, 0)

    for c in range(NC):
        t_share(c, False).wait_recv()

    def h_copy(c, s, e, mine):
        to = moved(p, y=s, z=2 * e)
        frm = p if mine else moved(p, y=-s, z=2 * e)
        return remote(
            hs.at[c, to["y"] * 2 + to["z"] // 2],
            hr.at[c, :, frm["y"] * 2 + frm["z"] // 2],
            hss.at[c, s, e], hrs.at[c, s, e], to,
        )

    def h_own(c):
        chip = y * 2 + zh
        return pltpu.make_async_copy(hs.at[c, chip], hr.at[c, :, chip], hl.at[c])

    def first(i, carry):
        n, c = i // 4, lax.rem(i, 4)
        s = turn(n)

        @pl.when(i == 0)
        def _():
            for n in (0, 1):
                pass_on(vx, n)
                own_out(vx, n + 2)

        @pl.when(i == 4)
        def _():
            pass_on(vx, 2)

        @pl.when(i == 8)
        def _():
            pass_on(vx, 3)
            for d in (1, 2, 3):
                o2(d, False).wait_recv()
            own_out(o3, 0)
            own_out(o3, 1)

        @pl.when(c == 0)
        def _():
            rest_in(vx, n)
            for d in (1, 2, 3):
                vy(n, d, False).wait_recv()

        pair = lax.rem(y + s, 4)
        rhs = jnp.concatenate([gvb[q, pair].reshape(2048, 128) for q in range(2)], axis=1)
        lhs = t2[pl.ds(c * 2, 2)].reshape(512, 2048)
        h = jnp.dot(lhs, rhs, preferred_element_type=F32).astype(BF)
        for q in range(2):
            hs[c, pair * 2 + q] = h[:, q * 128:(q + 1) * 128].reshape(2, 256, 128)
        h_copy(c, s, 1, True).start()

        @pl.when(s == 0)
        def _():
            h_own(c).start()

        @pl.when(s > 0)
        def _():
            h_copy(c, s, 0, True).start()

        return carry

    lax.fori_loop(0, NC * 4, first, 0)

    for t in (0, 1):
        pass_on(o3, t)
        own_out(o3, t + 2)
    for t in (0, 1):
        rest_in(o3, t)
        o4(t, True).start()
        pass_on(o3, t + 2)

    def s_copy(c, d, e, mine):
        to = moved(p, x=d)
        frm = p if mine else moved(p, x=-d)
        if e:
            to = flip(to, "z")
            if not mine:
                frm = flip(frm, "z")
        frm_row = lax.rem(frm["z"], 2) * 4 + frm["x"]
        return remote(ss.at[c, d, e], out.at[pl.ds(frm_row * 8 + c * 2, 2)], sss.at[c, d, e], srs.at[c, d, e], to)

    def s_own(c):
        return pltpu.make_async_copy(ss.at[c, 0, 0], out.at[pl.ds(row * 8 + c * 2, 2)], sl.at[c])

    def lined_up(c, q):
        rows = []
        for b in range(16):
            for j in range(4):
                n = (b // 2) * 8 + j * 2 + b % 2
                rows.append(hr[c, q, n // 8, (n % 8) * 32:(n % 8) * 32 + 32, :])
        return jnp.concatenate(rows, axis=0)

    def second(j, carry):
        c, t = j // 4, lax.rem(j, 4)

        @pl.when(t == 0)
        def _():
            h_own(c).wait()
            h_copy(c, 0, 1, False).wait_recv()
            for s in (1, 2, 3):
                for e in (0, 1):
                    h_copy(c, s, e, False).wait_recv()

        @pl.when(c == 0)
        def _():
            @pl.when(t >= 2)
            def _():
                rest_in(o3, t)
                o4(t, True).start()

            o4(t, False).wait_recv()

        rows = pl.ds(pl.multiple_of(t * 256, 256), 256)
        lhs = jnp.concatenate(
            [
                jnp.concatenate(
                    [got[b // 8, (b // 2) % 4, b % 2, zl if e == 0 else 1 - zl, rows, :] for b in range(16)], axis=1
                )
                for e in (0, 1)
            ],
            axis=0,
        )
        rhs = jnp.concatenate([lined_up(c, q) for q in range(2)], axis=1)
        r = jnp.dot(lhs, rhs, preferred_element_type=F32).astype(BF)
        d = lax.rem(t - x + 4, 4)
        for e in (0, 1):
            for q in range(2):
                ss[c, d, e, q] = r[e * 256:(e + 1) * 256, q * 128:(q + 1) * 128]
        s_copy(c, d, 1, True).start()

        @pl.when(d == 0)
        def _():
            s_own(c).start()

        @pl.when(d > 0)
        def _():
            s_copy(c, d, 0, True).start()

        return carry

    lax.fori_loop(0, NC * 4, second, 0)

    v1_sibling(True).wait_send()
    for part in (0, 1):
        for d in (1, 2, 3):
            for e in (0, 1):
                v1(part, d, e, True).wait_send()
            v2(part, d, True).wait_send()
    for de in group:
        o1(*de, True).wait_send()
    for d in (1, 2, 3):
        o2(d, True).wait_send()

    def drain(c, carry):
        t_share(c, True).wait_send()
        for d in (1, 2, 3):
            vy(c, d, True).wait_send()
        for side in (0, 1):
            for n in range(3):
                vx(c, side, n, True).wait_send()
                o3(c, side, n, True).wait_send()
        o4(c, True).wait_send()
        s_own(c).wait()
        for s in range(4):
            for e in (0, 1):
                if s or e:
                    h_copy(c, s, e, True).wait_send()
                    s_copy(c, s, e, True).wait_send()
                    s_copy(c, s, e, False).wait_recv()
        return carry

    lax.fori_loop(0, NC, drain, 0)


def per_device(three_centre, green_virt, green_occ, pattern, block_sizes, atom_order):
    vmem = pl.BlockSpec(memory_space=pltpu.VMEM)
    dma = pltpu.SemaphoreType.DMA
    blocks = pl.pallas_call(
        kernel,
        out_shape=jax.ShapeDtypeStruct((64, 256, 128), BF),
        in_specs=[vmem, vmem, pl.BlockSpec(memory_space=pltpu.SMEM), vmem, vmem, pl.BlockSpec(memory_space=pl.ANY)],
        out_specs=pl.BlockSpec(memory_space=pl.ANY),
        scratch_shapes=[
            pltpu.VMEM((4, 16, 16, 128), F32),
            pltpu.VMEM((2, 2, 4, 16, 128), BF),
            pltpu.VMEM((2, 4, 2, 4, 4, 2, 32, 128), BF),
            pltpu.VMEM((8, 2, 128, 2048), BF),
            pltpu.VMEM((128, 2048), BF),
            pltpu.VMEM((NC, 8, 2, 256, 128), BF),
            pltpu.VMEM((NC, 2, 8, 256, 128), BF),
            pltpu.VMEM((8, 16, 1024), BF),
            pltpu.VMEM((2, 4, 2, 2, 1024, 128), BF),
            pltpu.VMEM((NC, 4, 2, 2, 256, 128), BF),
            dma((NC,)), dma((2,)), dma((NC,)), dma((NC,)),
            dma((3, 3, 2)), dma((3, 3, 2)), dma((2, 3)), dma((2, 3)), dma((4, 3)), dma((4, 3)), dma((4, 2, 3)), dma((4, 2, 3)),
            dma((4, 2)), dma((4, 2)), dma((3,)), dma((3,)), dma((4, 2, 3)), dma((4, 2, 3)), dma((4,)), dma((4,)),
            dma((NC, 4, 2)), dma((NC, 4, 2)), dma((NC,)), dma((NC, 4, 2)), dma((NC, 4, 2)), dma((NC,)),
        ],
        compiler_params=pltpu.CompilerParams(
            collective_id=0, has_side_effects=True, vmem_limit_bytes=56 * 2**20
        ),
        name="contract",
    )(green_virt, green_occ, atom_order, block_sizes.reshape(1, -1), pattern, three_centre)
    return jnp.transpose(blocks, (1, 0, 2))


def solution(mesh):
    in_specs = (P("row", "col", None), P(("row", "col"), None), P(("row", "col"), None), P(), P(), P())
    return jax.shard_map(
        per_device, mesh=mesh, in_specs=in_specs, out_specs=P("row", None, "col"), check_vma=False
    )
```

```python
import jax
import jax.numpy as jnp
from jax import lax
from jax.experimental import pallas as pl
from jax.experimental.pallas import tpu as pltpu
from jax.sharding import PartitionSpec as P

MESH = pl.DeviceIdType.MESH
BF = jnp.bfloat16
F32 = jnp.float32
NC = 4
ORDERS = ("zyx", "zxy")
FAR_ORDER = (1, 3, 2, 0)


def me():
    r = lax.axis_index("row")
    c = lax.axis_index("col")
    return {
        "x": lax.rem(r, 4),
        "y": c // 4,
        "z": lax.rem(c // 2, 2) * 2 + r // 4,
        "k": lax.rem(c, 2),
    }


def turn(i):
    return i + (i // 2) * (5 - 2 * i)


def device(p):
    return {"row": lax.rem(p["z"], 2) * 4 + p["x"], "col": (p["y"] * 2 + p["z"] // 2) * 2 + p["k"]}


def moved(p, **by):
    q = dict(p)
    for axis, d in by.items():
        q[axis] = lax.rem(p[axis] + d, 2) if axis == "k" else lax.rem(p[axis] + d + 4, 4)
    return q


def flip(p, axis):
    q = dict(p)
    q[axis] = p[axis] + 1 - 2 * lax.rem(p[axis], 2)
    return q


def partners(p):
    found = [moved(p, k=1)]
    for d in (1, 2, 3):
        for e in (0, 1):
            found.append(moved(p, y=d, k=e))
            found.append(moved(p, z=d, k=e))
        found.append(moved(p, x=d))
        found.append(flip(moved(p, x=d), "z"))
    return found


def kernel(gv, go, order, sizes, pattern, t_hbm, out,
           turned, gp, gvb, t2, mask, hs, hz, hr, gst, got, ss,
           t_sem, own_sem, ts_sem, tr_sem, v1s, v1r, v2s, v2r, vys, vyr, vxs, vxr,
           o1s, o1r, o2s, o2r, o3s, o3r, o4s, o4r, hus, hur, hss, hrs, hl, sss, srs, sl):
    p = me()
    x, y, z, k = p["x"], p["y"], p["z"], p["k"]
    zl, zh, yl, yh = lax.rem(z, 2), z // 2, lax.rem(y, 2), y // 2
    row, col = lax.axis_index("row"), lax.axis_index("col")

    def remote(src, dst, send, recv, to):
        return pltpu.make_async_remote_copy(
            src_ref=src, dst_ref=dst, send_sem=send, recv_sem=recv, device_id=device(to), device_id_type=MESH
        )

    def t_load(c):
        two = pl.ds(c * 2, 2)
        return pltpu.make_async_copy(t_hbm.at[two], t2.at[two, k], t_sem.at[c])

    for c in range(NC):
        t_load(c).start()

    barrier = pltpu.get_barrier_semaphore()
    peers = partners(p)
    for q in peers:
        pl.semaphore_signal(barrier, inc=1, device_id=device(q), device_id_type=MESH)

    lane_slot = lax.broadcasted_iota(jnp.int32, (16, 128), 1) // 32
    for b in range(16):
        source = gv[:, b * 128:(b + 1) * 128].astype(F32)
        for t in range(4):
            turned[t, b] = pltpu.roll(source, t * 32, 1) if t else source

    def permute(j, carry):
        wanted = jnp.zeros((16, 128), jnp.int32)
        for s in range(4):
            wanted = jnp.where(lane_slot == s, order[4 * j + s], wanted)
        block = jnp.zeros((16, 128), F32)
        for t in range(4):
            first_atom = wanted - lax.rem(lane_slot - t + 4, 4)
            for b in range(16):
                block = jnp.where(first_atom == 4 * b, turned[t, b], block)
        gp[lax.rem(j, 2), lax.rem(j // 2, 2), j // 4] = block.astype(BF)
        return carry

    lax.fori_loop(0, 16, permute, 0)

    def rows16(core):
        return pl.ds(pl.multiple_of(core * 16, 16), 16)

    own = pltpu.make_async_copy(gp.at[k], gvb.at[:, :, zl, x, y, zh, rows16(k)], own_sem.at[0])
    own.start()
    own_o = pltpu.make_async_copy(
        go.at[:, pl.ds(pl.multiple_of(k * 1024, 1024), 1024)], gst.at[y * 2 + k], own_sem.at[1]
    )
    own_o.start()

    pl.semaphore_wait(barrier, len(peers))

    def v1(d, e, mine):
        to = moved(p, z=d, k=e)
        frm = p if mine else moved(p, z=-d, k=e)
        dst = gvb.at[:, :, lax.rem(frm["z"], 2), x, y, frm["z"] // 2, rows16(frm["k"])]
        return remote(gp.at[to["k"]], dst, v1s.at[d - 1, e], v1r.at[d - 1, e], to)

    def v1_sibling(mine):
        frm = p if mine else moved(p, k=1)
        return remote(
            gp.at[1 - k], gvb.at[:, :, zl, x, y, zh, rows16(frm["k"])], v1s.at[3, 0], v1r.at[3, 0], moved(p, k=1)
        )

    v1_sibling(True).start()
    for d in (1, 3, 2):
        for e in (0, 1):
            v1(d, e, True).start()

    def o1(d, e, mine):
        to = moved(p, y=d, k=e)
        frm = p if mine else moved(p, y=-d, k=e)
        half = pl.ds(pl.multiple_of(to["k"] * 1024, 1024), 1024)
        return remote(go.at[:, half], gst.at[frm["y"] * 2 + frm["k"]], o1s.at[d, e], o1r.at[d, e], to)

    group = [(d, e) for d in range(4) for e in (0, 1) if d or e]
    for de in group:
        o1(*de, True).start()

    atom_of_row = lax.broadcasted_iota(jnp.int32, (128, 64), 0) // 32 + col * 4
    pick = (lax.broadcasted_iota(jnp.int32, (128, 64), 1) == atom_of_row).astype(F32)
    spread = (
        lax.broadcasted_iota(jnp.int32, (64, 2048), 1) // 32 == lax.broadcasted_iota(jnp.int32, (64, 2048), 0)
    ).astype(BF)
    size_row = sizes[...].astype(F32)
    own_size = jnp.sum(pick * size_row, axis=1, keepdims=True)
    row_ok = lax.rem(lax.broadcasted_iota(jnp.int32, (128, 1), 0), 32).astype(F32) < own_size
    paired = jnp.dot(pick.astype(BF), pattern[...].astype(F32).astype(BF), preferred_element_type=F32)
    paired = jnp.where(row_ok, paired, 0.0)
    paired = jnp.dot(paired.astype(BF), spread, preferred_element_type=F32)
    all_sizes = jnp.dot(jnp.broadcast_to(size_row, (8, 64)).astype(BF), spread, preferred_element_type=F32)[0:1]
    column_ok = lax.rem(lax.broadcasted_iota(jnp.int32, (1, 2048), 1), 32).astype(F32) < all_sizes
    mask[...] = jnp.where(column_ok, paired, 0.0).astype(BF)

    def t_share(c, mine):
        part = t2.at[pl.ds(c * 2, 2), k if mine else 1 - k]
        return remote(part, part, ts_sem.at[c], tr_sem.at[c], moved(p, k=1))

    def filter_chunk(c, carry):
        t_load(c).wait()

        def strip(i, inner):
            rows = pl.ds(pl.multiple_of(i * 16, 16), 16)
            m = mask[rows, :]
            for q in range(2):
                t2[c * 2 + q, k, rows, :] = t2[c * 2 + q, k, rows, :] * m
            return inner

        lax.fori_loop(0, 8, strip, 0)
        t_share(c, True).start()
        return carry

    lax.fori_loop(0, NC, filter_chunk, 0)

    def v2(part, j, d, mine):
        axis = ORDERS[part][1]
        at = p if mine else moved(p, **{axis: -d})
        if part == 0:
            slot = gvb.at[0, lax.rem((y + d if mine else y) + turn(j), 4), :, x, at["y"], :]
        else:
            slot = gvb.at[1, lax.rem(y + FAR_ORDER[j], 4), :, at["x"], y, :]
        return remote(slot, slot, v2s.at[part, j, d - 1], v2r.at[part, j, d - 1], moved(p, **{axis: d}))

    def v2_out(part, j):
        for d in (1, 3, 2):
            v2(part, j, d, True).start()

    def v2_in(part, j):
        for d in (1, 2, 3):
            v2(part, j, d, False).wait_recv()

    own.wait()
    v1_sibling(False).wait_recv()
    for d in (1, 2, 3):
        for e in (0, 1):
            v1(d, e, False).wait_recv()
    for j in range(4):
        v2_out(0, j)
        if j < 3:
            v2_out(1, j)

    own_o.wait()
    for de in group:
        o1(*de, False).wait_recv()
    got[zl, x, zh, k] = gst[...].reshape(128, 1024).T

    def o2(d, mine):
        at = p if mine else moved(p, z=-d)
        slot = got.at[lax.rem(at["z"], 2), x, at["z"] // 2, k]
        return remote(slot, slot, o2s.at[d - 1], o2r.at[d - 1], moved(p, z=d))

    for d in (1, 3, 2):
        o2(d, True).start()

    def vy(s, d, mine):
        pair = lax.rem((y + d if mine else y) + turn(s), 4)
        slot = gvb.at[1, pair, :, :, y if mine else moved(p, y=-d)["y"], :]
        return remote(slot, slot, vys.at[s, d - 1], vyr.at[s, d - 1], moved(p, y=d))

    def along_x(ref_of, send, recv, side, n, mine):
        step = 1 - 2 * side
        origin = (x if n < 2 else moved(p, x=-step)["x"]) if mine else moved(p, x=-step if n < 2 else 2)["x"]
        slot = ref_of(side if n == 2 else n, origin)
        return remote(slot, slot, send.at[side, n], recv.at[side, n], moved(p, x=step))

    def vx(s, side, n, mine):
        pair = lax.rem(y + turn(s), 4)
        return along_x(lambda half, at: gvb.at[0, pair, half, at], vxs.at[s], vxr.at[s], side, n, mine)

    def o3(t, side, n, mine):
        rows = pl.ds(t * 256, 256)
        return along_x(lambda half, at: got.at[half, at, :, k, rows], o3s.at[t], o3r.at[t], side, n, mine)

    def own_out(copy, i):
        for n in (0, 1):
            for side in (0, 1):
                copy(i, side, n if side == 0 else 1 - n, True).start()

    def pass_on(copy, i):
        for side in (0, 1):
            copy(i, side, side, False).wait_recv()
            copy(i, side, 2, True).start()

    def rest_in(copy, i):
        for side in (0, 1):
            copy(i, side, 1 - side, False).wait_recv()
            copy(i, side, 2, False).wait_recv()

    def o4(t, mine):
        slot = got.at[:, :, :, k if mine else 1 - k, pl.ds(t * 256, 256)]
        return remote(slot, slot, o4s.at[t], o4r.at[t], moved(p, k=1))

    v2_in(0, 0)
    own_out(vx, 0)
    v2_out(1, 3)
    for j in range(3):
        v2_in(1, j)
        vy(0, FAR_ORDER[j], True).start()
    vy(1, 1, True).start()
    vy(1, 2, True).start()
    for j in range(1, 4):
        v2_in(0, j)
    v2_in(1, 3)
    vy(1, 3, True).start()
    for s in (2, 3):
        for d in (1, 3, 2):
            vy(s, d, True).start()

    for c in range(NC):
        t_share(c, False).wait_recv()

    def h_own(c):
        chip = y * 2 + zh
        return pltpu.make_async_copy(hs.at[c, chip], hr.at[c, :, chip], hl.at[c])

    def h_side(c, s, mine):
        source = moved(p, y=0 if mine else -s)["y"] * 2 + zh
        return remote(
            hs.at[c, lax.rem(y + s, 4) * 2 + zh], hr.at[c, :, source], hss.at[c, s, 0], hrs.at[c, s, 0], moved(p, y=s)
        )

    def h_cross(c, s, mine):
        if isinstance(s, int) and s == 0:
            dst = hr.at[c, :, y * 2 + (zh if mine else 1 - zh)]
        else:
            dst = hz.at[c, s - 1]
        return remote(
            hs.at[c, lax.rem(y + s, 4) * 2 + 1 - zh], dst, hus.at[c, s], hur.at[c, s], moved(p, z=2)
        )

    def h_pass(c, s, mine):
        source = moved(p, y=0 if mine else -s)["y"] * 2 + 1 - zh
        return remote(hz.at[c, s - 1], hr.at[c, :, source], hss.at[c, s, 1], hrs.at[c, s, 1], moved(p, y=s))

    def h_on(half, s):
        for c in (half * 2, half * 2 + 1):
            h_cross(c, s, False).wait_recv()
            h_pass(c, s, True).start()

    def first(i, carry):
        half, n = i // 4, lax.rem(i, 4)
        s = turn(n)

        @pl.when(i == 0)
        def _():
            pass_on(vx, 0)
            own_out(vx, 1)
            own_out(vx, 2)

        @pl.when(i == 1)
        def _():
            pass_on(vx, 1)
            own_out(vx, 3)
            pass_on(vx, 2)

        @pl.when(i == 2)
        def _():
            pass_on(vx, 3)
            for d in (1, 2, 3):
                o2(d, False).wait_recv()
            own_out(o3, 0)
            own_out(o3, 1)

        @pl.when(half == 0)
        def _():
            rest_in(vx, n)
            for d in (1, 2, 3):
                vy(n, d, False).wait_recv()

        @pl.when(i == 4)
        def _():
            h_on(0, 1)
            pass_on(o3, 0)
            own_out(o3, 2)

        @pl.when(i == 6)
        def _():
            h_on(0, 3)

        pair = lax.rem(y + s, 4)
        rhs = jnp.concatenate([gvb[q, pair].reshape(2048, 128) for q in range(2)], axis=1)
        lhs = t2[pl.ds(half * 4, 4)].reshape(1024, 2048)
        h = jnp.dot(lhs, rhs, preferred_element_type=F32).astype(BF)
        for m in range(2):
            for q in range(2):
                hs[half * 2 + m, pair * 2 + q] = h[m * 512:(m + 1) * 512, q * 128:(q + 1) * 128].reshape(2, 256, 128)
        for m in range(2):
            c = half * 2 + m

            @pl.when(n == 0)
            def _():
                h_cross(c, 0, True).start()
                h_own(c).start()

            @pl.when(n > 0)
            def _():
                h_cross(c, s, True).start()

            @pl.when((n > 0) & (half == 0))
            def _():
                h_side(c, s, True).start()

        return carry

    lax.fori_loop(0, 8, first, 0)

    pass_on(o3, 1)
    own_out(o3, 3)
    h_on(0, 2)
    for s in (1, 3, 2):
        for c in (2, 3):
            h_side(c, s, True).start()
    rest_in(o3, 0)
    o4(0, True).start()
    pass_on(o3, 2)
    rest_in(o3, 1)
    o4(1, True).start()
    h_on(1, 1)
    pass_on(o3, 3)

    def s_copy(c, d, e, mine):
        to = moved(p, x=d)
        frm = p if mine else moved(p, x=-d)
        if e:
            to = flip(to, "z")
            if not mine:
                frm = flip(frm, "z")
        frm_row = lax.rem(frm["z"], 2) * 4 + frm["x"]
        return remote(ss.at[c, d, e], out.at[pl.ds(frm_row * 8 + c * 2, 2)], sss.at[c, d, e], srs.at[c, d, e], to)

    def s_own(c):
        return pltpu.make_async_copy(ss.at[c, 0, 0], out.at[pl.ds(row * 8 + c * 2, 2)], sl.at[c])

    def lined_up(c, q):
        rows = []
        for b in range(16):
            for j in range(4):
                n = (b // 2) * 8 + j * 2 + b % 2
                rows.append(hr[c, q, n // 8, (n % 8) * 32:(n % 8) * 32 + 32, :])
        return jnp.concatenate(rows, axis=0)

    def second(j, carry):
        half, t = j // 4, lax.rem(j, 4)

        @pl.when(t == 0)
        def _():
            for m in range(2):
                c = half * 2 + m
                h_own(c).wait()
                h_cross(c, 0, False).wait_recv()
                for s in (1, 2, 3):
                    h_side(c, s, False).wait_recv()
                    h_pass(c, s, False).wait_recv()

        @pl.when(j == 2)
        def _():
            h_on(1, 3)

        @pl.when(half == 0)
        def _():
            @pl.when(t >= 2)
            def _():
                rest_in(o3, t)
                o4(t, True).start()

            @pl.when(t == 3)
            def _():
                h_on(1, 2)

            o4(t, False).wait_recv()

        rows = pl.ds(pl.multiple_of(t * 256, 256), 256)
        lhs = jnp.concatenate(
            [
                jnp.concatenate(
                    [got[b // 8, (b // 2) % 4, b % 2, zl if e == 0 else 1 - zl, rows, :] for b in range(16)], axis=1
                )
                for e in (0, 1)
            ],
            axis=0,
        )
        rhs = jnp.concatenate([lined_up(half * 2 + m, q) for m in range(2) for q in range(2)], axis=1)
        r = jnp.dot(lhs, rhs, preferred_element_type=F32).astype(BF)
        d = lax.rem(t - x + 4, 4)
        for m in range(2):
            c = half * 2 + m
            for e in (0, 1):
                for q in range(2):
                    ss[c, d, e, q] = r[e * 256:(e + 1) * 256, (m * 2 + q) * 128:(m * 2 + q + 1) * 128]

            @pl.when((d == 0) | (half == 1))
            def _():
                s_copy(c, d, 1, True).start()

            @pl.when(d == 0)
            def _():
                s_own(c).start()

            @pl.when(d > 0)
            def _():
                s_copy(c, d, 0, True).start()

        @pl.when(j == 3)
        def _():
            for d1 in (1, 3, 2):
                for c in (0, 1):
                    s_copy(c, d1, 1, True).start()

        return carry

    lax.fori_loop(0, 8, second, 0)

    v1_sibling(True).wait_send()
    for d in (1, 2, 3):
        for e in (0, 1):
            v1(d, e, True).wait_send()
        for part in (0, 1):
            for j in range(4):
                v2(part, j, d, True).wait_send()
    for de in group:
        o1(*de, True).wait_send()
    for d in (1, 2, 3):
        o2(d, True).wait_send()

    def drain(c, carry):
        t_share(c, True).wait_send()
        for d in (1, 2, 3):
            vy(c, d, True).wait_send()
        for side in (0, 1):
            for n in range(3):
                vx(c, side, n, True).wait_send()
                o3(c, side, n, True).wait_send()
        o4(c, True).wait_send()
        s_own(c).wait()
        h_cross(c, 0, True).wait_send()
        for s in (1, 2, 3):
            h_cross(c, s, True).wait_send()
            h_side(c, s, True).wait_send()
            h_pass(c, s, True).wait_send()
        for s in range(4):
            for e in (0, 1):
                if s or e:
                    s_copy(c, s, e, True).wait_send()
                    s_copy(c, s, e, False).wait_recv()
        return carry

    lax.fori_loop(0, NC, drain, 0)


def restack(blocks, out, source, target, in_sem, out_sem):
    parts = in_sem.shape[0]
    lams = out.shape[0] // parts

    def load(i):
        some = pl.ds(i * lams, lams)
        return pltpu.make_async_copy(blocks.at[:, some], source.at[:, some], in_sem.at[i])

    def store(i):
        some = pl.ds(i * lams, lams)
        return pltpu.make_async_copy(target.at[some], out.at[some], out_sem.at[i])

    for i in range(parts):
        load(i).start()
    to = lax.broadcasted_iota(jnp.int32, (256, 256), 0)
    frm = lax.broadcasted_iota(jnp.int32, (256, 256), 1)
    one_hot = ((to // 16 == lax.rem(frm, 16)) & (lax.rem(to, 16) == frm // 16)).astype(BF)

    def part(i, carry):
        load(i).wait()
        for pair in range(lams // 32):
            for group in range(blocks.shape[0] // 16):
                ps = slice(group * 16, group * 16 + 16)
                at = [pl.ds(pl.multiple_of(i * lams + pair * 32 + h * 16, 16), 16) for h in range(2)]
                rows = jnp.concatenate([source[ps, at[h], :].reshape(256, 128) for h in range(2)], axis=1)
                moved_rows = jnp.dot(one_hot, rows, preferred_element_type=F32).astype(BF)
                for h in range(2):
                    target[at[h], ps, :] = moved_rows[:, h * 128:(h + 1) * 128].reshape(16, 16, 128)
        store(i).start()
        return carry

    lax.fori_loop(0, parts, part, 0)
    for i in range(parts):
        store(i).wait()


def per_device(three_centre, green_virt, green_occ, pattern, block_sizes, atom_order):
    vmem = pl.BlockSpec(memory_space=pltpu.VMEM)
    dma = pltpu.SemaphoreType.DMA
    blocks = pl.pallas_call(
        kernel,
        out_shape=jax.ShapeDtypeStruct((64, 256, 128), BF),
        in_specs=[vmem, vmem, pl.BlockSpec(memory_space=pltpu.SMEM), vmem, vmem, pl.BlockSpec(memory_space=pl.ANY)],
        out_specs=pl.BlockSpec(memory_space=pl.ANY),
        scratch_shapes=[
            pltpu.VMEM((4, 16, 16, 128), F32),
            pltpu.VMEM((2, 2, 4, 16, 128), BF),
            pltpu.VMEM((2, 4, 2, 4, 4, 2, 32, 128), BF),
            pltpu.VMEM((8, 2, 128, 2048), BF),
            pltpu.VMEM((128, 2048), BF),
            pltpu.VMEM((NC, 8, 2, 256, 128), BF),
            pltpu.VMEM((NC, 3, 2, 256, 128), BF),
            pltpu.VMEM((NC, 2, 8, 256, 128), BF),
            pltpu.VMEM((8, 16, 1024), BF),
            pltpu.VMEM((2, 4, 2, 2, 1024, 128), BF),
            pltpu.VMEM((NC, 4, 2, 2, 256, 128), BF),
            dma((NC,)), dma((2,)), dma((NC,)), dma((NC,)),
            dma((4, 2)), dma((4, 2)), dma((2, 4, 3)), dma((2, 4, 3)), dma((4, 3)), dma((4, 3)), dma((4, 2, 3)), dma((4, 2, 3)),
            dma((4, 2)), dma((4, 2)), dma((3,)), dma((3,)), dma((4, 2, 3)), dma((4, 2, 3)), dma((4,)), dma((4,)),
            dma((NC, 4)), dma((NC, 4)), dma((NC, 4, 2)), dma((NC, 4, 2)), dma((NC,)), dma((NC, 4, 2)), dma((NC, 4, 2)), dma((NC,)),
        ],
        compiler_params=pltpu.CompilerParams(
            collective_id=0, has_side_effects=True, vmem_limit_bytes=56 * 2**20
        ),
        name="contract",
    )(green_virt, green_occ, atom_order, block_sizes.reshape(1, -1), pattern, three_centre)
    anywhere = pl.BlockSpec(memory_space=pl.ANY)
    return pl.pallas_call(
        restack,
        out_shape=jax.ShapeDtypeStruct((256, 64, 128), BF),
        in_specs=[anywhere],
        out_specs=anywhere,
        scratch_shapes=[pltpu.VMEM((64, 256, 128), BF), pltpu.VMEM((256, 64, 128), BF), dma((2,)), dma((2,))],
        compiler_params=pltpu.CompilerParams(vmem_limit_bytes=60 * 2**20),
        name="restack",
    )(blocks)


def solution(mesh):
    in_specs = (P("row", "col", None), P(("row", "col"), None), P(("row", "col"), None), P(), P(), P())
    return jax.shard_map(
        per_device, mesh=mesh, in_specs=in_specs, out_specs=P("row", None, "col"), check_vma=False
    )
```

```python
import jax
import jax.numpy as jnp
from jax import lax
from jax.experimental import pallas as pl
from jax.experimental.pallas import tpu as pltpu
from jax.sharding import PartitionSpec as P

MESH = pl.DeviceIdType.MESH
BF = jnp.bfloat16
F32 = jnp.float32
NC = 4
ORDERS = ("zyx", "zxy")
TS, V1, V2, VY, VX, O1, O2, O3, O4, HC, HD, HP, SC, SD, SP = range(15)
FAR_ORDER = (1, 3, 2, 0)


def me():
    r = lax.axis_index("row")
    c = lax.axis_index("col")
    return {
        "x": lax.rem(r, 4),
        "y": c // 4,
        "z": lax.rem(c // 2, 2) * 2 + r // 4,
        "k": lax.rem(c, 2),
    }


def turn(i):
    return i + (i // 2) * (5 - 2 * i)


def device(p):
    return {"row": lax.rem(p["z"], 2) * 4 + p["x"], "col": (p["y"] * 2 + p["z"] // 2) * 2 + p["k"]}


def moved(p, **by):
    q = dict(p)
    for axis, d in by.items():
        q[axis] = lax.rem(p[axis] + d, 2) if axis == "k" else lax.rem(p[axis] + d + 4, 4)
    return q


def flip(p, axis):
    q = dict(p)
    q[axis] = p[axis] + 1 - 2 * lax.rem(p[axis], 2)
    return q


def partners(p):
    found = [moved(p, k=1)]
    for d in (1, 2, 3):
        for e in (0, 1):
            found.append(moved(p, y=d, k=e))
            found.append(moved(p, z=d, k=e))
        found.append(moved(p, x=d))
    return found


def kernel(gv, go, order, sizes, pattern, t_hbm, out,
           turned, gp, gvb, t2, mask, hs, hz, hr, gst, got, ss, sz,
           t_sem, own_sem, sent, tr, v1r, v2r, vyr, vxr, o1r, o2r, o3r, o4r, hur, hrr, zr, srr):
    p = me()
    x, y, z, k = p["x"], p["y"], p["z"], p["k"]
    zl, zh, yl, yh = lax.rem(z, 2), z // 2, lax.rem(y, 2), y // 2
    row, col = lax.axis_index("row"), lax.axis_index("col")

    def remote(src, dst, send, recv, to):
        return pltpu.make_async_remote_copy(
            src_ref=src, dst_ref=dst, send_sem=send, recv_sem=recv, device_id=device(to), device_id_type=MESH
        )

    def arrived(ref, sem):
        pltpu.make_async_copy(ref, ref, sem).wait()

    def t_load(c):
        two = pl.ds(c * 2, 2)
        return pltpu.make_async_copy(t_hbm.at[two], t2.at[two, k], t_sem.at[c])

    for c in range(NC):
        t_load(c).start()

    barrier = pltpu.get_barrier_semaphore()
    peers = partners(p)
    for q in peers:
        pl.semaphore_signal(barrier, inc=1, device_id=device(q), device_id_type=MESH)

    lane_slot = lax.broadcasted_iota(jnp.int32, (16, 128), 1) // 32
    for b in range(16):
        source = gv[:, b * 128:(b + 1) * 128].astype(F32)
        for t in range(4):
            turned[t, b] = pltpu.roll(source, t * 32, 1) if t else source

    def permute(j, carry):
        wanted = jnp.zeros((16, 128), jnp.int32)
        for s in range(4):
            wanted = jnp.where(lane_slot == s, order[4 * j + s], wanted)
        block = jnp.zeros((16, 128), F32)
        for t in range(4):
            first_atom = wanted - lax.rem(lane_slot - t + 4, 4)
            for b in range(16):
                block = jnp.where(first_atom == 4 * b, turned[t, b], block)
        gp[lax.rem(j, 2), lax.rem(j // 2, 2), j // 4] = block.astype(BF)
        return carry

    lax.fori_loop(0, 16, permute, 0)

    def rows16(core):
        return pl.ds(pl.multiple_of(core * 16, 16), 16)

    own = pltpu.make_async_copy(gp.at[k], gvb.at[:, :, zl, x, y, zh, rows16(k)], own_sem.at[0])
    own.start()
    own_o = pltpu.make_async_copy(
        go.at[:, pl.ds(pl.multiple_of(k * 1024, 1024), 1024)], gst.at[y * 2 + k], own_sem.at[1]
    )
    own_o.start()

    pl.semaphore_wait(barrier, len(peers))

    def v1(d, e, mine):
        to = moved(p, z=d, k=e)
        frm = p if mine else moved(p, z=-d, k=e)
        dst = gvb.at[:, :, lax.rem(frm["z"], 2), x, y, frm["z"] // 2, rows16(frm["k"])]
        return remote(gp.at[to["k"]], dst, sent.at[V1], v1r.at[0], to)

    def v1_sibling(mine):
        frm = p if mine else moved(p, k=1)
        return remote(
            gp.at[1 - k], gvb.at[:, :, zl, x, y, zh, rows16(frm["k"])], sent.at[V1], v1r.at[0], moved(p, k=1)
        )

    v1_sibling(True).start()
    for d in (1, 3, 2):
        for e in (0, 1):
            v1(d, e, True).start()

    def o1(d, e, mine):
        to = moved(p, y=d, k=e)
        frm = p if mine else moved(p, y=-d, k=e)
        half = pl.ds(pl.multiple_of(to["k"] * 1024, 1024), 1024)
        return remote(go.at[:, half], gst.at[frm["y"] * 2 + frm["k"]], sent.at[O1], o1r.at[0], to)

    group = [(d, e) for d in range(4) for e in (0, 1) if d or e]
    for de in group:
        o1(*de, True).start()

    atom_of_row = lax.broadcasted_iota(jnp.int32, (128, 64), 0) // 32 + col * 4
    pick = (lax.broadcasted_iota(jnp.int32, (128, 64), 1) == atom_of_row).astype(F32)
    spread = (
        lax.broadcasted_iota(jnp.int32, (64, 2048), 1) // 32 == lax.broadcasted_iota(jnp.int32, (64, 2048), 0)
    ).astype(BF)
    size_row = sizes[...].astype(F32)
    own_size = jnp.sum(pick * size_row, axis=1, keepdims=True)
    row_ok = lax.rem(lax.broadcasted_iota(jnp.int32, (128, 1), 0), 32).astype(F32) < own_size
    paired = jnp.dot(pick.astype(BF), pattern[...].astype(F32).astype(BF), preferred_element_type=F32)
    paired = jnp.where(row_ok, paired, 0.0)
    paired = jnp.dot(paired.astype(BF), spread, preferred_element_type=F32)
    all_sizes = jnp.dot(jnp.broadcast_to(size_row, (8, 64)).astype(BF), spread, preferred_element_type=F32)[0:1]
    column_ok = lax.rem(lax.broadcasted_iota(jnp.int32, (1, 2048), 1), 32).astype(F32) < all_sizes
    mask[...] = jnp.where(column_ok, paired, 0.0).astype(BF)

    def t_share(c, mine):
        part = t2.at[pl.ds(c * 2, 2), k if mine else 1 - k]
        return remote(part, part, sent.at[TS], tr.at[0], moved(p, k=1))

    def filter_chunk(c, carry):
        t_load(c).wait()

        def strip(i, inner):
            rows = pl.ds(pl.multiple_of(i * 16, 16), 16)
            m = mask[rows, :]
            for q in range(2):
                t2[c * 2 + q, k, rows, :] = t2[c * 2 + q, k, rows, :] * m
            return inner

        lax.fori_loop(0, 8, strip, 0)
        t_share(c, True).start()
        return carry

    lax.fori_loop(0, NC, filter_chunk, 0)

    def v2(part, j, d, mine):
        axis = ORDERS[part][1]
        at = p if mine else moved(p, **{axis: -d})
        if part == 0:
            slot = gvb.at[0, lax.rem((y + d if mine else y) + turn(j), 4), :, x, at["y"], :]
        else:
            slot = gvb.at[1, lax.rem(y + FAR_ORDER[j], 4), :, at["x"], y, :]
        return remote(slot, slot, sent.at[V2], v2r.at[part, j], moved(p, **{axis: d}))

    def v2_out(part, j):
        for d in (1, 3, 2):
            v2(part, j, d, True).start()

    def v2_in(part, j):
        arrived(got.at[0, 0, 0, 0, pl.ds(0, 384)], v2r.at[part, j])

    own.wait()
    arrived(got.at[0, 0, 0, 0, pl.ds(0, 896)], v1r.at[0])
    for j in range(4):
        v2_out(0, j)
        if j < 3:
            v2_out(1, j)

    own_o.wait()
    arrived(got.at[0, 0, 0, 0, pl.ds(0, 896)], o1r.at[0])
    got[zl, x, zh, k] = gst[...].reshape(128, 1024).T

    def o2(d, mine):
        at = p if mine else moved(p, z=-d)
        slot = got.at[lax.rem(at["z"], 2), x, at["z"] // 2, k]
        return remote(slot, slot, sent.at[O2], o2r.at[0], moved(p, z=d))

    for d in (1, 3, 2):
        o2(d, True).start()

    def vy(s, d, mine):
        pair = lax.rem((y + d if mine else y) + turn(s), 4)
        slot = gvb.at[1, pair, :, :, y if mine else moved(p, y=-d)["y"], :]
        return remote(slot, slot, sent.at[VY], vyr.at[s], moved(p, y=d))

    def along_x(ref_of, send, recv, side, n, mine):
        step = 1 - 2 * side
        origin = (x if n < 2 else moved(p, x=-step)["x"]) if mine else moved(p, x=-step if n < 2 else 2)["x"]
        slot = ref_of(side if n == 2 else n, origin)
        return remote(slot, slot, send, recv.at[0 if n == side else 1], moved(p, x=step))

    def vx(s, side, n, mine):
        pair = lax.rem(y + turn(s), 4)
        return along_x(lambda half, at: gvb.at[0, pair, half, at], sent.at[VX], vxr.at[s], side, n, mine)

    def o3(t, side, n, mine):
        rows = pl.ds(t * 256, 256)
        return along_x(lambda half, at: got.at[half, at, :, k, rows], sent.at[O3], o3r.at[t], side, n, mine)

    def own_out(copy, i):
        for n in (0, 1):
            for side in (0, 1):
                copy(i, side, n if side == 0 else 1 - n, True).start()

    def pass_on(copy, i):
        if copy is vx:
            arrived(hs.at[0, 0], vxr.at[i, 0])
        else:
            arrived(hs.at[0, pl.ds(0, 2)], o3r.at[i, 0])
        for side in (0, 1):
            copy(i, side, 2, True).start()

    def rest_in(copy, i):
        if copy is vx:
            arrived(hs.at[0, pl.ds(0, 2)], vxr.at[i, 1])
        else:
            arrived(hs.at[0, pl.ds(0, 4)], o3r.at[i, 1])

    def vy_in(s):
        arrived(hs.at[0, pl.ds(0, 3)], vyr.at[s])

    def o4(t, mine):
        slot = got.at[:, :, :, k if mine else 1 - k, pl.ds(t * 256, 256)]
        return remote(slot, slot, sent.at[O4], o4r.at[t], moved(p, k=1))

    v2_in(0, 0)
    own_out(vx, 0)
    v2_out(1, 3)
    for j in range(3):
        v2_in(1, j)
        vy(0, FAR_ORDER[j], True).start()
    vy(1, 1, True).start()
    vy(1, 2, True).start()
    for j in range(1, 4):
        v2_in(0, j)
    v2_in(1, 3)
    vy(1, 3, True).start()
    for s in (2, 3):
        for d in (1, 3, 2):
            vy(s, d, True).start()

    arrived(t2.at[:, 0], tr.at[0])

    def h_own(c):
        chip = y * 2 + zh
        return pltpu.make_async_copy(hs.at[c, chip], hr.at[c, :, chip], hrr.at[c // 2])

    def h_side(c, s, mine):
        source = moved(p, y=0 if mine else -s)["y"] * 2 + zh
        return remote(
            hs.at[c, lax.rem(y + s, 4) * 2 + zh], hr.at[c, :, source], sent.at[HD], hrr.at[c // 2], moved(p, y=s)
        )

    def h_cross(c, s, mine):
        if isinstance(s, int) and s == 0:
            dst, sem = hr.at[c, :, y * 2 + (zh if mine else 1 - zh)], hrr.at[c // 2]
        else:
            dst, sem = hz.at[c, s - 1], hur.at[c, s]
        return remote(hs.at[c, lax.rem(y + s, 4) * 2 + 1 - zh], dst, sent.at[HC], sem, moved(p, z=2))

    def h_pass(c, s, mine):
        source = moved(p, y=0 if mine else -s)["y"] * 2 + 1 - zh
        return remote(hz.at[c, s - 1], hr.at[c, :, source], sent.at[HP], hrr.at[c // 2], moved(p, y=s))

    def h_on(half, s):
        for c in (half * 2, half * 2 + 1):
            h_cross(c, s, False).wait_recv()
            h_pass(c, s, True).start()

    def first(i, carry):
        half, n = i // 4, lax.rem(i, 4)
        s = turn(n)

        @pl.when(i == 0)
        def _():
            pass_on(vx, 0)
            own_out(vx, 1)
            own_out(vx, 2)

        @pl.when(i == 1)
        def _():
            pass_on(vx, 1)
            own_out(vx, 3)
            pass_on(vx, 2)

        @pl.when(i == 2)
        def _():
            pass_on(vx, 3)
            arrived(got.at[0, pl.ds(0, 3), 0, 0], o2r.at[0])
            own_out(o3, 0)
            own_out(o3, 1)

        @pl.when(half == 0)
        def _():
            rest_in(vx, n)
            vy_in(n)

        @pl.when(i == 4)
        def _():
            h_on(0, 1)
            pass_on(o3, 0)
            own_out(o3, 2)

        @pl.when(i == 6)
        def _():
            h_on(0, 3)

        pair = lax.rem(y + s, 4)
        rhs = jnp.concatenate([gvb[q, pair].reshape(2048, 128) for q in range(2)], axis=1)
        lhs = t2[pl.ds(half * 4, 4)].reshape(1024, 2048)
        h = jnp.dot(lhs, rhs, preferred_element_type=F32).astype(BF)
        for m in range(2):
            for q in range(2):
                hs[half * 2 + m, pair * 2 + q] = h[m * 512:(m + 1) * 512, q * 128:(q + 1) * 128].reshape(2, 256, 128)
        for m in range(2):
            c = half * 2 + m

            @pl.when(n == 0)
            def _():
                h_cross(c, 0, True).start()
                h_own(c).start()

            @pl.when(n > 0)
            def _():
                h_cross(c, s, True).start()

            @pl.when((n > 0) & (half == 0))
            def _():
                h_side(c, s, True).start()

        return carry

    lax.fori_loop(0, 8, first, 0)

    pass_on(o3, 1)
    own_out(o3, 3)
    h_on(0, 2)
    for s in (1, 3, 2):
        for c in (2, 3):
            h_side(c, s, True).start()
    rest_in(o3, 0)
    o4(0, True).start()
    pass_on(o3, 2)
    rest_in(o3, 1)
    o4(1, True).start()
    h_on(1, 1)
    pass_on(o3, 3)

    def s_slot(c, at):
        return out.at[pl.ds((lax.rem(at["z"], 2) * 4 + at["x"]) * 8 + c * 2, 2)]

    def s_own(c):
        return pltpu.make_async_copy(ss.at[c, 0, 0], s_slot(c, p), srr.at[0])

    def s_side(c, d):
        return remote(ss.at[c, d, 0], s_slot(c, p), sent.at[SD], srr.at[0], moved(p, x=d))

    def s_cross(c, d, straight):
        dst, sem = (s_slot(c, p), srr.at[0]) if straight else (sz.at[c, d - 1], zr.at[c, d])
        return remote(ss.at[c, d, 1], dst, sent.at[SC], sem, flip(p, "z"))

    def s_on(half, d):
        for c in (half * 2, half * 2 + 1):
            s_cross(c, d, False).wait_recv()
            remote(sz.at[c, d - 1], s_slot(c, flip(p, "z")), sent.at[SP], srr.at[0], moved(p, x=d)).start()

    def s_on_tile(t):
        d = lax.rem(t - x + 4, 4)

        @pl.when(d > 0)
        def _():
            s_on(0, d)

    def lined_up(c, q):
        rows = []
        for b in range(16):
            for j in range(4):
                n = (b // 2) * 8 + j * 2 + b % 2
                rows.append(hr[c, q, n // 8, (n % 8) * 32:(n % 8) * 32 + 32, :])
        return jnp.concatenate(rows, axis=0)

    def second(j, carry):
        half = j // 4
        d = lax.rem(j + half + (1 - half) * (4 - x), 4)
        t = lax.rem(x + d, 4)

        @pl.when(lax.rem(j, 4) == 0)
        def _():
            arrived(hr.at[pl.ds(half * 2, 2)], hrr.at[half])

        @pl.when(j == 2)
        def _():
            h_on(1, 3)

        @pl.when(half == 0)
        def _():
            @pl.when(j >= 2)
            def _():
                rest_in(o3, j)
                o4(j, True).start()

            @pl.when(j == 3)
            def _():
                h_on(1, 2)

            o4(j, False).wait_recv()

        rows = pl.ds(pl.multiple_of(t * 256, 256), 256)
        lhs = jnp.concatenate(
            [
                jnp.concatenate(
                    [got[b // 8, (b // 2) % 4, b % 2, zl if e == 0 else 1 - zl, rows, :] for b in range(16)], axis=1
                )
                for e in (0, 1)
            ],
            axis=0,
        )
        rhs = jnp.concatenate([lined_up(half * 2 + m, q) for m in range(2) for q in range(2)], axis=1)
        r = jnp.dot(lhs, rhs, preferred_element_type=F32).astype(BF)
        for m in range(2):
            c = half * 2 + m
            for e in (0, 1):
                for q in range(2):
                    ss[c, d, e, q] = r[e * 256:(e + 1) * 256, (m * 2 + q) * 128:(m * 2 + q + 1) * 128]

            @pl.when(d == 0)
            def _():
                s_cross(c, 0, True).start()
                s_own(c).start()

            @pl.when(d > 0)
            def _():
                s_cross(c, d, False).start()
                s_side(c, d).start()

        @pl.when(j == 3)
        def _():
            s_on_tile(0)

        @pl.when(j == 4)
        def _():
            s_on_tile(1)

        return carry

    lax.fori_loop(0, 8, second, 0)
    s_on_tile(2)
    s_on_tile(3)
    for d in (1, 2, 3):
        s_on(1, d)

    arrived(out, srr.at[0])
    arrived(t2.at[:, 0], sent.at[TS])
    for kind, ref in (
        (V1, got.at[0, 0, 0, 0, pl.ds(0, 896)]), (O1, got.at[0, 0, 0, 0, pl.ds(0, 896)]),
        (V2, got.at[0, pl.ds(0, 3), 0, 0]), (O2, got.at[0, pl.ds(0, 3), 0, 0]),
        (VY, got.at[0, pl.ds(0, 3), :, 0]), (VX, got.at[0, pl.ds(0, 3), :, 0]),
        (O3, got.at[0, pl.ds(0, 3)]), (O4, got.at[0]),
        (HC, got.at[0, pl.ds(0, 2)]), (HD, got.at[0, pl.ds(0, 3), :, 0]), (HP, got.at[0, pl.ds(0, 3), :, 0]),
        (SC, got.at[0, pl.ds(0, 2)]), (SD, got.at[0, pl.ds(0, 3), :, 0]), (SP, got.at[0, pl.ds(0, 3), :, 0]),
    ):
        arrived(ref, sent.at[kind])


def restack(blocks, out, source, target, in_sem, out_sem):
    parts = in_sem.shape[0]
    lams = out.shape[0] // parts

    def load(i):
        some = pl.ds(i * lams, lams)
        return pltpu.make_async_copy(blocks.at[:, some], source.at[:, some], in_sem.at[i])

    def store(i):
        some = pl.ds(i * lams, lams)
        return pltpu.make_async_copy(target.at[some], out.at[some], out_sem.at[i])

    for i in range(parts):
        load(i).start()
    to = lax.broadcasted_iota(jnp.int32, (256, 256), 0)
    frm = lax.broadcasted_iota(jnp.int32, (256, 256), 1)
    one_hot = ((to // 16 == lax.rem(frm, 16)) & (lax.rem(to, 16) == frm // 16)).astype(BF)

    def part(i, carry):
        load(i).wait()
        for pair in range(lams // 32):
            for group in range(blocks.shape[0] // 16):
                ps = slice(group * 16, group * 16 + 16)
                at = [pl.ds(pl.multiple_of(i * lams + pair * 32 + h * 16, 16), 16) for h in range(2)]
                rows = jnp.concatenate([source[ps, at[h], :].reshape(256, 128) for h in range(2)], axis=1)
                moved_rows = jnp.dot(one_hot, rows, preferred_element_type=F32).astype(BF)
                for h in range(2):
                    target[at[h], ps, :] = moved_rows[:, h * 128:(h + 1) * 128].reshape(16, 16, 128)
        store(i).start()
        return carry

    lax.fori_loop(0, parts, part, 0)
    for i in range(parts):
        store(i).wait()


def per_device(three_centre, green_virt, green_occ, pattern, block_sizes, atom_order):
    vmem = pl.BlockSpec(memory_space=pltpu.VMEM)
    dma = pltpu.SemaphoreType.DMA
    blocks = pl.pallas_call(
        kernel,
        out_shape=jax.ShapeDtypeStruct((64, 256, 128), BF),
        in_specs=[vmem, vmem, pl.BlockSpec(memory_space=pltpu.SMEM), vmem, vmem, pl.BlockSpec(memory_space=pl.ANY)],
        out_specs=pl.BlockSpec(memory_space=pl.ANY),
        scratch_shapes=[
            pltpu.VMEM((4, 16, 16, 128), F32),
            pltpu.VMEM((2, 2, 4, 16, 128), BF),
            pltpu.VMEM((2, 4, 2, 4, 4, 2, 32, 128), BF),
            pltpu.VMEM((8, 2, 128, 2048), BF),
            pltpu.VMEM((128, 2048), BF),
            pltpu.VMEM((NC, 8, 2, 256, 128), BF),
            pltpu.VMEM((NC, 3, 2, 256, 128), BF),
            pltpu.VMEM((NC, 2, 8, 256, 128), BF),
            pltpu.VMEM((8, 16, 1024), BF),
            pltpu.VMEM((2, 4, 2, 2, 1024, 128), BF),
            pltpu.VMEM((NC, 4, 2, 2, 256, 128), BF),
            pltpu.VMEM((NC, 3, 2, 256, 128), BF),
            dma((NC,)), dma((2,)), dma((15,)), dma((1,)), dma((1,)), dma((2, 4)), dma((4,)), dma((4, 2)),
            dma((1,)), dma((1,)), dma((4, 2)), dma((4,)), dma((NC, 4)), dma((2,)), dma((NC, 4)), dma((1,)),
        ],
        compiler_params=pltpu.CompilerParams(
            collective_id=0, has_side_effects=True, vmem_limit_bytes=56 * 2**20
        ),
        name="contract",
    )(green_virt, green_occ, atom_order, block_sizes.reshape(1, -1), pattern, three_centre)
    anywhere = pl.BlockSpec(memory_space=pl.ANY)
    return pl.pallas_call(
        restack,
        out_shape=jax.ShapeDtypeStruct((256, 64, 128), BF),
        in_specs=[anywhere],
        out_specs=anywhere,
        scratch_shapes=[pltpu.VMEM((64, 256, 128), BF), pltpu.VMEM((256, 64, 128), BF), dma((2,)), dma((2,))],
        compiler_params=pltpu.CompilerParams(vmem_limit_bytes=60 * 2**20),
        name="restack",
    )(blocks)


def solution(mesh):
    in_specs = (P("row", "col", None), P(("row", "col"), None), P(("row", "col"), None), P(), P(), P())
    return jax.shard_map(
        per_device, mesh=mesh, in_specs=in_specs, out_specs=P("row", None, "col"), check_vma=False
    )
```

```python
import jax
import jax.numpy as jnp
from jax import lax
from jax.experimental import pallas as pl
from jax.experimental.pallas import tpu as pltpu
from jax.sharding import PartitionSpec as P

MESH = pl.DeviceIdType.MESH
BF = jnp.bfloat16
F32 = jnp.float32
NC = 4
ORDERS = ("zyx", "zxy")
TS, V1, V2, VY, VX, O1, O2, O3, O4, HC, HD, HP, SC, SD, SP = range(15)
FAR_ORDER = (1, 3, 2, 0)


def me():
    r = lax.axis_index("row")
    c = lax.axis_index("col")
    return {
        "x": lax.rem(r, 4),
        "y": c // 4,
        "z": lax.rem(c // 2, 2) * 2 + r // 4,
        "k": lax.rem(c, 2),
    }


def turn(i):
    return i + (i // 2) * (5 - 2 * i)


def far_first(i):
    return (2 + 3 * i + (i // 2) * (7 - 2 * i)) % 4 if isinstance(i, int) else lax.rem(2 + 3 * i + (i // 2) * (7 - 2 * i), 4)


def stage(c):
    return c // 2 + c // 3


def device(p):
    return {"row": lax.rem(p["z"], 2) * 4 + p["x"], "col": (p["y"] * 2 + p["z"] // 2) * 2 + p["k"]}


def moved(p, **by):
    q = dict(p)
    for axis, d in by.items():
        q[axis] = lax.rem(p[axis] + d, 2) if axis == "k" else lax.rem(p[axis] + d + 4, 4)
    return q


def flip(p, axis):
    q = dict(p)
    q[axis] = p[axis] + 1 - 2 * lax.rem(p[axis], 2)
    return q


def partners(p):
    found = [moved(p, k=1)]
    for d in (1, 2, 3):
        for e in (0, 1):
            found.append(moved(p, y=d, k=e))
            found.append(moved(p, z=d, k=e))
        found.append(moved(p, x=d))
    return found


def kernel(gv_hbm, go_hbm, order, sizes, pattern, t_hbm, out,
           gv, go, turned, gp, gvb, t2, mask, hs, hz, hr, gst, got, ss, sz,
           t_sem, own_sem, sent, tr, v1r, v2r, vyr, vxr, o1r, o2r, o3r, o4r, hur, hrr, zr, srr):
    p = me()
    x, y, z, k = p["x"], p["y"], p["z"], p["k"]
    zl, zh, yl, yh = lax.rem(z, 2), z // 2, lax.rem(y, 2), y // 2
    row, col = lax.axis_index("row"), lax.axis_index("col")

    def remote(src, dst, send, recv, to):
        return pltpu.make_async_remote_copy(
            src_ref=src, dst_ref=dst, send_sem=send, recv_sem=recv, device_id=device(to), device_id_type=MESH
        )

    def arrived(ref, sem):
        pltpu.make_async_copy(ref, ref, sem).wait()

    def t_load(c):
        two = pl.ds(c * 2, 2)
        return pltpu.make_async_copy(t_hbm.at[two], t2.at[two, k], t_sem.at[c])

    barrier = pltpu.get_barrier_semaphore()
    peers = partners(p)
    for q in peers:
        pl.semaphore_signal(barrier, inc=1, device_id=device(q), device_id_type=MESH)

    gv_load = pltpu.make_async_copy(gv_hbm, gv, own_sem.at[2])
    go_load = pltpu.make_async_copy(go_hbm, go, own_sem.at[3])
    gv_load.start()
    go_load.start()
    for c in range(NC):
        t_load(c).start()

    lane_slot = lax.broadcasted_iota(jnp.int32, (16, 128), 1) // 32
    gv_load.wait()
    for b in range(16):
        source = gv[:, b * 128:(b + 1) * 128].astype(F32)
        for t in range(4):
            turned[t, b] = pltpu.roll(source, t * 32, 1) if t else source

    def permute(j, carry):
        wanted = jnp.zeros((16, 128), jnp.int32)
        for s in range(4):
            wanted = jnp.where(lane_slot == s, order[4 * j + s], wanted)
        block = jnp.zeros((16, 128), F32)
        for t in range(4):
            first_atom = wanted - lax.rem(lane_slot - t + 4, 4)
            for b in range(16):
                block = jnp.where(first_atom == 4 * b, turned[t, b], block)
        gp[lax.rem(j, 2), lax.rem(j // 2, 2), j // 4] = block.astype(BF)
        return carry

    lax.fori_loop(0, 16, permute, 0)

    def rows16(core):
        return pl.ds(pl.multiple_of(core * 16, 16), 16)

    own = pltpu.make_async_copy(gp.at[k], gvb.at[:, :, zl, x, y, zh, rows16(k)], own_sem.at[0])
    own.start()
    own_o = pltpu.make_async_copy(
        go.at[:, pl.ds(pl.multiple_of(k * 1024, 1024), 1024)], gst.at[y * 2 + k], own_sem.at[1]
    )
    go_load.wait()
    own_o.start()

    pl.semaphore_wait(barrier, len(peers))

    def v1(part, d, e):
        to = moved(p, z=d, k=e)
        return remote(
            gp.at[to["k"], part], gvb.at[part, :, zl, x, y, zh, rows16(k)], sent.at[V1], v1r.at[part], to
        )

    v1_targets = [(0, 1)] + [(d, e) for d in (1, 3, 2) for e in (0, 1)]
    for part in (1, 0):
        for d, e in v1_targets:
            v1(part, d, e).start()

    def o1(d, e, mine):
        to = moved(p, y=d, k=e)
        frm = p if mine else moved(p, y=-d, k=e)
        half = pl.ds(pl.multiple_of(to["k"] * 1024, 1024), 1024)
        return remote(go.at[:, half], gst.at[frm["y"] * 2 + frm["k"]], sent.at[O1], o1r.at[0], to)

    group = [(d, e) for d in range(4) for e in (0, 1) if d or e]
    for de in group:
        o1(*de, True).start()

    atom_of_row = lax.broadcasted_iota(jnp.int32, (128, 64), 0) // 32 + col * 4
    pick = (lax.broadcasted_iota(jnp.int32, (128, 64), 1) == atom_of_row).astype(F32)
    spread = (
        lax.broadcasted_iota(jnp.int32, (64, 2048), 1) // 32 == lax.broadcasted_iota(jnp.int32, (64, 2048), 0)
    ).astype(BF)
    size_row = sizes[...].astype(F32)
    own_size = jnp.sum(pick * size_row, axis=1, keepdims=True)
    row_ok = lax.rem(lax.broadcasted_iota(jnp.int32, (128, 1), 0), 32).astype(F32) < own_size
    paired = jnp.dot(pick.astype(BF), pattern[...].astype(F32).astype(BF), preferred_element_type=F32)
    paired = jnp.where(row_ok, paired, 0.0)
    paired = jnp.dot(paired.astype(BF), spread, preferred_element_type=F32)
    all_sizes = jnp.dot(jnp.broadcast_to(size_row, (8, 64)).astype(BF), spread, preferred_element_type=F32)[0:1]
    column_ok = lax.rem(lax.broadcasted_iota(jnp.int32, (1, 2048), 1), 32).astype(F32) < all_sizes
    mask[...] = jnp.where(column_ok, paired, 0.0).astype(BF)

    def t_share(c, mine):
        part = t2.at[pl.ds(c * 2, 2), k if mine else 1 - k]
        return remote(part, part, sent.at[TS], tr.at[0], moved(p, k=1))

    def filter_chunk(c, carry):
        t_load(c).wait()

        def strip(i, inner):
            rows = pl.ds(pl.multiple_of(i * 16, 16), 16)
            m = mask[rows, :]
            for q in range(2):
                t2[c * 2 + q, k, rows, :] = t2[c * 2 + q, k, rows, :] * m
            return inner

        lax.fori_loop(0, 8, strip, 0)
        t_share(c, True).start()
        return carry

    lax.fori_loop(0, NC, filter_chunk, 0)

    def v2(part, j, d, mine):
        axis = ORDERS[part][1]
        at = p if mine else moved(p, **{axis: -d})
        if part == 0:
            slot = gvb.at[0, lax.rem((y + d if mine else y) + turn(j), 4), :, x, at["y"], :]
        else:
            slot = gvb.at[1, lax.rem(y + FAR_ORDER[j], 4), :, at["x"], y, :]
        return remote(slot, slot, sent.at[V2], v2r.at[part, j], moved(p, **{axis: d}))

    def v2_out(part, j):
        for d in (1, 3, 2):
            v2(part, j, d, True).start()

    def v2_in(part, j):
        arrived(gst.at[pl.ds(0, 3)], v2r.at[part, j])

    own.wait()
    for part in (1, 0):
        arrived(turned.at[0, pl.ds(0, 14)], v1r.at[part])
        for j in range(3):
            v2_out(part, j)

    own_o.wait()
    arrived(gst.at[pl.ds(0, 7)], o1r.at[0])
    got[zl, x, zh, k] = gst[...].reshape(128, 1024).T.reshape(4, 4, 64, 128)

    def o2(d, mine):
        at = p if mine else moved(p, z=-d)
        slot = got.at[lax.rem(at["z"], 2), x, at["z"] // 2, k]
        return remote(slot, slot, sent.at[O2], o2r.at[0], moved(p, z=d))

    for d in (1, 3, 2):
        o2(d, True).start()

    def vy(s, d, mine):
        pair = lax.rem((y + d if mine else y) + turn(s), 4)
        slot = gvb.at[1, pair, :, :, y if mine else moved(p, y=-d)["y"], :]
        return remote(slot, slot, sent.at[VY], vyr.at[s], moved(p, y=d))

    def along_x(ref_of, send, recv, side, n, mine):
        step = 1 - 2 * side
        origin = (x if n < 2 else moved(p, x=-step)["x"]) if mine else moved(p, x=-step if n < 2 else 2)["x"]
        slot = ref_of(side if n == 2 else n, origin)
        return remote(slot, slot, send, recv.at[0 if n == side else 1], moved(p, x=step))

    def vx(s, side, n, mine):
        pair = lax.rem(y + turn(s), 4)
        return along_x(lambda half, at: gvb.at[0, pair, half, at], sent.at[VX], vxr.at[s], side, n, mine)

    def o3(t, side, n, mine):
        return along_x(lambda half, at: got.at[half, at, :, k, :, t], sent.at[O3], o3r.at[t], side, n, mine)

    def own_out(copy, i):
        for n in (0, 1):
            for side in (0, 1):
                copy(i, side, n if side == 0 else 1 - n, True).start()

    def pass_on(copy, i):
        if copy is vx:
            arrived(hs.at[0, 0], vxr.at[i, 0])
        else:
            arrived(hs.at[0, pl.ds(0, 2)], o3r.at[i, 0])
        for side in (0, 1):
            copy(i, side, 2, True).start()

    def rest_in(copy, i):
        if copy is vx:
            arrived(hs.at[0, pl.ds(0, 2)], vxr.at[i, 1])
        else:
            arrived(hs.at[0, pl.ds(0, 4)], o3r.at[i, 1])

    def vy_in(s):
        arrived(hs.at[0, pl.ds(0, 3)], vyr.at[s])

    def o4(t, mine):
        slot = got.at[:, :, :, k if mine else 1 - k, :, t]
        return remote(slot, slot, sent.at[O4], o4r.at[t], moved(p, k=1))

    v2_in(1, 0)
    vy(0, FAR_ORDER[0], True).start()
    v2_in(0, 0)
    own_out(vx, 0)
    for j in (1, 2):
        v2_in(1, j)
        vy(0, FAR_ORDER[j], True).start()
    v2_out(1, 3)
    v2_out(0, 3)
    vy(1, 1, True).start()
    vy(1, 2, True).start()
    v2_in(0, 1)
    pass_on(vx, 0)
    own_out(vx, 1)
    v2_in(0, 2)
    own_out(vx, 2)
    v2_in(1, 3)
    vy(1, 3, True).start()
    for s in (2, 3):
        for d in (1, 3, 2):
            vy(s, d, True).start()

    arrived(t2.at[:, 0], tr.at[0])

    def h_own(c):
        chip = y * 2 + zh
        return pltpu.make_async_copy(hs.at[c, chip], hr.at[c, :, chip], hrr.at[stage(c)])

    def h_side(c, s, mine):
        source = moved(p, y=0 if mine else -s)["y"] * 2 + zh
        return remote(
            hs.at[c, lax.rem(y + s, 4) * 2 + zh], hr.at[c, :, source], sent.at[HD], hrr.at[stage(c)], moved(p, y=s)
        )

    def h_cross(c, s, mine):
        if isinstance(s, int) and s == 0:
            dst, sem = hr.at[c, :, y * 2 + (zh if mine else 1 - zh)], hrr.at[stage(c)]
        else:
            dst, sem = hz.at[c, s - 1], hur.at[c, s]
        return remote(hs.at[c, lax.rem(y + s, 4) * 2 + 1 - zh], dst, sent.at[HC], sem, moved(p, z=2))

    def h_pass(c, s, mine):
        source = moved(p, y=0 if mine else -s)["y"] * 2 + 1 - zh
        return remote(hz.at[c, s - 1], hr.at[c, :, source], sent.at[HP], hrr.at[stage(c)], moved(p, y=s))

    def h_on(c, s):
        h_cross(c, s, False).wait_recv()
        h_pass(c, s, True).start()

    def first(half, n):
        s = turn(n)
        pair = lax.rem(y + s, 4)
        rhs = jnp.concatenate([gvb[q, pair].reshape(2048, 128) for q in range(2)], axis=1)
        lhs = t2[pl.ds(half * 4, 4)].reshape(1024, 2048)
        h = jnp.dot(lhs, rhs, preferred_element_type=F32).astype(BF)
        for m in range(2):
            c = half * 2 + m
            for q in range(2):
                hs[c, pair * 2 + q] = h[m * 512:(m + 1) * 512, q * 128:(q + 1) * 128].reshape(2, 256, 128)
            if isinstance(n, int):
                h_cross(c, s, True).start()
                h_own(c).start()
            elif half == 0:
                h_cross(c, s, True).start()
                h_side(c, s, True).start()
            elif m == 0:
                h_cross(c, s, True).start()

    def first_own(half, carry):
        first(half, 0)
        return carry

    def first_early(n, carry):
        @pl.when(n == 1)
        def _():
            pass_on(vx, 1)
            v2_in(0, 3)
            own_out(vx, 3)
            pass_on(vx, 2)

        @pl.when(n == 2)
        def _():
            pass_on(vx, 3)
            arrived(got.at[0, pl.ds(0, 3), 0, 0], o2r.at[0])
            own_out(o3, 0)
            own_out(o3, 1)

        rest_in(vx, n)
        vy_in(n)
        first(0, n)
        return carry

    def first_late(n, carry):
        @pl.when(n == 1)
        def _():
            h_on(0, 1)
            h_on(1, 1)
            pass_on(o3, 0)
            own_out(o3, 2)

        @pl.when(n == 3)
        def _():
            h_on(0, 3)
            h_on(1, 3)

        first(1, n)
        return carry

    rest_in(vx, 0)
    vy_in(0)
    lax.fori_loop(0, 2, first_own, 0)
    lax.fori_loop(1, 4, first_early, 0)
    lax.fori_loop(1, 4, first_late, 0)

    for s in (1, 3, 2):
        h_cross(3, s, True).start()
    pass_on(o3, 1)
    own_out(o3, 3)
    h_on(0, 2)
    h_on(1, 2)
    for s in (1, 3, 2):
        h_side(2, s, True).start()
    rest_in(o3, 0)
    o4(0, True).start()
    pass_on(o3, 2)
    h_on(2, 1)
    rest_in(o3, 1)
    o4(1, True).start()
    h_on(2, 3)
    pass_on(o3, 3)

    whole = pl.ds(0, 256)

    def s_slot(c, at, rows):
        return out.at[pl.ds((lax.rem(at["z"], 2) * 4 + at["x"]) * 8 + c * 2, 2), rows]

    def s_out(c, d, rows, part):
        block = ss.at[c, lax.rem(x + d, 4)]

        def stay():
            pltpu.make_async_copy(block.at[0, :, rows], s_slot(c, p, rows), srr.at[0]).start()
            remote(block.at[1, :, rows], s_slot(c, p, rows), sent.at[SC], srr.at[0], flip(p, "z")).start()

        def leave():
            s_cross(c, d, rows, part).start()
            remote(block.at[0, :, rows], s_slot(c, p, rows), sent.at[SD], srr.at[0], moved(p, x=d)).start()

        if isinstance(d, int):
            leave() if d else stay()
        else:
            pl.when(d == 0)(stay)
            pl.when(d > 0)(leave)

    def s_cross(c, d, rows, part):
        return remote(
            ss.at[c, lax.rem(x + d, 4), 1, :, rows], sz.at[c, d - 1, :, rows], sent.at[SC], zr.at[part, c, d], flip(p, "z")
        )

    def s_on(c, d, rows, part):
        s_cross(c, d, rows, part).wait_recv()
        remote(
            sz.at[c, d - 1, :, rows], s_slot(c, flip(p, "z"), rows), sent.at[SP], srr.at[0], moved(p, x=d)
        ).start()

    def s_on_early(part):
        for i in range(3):
            for c in (0, 1):
                s_on(c, far_first(i), pl.ds(part * 128, 128), part)

    def lined_up(c, q):
        rows = []
        for b in range(16):
            for j in range(4):
                n = (b // 2) * 8 + j * 2 + b % 2
                rows.append(hr[c, q, n // 8, (n % 8) * 32:(n % 8) * 32 + 32, :])
        return jnp.concatenate(rows, axis=0)

    def second(chunks, rows_of):
        lhs = jnp.concatenate(
            [
                jnp.concatenate(
                    [
                        rows_of(got.at[b // 8, (b // 2) % 4, b % 2, zl if e == 0 else 1 - zl]).reshape(256, 128)
                        for b in range(16)
                    ],
                    axis=1,
                )
                for e in (0, 1)
            ],
            axis=0,
        )
        rhs = jnp.concatenate([lined_up(c, q) for c in chunks for q in range(2)], axis=1)
        return jnp.dot(lhs, rhs, preferred_element_type=F32).astype(BF)

    arrived(hr.at[pl.ds(0, 2)], hrr.at[0])

    def second_early(t, carry):
        @pl.when(t == 2)
        def _():
            h_on(2, 2)
            for s in (1, 3, 2):
                h_side(3, s, True).start()
            h_on(3, 1)
            rest_in(o3, 2)
            o4(2, True).start()

        @pl.when(t == 3)
        def _():
            rest_in(o3, 3)
            o4(3, True).start()
            h_on(3, 3)

        o4(t, False).wait_recv()
        r = second((0, 1), lambda ref: ref[:, t])
        rows = pl.ds(pl.multiple_of(t * 64, 64), 64)
        for c in (0, 1):
            for owner in range(4):
                for e in (0, 1):
                    at = e * 256 + owner * 64
                    for q in range(2):
                        ss[c, owner, e, q, rows] = r[at:at + 64, (c * 2 + q) * 128:(c * 2 + q + 1) * 128]

        for part in (0, 1):

            @pl.when(t == part * 2 + 1)
            def _():
                for i in range(4):
                    for c in (0, 1):
                        s_out(c, far_first(i), pl.ds(part * 128, 128), part)

        return carry

    lax.fori_loop(0, 4, second_early, 0)
    h_on(3, 2)

    def second_late(c, carry):
        arrived(hr.at[c], hrr.at[c - 1])

        def tile(i, inner):
            d = far_first(i)
            owner = lax.rem(x + d, 4)
            r = second((c,), lambda ref: ref[owner])
            for e in (0, 1):
                for q in range(2):
                    ss[c, owner, e, q] = r[e * 256:(e + 1) * 256, q * 128:(q + 1) * 128]
            s_out(c, d, whole, 0)
            return inner

        lax.fori_loop(0, 4, tile, 0)
        s_on_early(c - 2)
        return carry

    lax.fori_loop(2, 4, second_late, 0)

    def s_on_late(i, carry):
        s_on(2 + i // 3, far_first(lax.rem(i, 3)), whole, 0)
        return carry

    lax.fori_loop(0, 6, s_on_late, 0)

    arrived(out, srr.at[0])
    arrived(t2.at[:, 0], sent.at[TS])
    for kind, ref in (
        (V1, gst.at[pl.ds(0, 7)]), (O1, gst.at[pl.ds(0, 7)]),
        (V2, got.at[0, pl.ds(0, 3), 0, 0]), (O2, got.at[0, pl.ds(0, 3), 0, 0]),
        (VY, got.at[0, pl.ds(0, 3), :, 0]), (VX, got.at[0, pl.ds(0, 3), :, 0]),
        (O3, got.at[0, pl.ds(0, 3)]), (O4, got.at[0]),
        (HC, got.at[0, pl.ds(0, 2)]), (HD, got.at[0, pl.ds(0, 3), :, 0]), (HP, got.at[0, pl.ds(0, 3), :, 0]),
        (SC, got.at[0, pl.ds(0, 2)]), (SD, got.at[0, pl.ds(0, 3), :, 0]), (SP, got.at[0, pl.ds(0, 3), :, 0]),
    ):
        arrived(ref, sent.at[kind])


def restack(blocks, out, source, target, in_sem, out_sem):
    parts = in_sem.shape[0]
    lams = out.shape[0] // parts

    def load(i):
        some = pl.ds(i * lams, lams)
        return pltpu.make_async_copy(blocks.at[:, some], source.at[:, some], in_sem.at[i])

    def store(i):
        some = pl.ds(i * lams, lams)
        return pltpu.make_async_copy(target.at[some], out.at[some], out_sem.at[i])

    for i in range(parts):
        load(i).start()
    to = lax.broadcasted_iota(jnp.int32, (256, 256), 0)
    frm = lax.broadcasted_iota(jnp.int32, (256, 256), 1)
    one_hot = ((to // 16 == lax.rem(frm, 16)) & (lax.rem(to, 16) == frm // 16)).astype(BF)

    def part(i, carry):
        load(i).wait()
        for pair in range(lams // 32):
            for group in range(blocks.shape[0] // 16):
                ps = slice(group * 16, group * 16 + 16)
                at = [pl.ds(pl.multiple_of(i * lams + pair * 32 + h * 16, 16), 16) for h in range(2)]
                rows = jnp.concatenate([source[ps, at[h], :].reshape(256, 128) for h in range(2)], axis=1)
                moved_rows = jnp.dot(one_hot, rows, preferred_element_type=F32).astype(BF)
                for h in range(2):
                    target[at[h], ps, :] = moved_rows[:, h * 128:(h + 1) * 128].reshape(16, 16, 128)
        store(i).start()
        return carry

    lax.fori_loop(0, parts, part, 0)
    for i in range(parts):
        store(i).wait()


def per_device(three_centre, green_virt, green_occ, pattern, block_sizes, atom_order):
    vmem = pl.BlockSpec(memory_space=pltpu.VMEM)
    anywhere = pl.BlockSpec(memory_space=pl.ANY)
    dma = pltpu.SemaphoreType.DMA
    blocks = pl.pallas_call(
        kernel,
        out_shape=jax.ShapeDtypeStruct((64, 256, 128), BF),
        in_specs=[anywhere, anywhere, pl.BlockSpec(memory_space=pltpu.SMEM), vmem, vmem, anywhere],
        out_specs=anywhere,
        scratch_shapes=[
            pltpu.VMEM((16, 2048), BF),
            pltpu.VMEM((16, 2048), BF),
            pltpu.VMEM((4, 16, 16, 128), F32),
            pltpu.VMEM((2, 2, 4, 16, 128), BF),
            pltpu.VMEM((2, 4, 2, 4, 4, 2, 32, 128), BF),
            pltpu.VMEM((8, 2, 128, 2048), BF),
            pltpu.VMEM((128, 2048), BF),
            pltpu.VMEM((NC, 8, 2, 256, 128), BF),
            pltpu.VMEM((NC, 3, 2, 256, 128), BF),
            pltpu.VMEM((NC, 2, 8, 256, 128), BF),
            pltpu.VMEM((8, 16, 1024), BF),
            pltpu.VMEM((2, 4, 2, 2, 4, 4, 64, 128), BF),
            pltpu.VMEM((NC, 4, 2, 2, 256, 128), BF),
            pltpu.VMEM((NC, 3, 2, 256, 128), BF),
            dma((NC,)), dma((4,)), dma((15,)), dma((1,)), dma((2,)), dma((2, 4)), dma((4,)), dma((4, 2)),
            dma((1,)), dma((1,)), dma((4, 2)), dma((4,)), dma((NC, 4)), dma((3,)), dma((2, NC, 4)), dma((1,)),
        ],
        compiler_params=pltpu.CompilerParams(
            collective_id=0, has_side_effects=True, vmem_limit_bytes=56 * 2**20
        ),
        name="contract",
    )(green_virt, green_occ, atom_order, block_sizes.reshape(1, -1), pattern, three_centre)
    return pl.pallas_call(
        restack,
        out_shape=jax.ShapeDtypeStruct((256, 64, 128), BF),
        in_specs=[anywhere],
        out_specs=anywhere,
        scratch_shapes=[pltpu.VMEM((64, 256, 128), BF), pltpu.VMEM((256, 64, 128), BF), dma((2,)), dma((2,))],
        compiler_params=pltpu.CompilerParams(vmem_limit_bytes=60 * 2**20),
        name="restack",
    )(blocks)


def solution(mesh):
    in_specs = (P("row", "col", None), P(("row", "col"), None), P(("row", "col"), None), P(), P(), P())
    return jax.shard_map(
        per_device, mesh=mesh, in_specs=in_specs, out_specs=P("row", None, "col"), check_vma=False
    )
```

```python
import jax
import jax.numpy as jnp
from jax import lax
from jax.experimental import pallas as pl
from jax.experimental.pallas import tpu as pltpu
from jax.sharding import PartitionSpec as P

MESH = pl.DeviceIdType.MESH
BF = jnp.bfloat16
F32 = jnp.float32
NC = 4
ORDERS = ("zyx", "zxy")
TS, V1, V2, VY, VX, O1, O2, O3, O4, HC, HD, HP, SC, SD, SP = range(15)
FAR_ORDER = (1, 3, 2, 0)


def me():
    r = lax.axis_index("row")
    c = lax.axis_index("col")
    return {
        "x": lax.rem(r, 4),
        "y": c // 4,
        "z": lax.rem(c // 2, 2) * 2 + r // 4,
        "k": lax.rem(c, 2),
    }


def turn(i):
    return i + (i // 2) * (5 - 2 * i)


def far_first(i):
    return (2 + 3 * i + (i // 2) * (7 - 2 * i)) % 4 if isinstance(i, int) else lax.rem(2 + 3 * i + (i // 2) * (7 - 2 * i), 4)


def stage(c):
    return c // 2 + c // 3


def device(p):
    return {"row": lax.rem(p["z"], 2) * 4 + p["x"], "col": (p["y"] * 2 + p["z"] // 2) * 2 + p["k"]}


def moved(p, **by):
    q = dict(p)
    for axis, d in by.items():
        q[axis] = lax.rem(p[axis] + d, 2) if axis == "k" else lax.rem(p[axis] + d + 4, 4)
    return q


def flip(p, axis):
    q = dict(p)
    q[axis] = p[axis] + 1 - 2 * lax.rem(p[axis], 2)
    return q


def partners(p):
    found = [moved(p, k=1)]
    for d in (1, 2, 3):
        for e in (0, 1):
            found.append(moved(p, y=d, k=e))
            found.append(moved(p, z=d, k=e))
        found.append(moved(p, x=d))
    return found


def kernel(gv, go, order, sizes, pattern, t_hbm, out,
           turned, gp, gvb, t2, mask, hs, hz, hr, gst, got, ss, sz,
           t_sem, own_sem, sent, tr, v1r, v2r, vyr, vxr, o1r, o2r, o3r, o4r, hur, hrr, zr, srr):
    p = me()
    x, y, z, k = p["x"], p["y"], p["z"], p["k"]
    zl, zh, yl, yh = lax.rem(z, 2), z // 2, lax.rem(y, 2), y // 2
    row, col = lax.axis_index("row"), lax.axis_index("col")

    def remote(src, dst, send, recv, to):
        return pltpu.make_async_remote_copy(
            src_ref=src, dst_ref=dst, send_sem=send, recv_sem=recv, device_id=device(to), device_id_type=MESH
        )

    def arrived(ref, sem):
        pltpu.make_async_copy(ref, ref, sem).wait()

    def t_load(c):
        two = pl.ds(c * 2, 2)
        return pltpu.make_async_copy(t_hbm.at[two], t2.at[two, k], t_sem.at[c])

    barrier = pltpu.get_barrier_semaphore()
    peers = partners(p)
    for q in peers:
        pl.semaphore_signal(barrier, inc=1, device_id=device(q), device_id_type=MESH)

    for c in range(NC):
        t_load(c).start()

    lane_slot = lax.broadcasted_iota(jnp.int32, (16, 128), 1) // 32
    for b in range(16):
        source = gv[:, b * 128:(b + 1) * 128].astype(F32)
        for t in range(4):
            turned[t, b] = pltpu.roll(source, t * 32, 1) if t else source

    def permute(j, carry):
        wanted = jnp.zeros((16, 128), jnp.int32)
        for s in range(4):
            wanted = jnp.where(lane_slot == s, order[4 * j + s], wanted)
        block = jnp.zeros((16, 128), F32)
        for t in range(4):
            first_atom = wanted - lax.rem(lane_slot - t + 4, 4)
            for b in range(16):
                block = jnp.where(first_atom == 4 * b, turned[t, b], block)
        gp[lax.rem(j, 2), lax.rem(j // 2, 2), j // 4] = block.astype(BF)
        return carry

    lax.fori_loop(0, 16, permute, 0)

    def rows16(core):
        return pl.ds(pl.multiple_of(core * 16, 16), 16)

    own = pltpu.make_async_copy(gp.at[k], gvb.at[:, :, zl, x, y, zh, rows16(k)], own_sem.at[0])
    own.start()
    own_o = pltpu.make_async_copy(
        go.at[:, pl.ds(pl.multiple_of(k * 1024, 1024), 1024)], gst.at[y * 2 + k], own_sem.at[1]
    )
    own_o.start()

    pl.semaphore_wait(barrier, len(peers))

    def v1(part, d, e):
        to = moved(p, z=d, k=e)
        return remote(
            gp.at[to["k"], part], gvb.at[part, :, zl, x, y, zh, rows16(k)], sent.at[V1], v1r.at[part], to
        )

    v1_targets = [(0, 1)] + [(d, e) for d in (1, 3, 2) for e in (0, 1)]
    for part in (1, 0):
        for d, e in v1_targets:
            v1(part, d, e).start()

    def o1(d, e, mine):
        to = moved(p, y=d, k=e)
        frm = p if mine else moved(p, y=-d, k=e)
        half = pl.ds(pl.multiple_of(to["k"] * 1024, 1024), 1024)
        return remote(go.at[:, half], gst.at[frm["y"] * 2 + frm["k"]], sent.at[O1], o1r.at[0], to)

    group = [(d, e) for d in range(4) for e in (0, 1) if d or e]
    for de in group:
        o1(*de, True).start()

    atom_of_row = lax.broadcasted_iota(jnp.int32, (128, 64), 0) // 32 + col * 4
    pick = (lax.broadcasted_iota(jnp.int32, (128, 64), 1) == atom_of_row).astype(F32)
    spread = (
        lax.broadcasted_iota(jnp.int32, (64, 2048), 1) // 32 == lax.broadcasted_iota(jnp.int32, (64, 2048), 0)
    ).astype(BF)
    size_row = sizes[...].astype(F32)
    own_size = jnp.sum(pick * size_row, axis=1, keepdims=True)
    row_ok = lax.rem(lax.broadcasted_iota(jnp.int32, (128, 1), 0), 32).astype(F32) < own_size
    paired = jnp.dot(pick.astype(BF), pattern[...].astype(F32).astype(BF), preferred_element_type=F32)
    paired = jnp.where(row_ok, paired, 0.0)
    paired = jnp.dot(paired.astype(BF), spread, preferred_element_type=F32)
    all_sizes = jnp.dot(jnp.broadcast_to(size_row, (8, 64)).astype(BF), spread, preferred_element_type=F32)[0:1]
    column_ok = lax.rem(lax.broadcasted_iota(jnp.int32, (1, 2048), 1), 32).astype(F32) < all_sizes
    mask[...] = jnp.where(column_ok, paired, 0.0).astype(BF)

    def t_share(c, mine):
        part = t2.at[pl.ds(c * 2, 2), k if mine else 1 - k]
        return remote(part, part, sent.at[TS], tr.at[0], moved(p, k=1))

    def filter_chunk(c, carry):
        t_load(c).wait()

        def strip(i, inner):
            rows = pl.ds(pl.multiple_of(i * 16, 16), 16)
            m = mask[rows, :]
            for q in range(2):
                t2[c * 2 + q, k, rows, :] = t2[c * 2 + q, k, rows, :] * m
            return inner

        lax.fori_loop(0, 8, strip, 0)
        t_share(c, True).start()
        return carry

    lax.fori_loop(0, NC, filter_chunk, 0)

    def v2(part, j, d, mine):
        axis = ORDERS[part][1]
        at = p if mine else moved(p, **{axis: -d})
        if part == 0:
            slot = gvb.at[0, lax.rem((y + d if mine else y) + turn(j), 4), :, x, at["y"], :]
        else:
            slot = gvb.at[1, lax.rem(y + FAR_ORDER[j], 4), :, at["x"], y, :]
        return remote(slot, slot, sent.at[V2], v2r.at[part, j], moved(p, **{axis: d}))

    def v2_out(part, j):
        for d in (1, 3, 2):
            v2(part, j, d, True).start()

    def v2_in(part, j):
        arrived(gst.at[pl.ds(0, 3)], v2r.at[part, j])

    own.wait()
    for part in (1, 0):
        arrived(turned.at[0, pl.ds(0, 14)], v1r.at[part])
        for j in range(3):
            v2_out(part, j)

    own_o.wait()
    arrived(gst.at[pl.ds(0, 7)], o1r.at[0])
    got[zl, x, zh, k] = gst[...].reshape(128, 1024).T.reshape(4, 4, 64, 128)

    def o2(d, mine):
        at = p if mine else moved(p, z=-d)
        slot = got.at[lax.rem(at["z"], 2), x, at["z"] // 2, k]
        return remote(slot, slot, sent.at[O2], o2r.at[0], moved(p, z=d))

    for d in (1, 3, 2):
        o2(d, True).start()

    def vy(s, d, mine):
        pair = lax.rem((y + d if mine else y) + turn(s), 4)
        slot = gvb.at[1, pair, :, :, y if mine else moved(p, y=-d)["y"], :]
        return remote(slot, slot, sent.at[VY], vyr.at[s], moved(p, y=d))

    def along_x(ref_of, send, recv, side, n, mine):
        step = 1 - 2 * side
        origin = (x if n < 2 else moved(p, x=-step)["x"]) if mine else moved(p, x=-step if n < 2 else 2)["x"]
        slot = ref_of(side if n == 2 else n, origin)
        return remote(slot, slot, send, recv.at[0 if n == side else 1], moved(p, x=step))

    def vx(s, side, n, mine):
        pair = lax.rem(y + turn(s), 4)
        return along_x(lambda half, at: gvb.at[0, pair, half, at], sent.at[VX], vxr.at[s], side, n, mine)

    def o3(t, side, n, mine):
        return along_x(lambda half, at: got.at[half, at, :, k, :, t], sent.at[O3], o3r.at[t], side, n, mine)

    def own_out(copy, i):
        for n in (0, 1):
            for side in (0, 1):
                copy(i, side, n if side == 0 else 1 - n, True).start()

    def pass_on(copy, i):
        if copy is vx:
            arrived(hs.at[0, 0], vxr.at[i, 0])
        else:
            arrived(hs.at[0, pl.ds(0, 2)], o3r.at[i, 0])
        for side in (0, 1):
            copy(i, side, 2, True).start()

    def rest_in(copy, i):
        if copy is vx:
            arrived(hs.at[0, pl.ds(0, 2)], vxr.at[i, 1])
        else:
            arrived(hs.at[0, pl.ds(0, 4)], o3r.at[i, 1])

    def vy_in(s):
        arrived(hs.at[0, pl.ds(0, 3)], vyr.at[s])

    def o4(t, mine):
        slot = got.at[:, :, :, k if mine else 1 - k, :, t]
        return remote(slot, slot, sent.at[O4], o4r.at[t], moved(p, k=1))

    v2_in(1, 0)
    vy(0, FAR_ORDER[0], True).start()
    v2_in(0, 0)
    own_out(vx, 0)
    for j in (1, 2):
        v2_in(1, j)
        vy(0, FAR_ORDER[j], True).start()
    v2_out(1, 3)
    v2_out(0, 3)
    vy(1, 1, True).start()
    vy(1, 2, True).start()
    v2_in(0, 1)
    pass_on(vx, 0)
    own_out(vx, 1)
    v2_in(0, 2)
    own_out(vx, 2)
    v2_in(1, 3)
    vy(1, 3, True).start()
    for s in (2, 3):
        for d in (1, 3, 2):
            vy(s, d, True).start()

    arrived(t2.at[:, 0], tr.at[0])

    def h_own(c):
        chip = y * 2 + zh
        return pltpu.make_async_copy(hs.at[c, chip], hr.at[c, :, chip], hrr.at[stage(c)])

    def h_side(c, s, mine):
        source = moved(p, y=0 if mine else -s)["y"] * 2 + zh
        return remote(
            hs.at[c, lax.rem(y + s, 4) * 2 + zh], hr.at[c, :, source], sent.at[HD], hrr.at[stage(c)], moved(p, y=s)
        )

    def h_cross(c, s, mine):
        if isinstance(s, int) and s == 0:
            dst, sem = hr.at[c, :, y * 2 + (zh if mine else 1 - zh)], hrr.at[stage(c)]
        else:
            dst, sem = hz.at[c, s - 1], hur.at[c, s]
        return remote(hs.at[c, lax.rem(y + s, 4) * 2 + 1 - zh], dst, sent.at[HC], sem, moved(p, z=2))

    def h_pass(c, s, mine):
        source = moved(p, y=0 if mine else -s)["y"] * 2 + 1 - zh
        return remote(hz.at[c, s - 1], hr.at[c, :, source], sent.at[HP], hrr.at[stage(c)], moved(p, y=s))

    def h_on(c, s):
        h_cross(c, s, False).wait_recv()
        h_pass(c, s, True).start()

    def first(c0, chunks, n):
        pair = lax.rem(y + turn(n), 4)
        rhs = jnp.concatenate([gvb[q, pair].reshape(2048, 128) for q in range(2)], axis=1)
        lhs = t2[pl.ds(c0 * 2, chunks * 2)].reshape(chunks * 512, 2048)
        h = jnp.dot(lhs, rhs, preferred_element_type=F32).astype(BF)
        for m in range(chunks):
            for q in range(2):
                hs[c0 + m, pair * 2 + q] = h[m * 512:(m + 1) * 512, q * 128:(q + 1) * 128].reshape(2, 256, 128)

    def first_own(c, carry):
        first(c, 1, 0)
        h_cross(c, 0, True).start()
        h_own(c).start()
        return carry

    def first_early(n, carry):
        @pl.when(n == 1)
        def _():
            pass_on(vx, 1)
            v2_in(0, 3)
            own_out(vx, 3)
            pass_on(vx, 2)

        @pl.when(n == 2)
        def _():
            pass_on(vx, 3)
            arrived(got.at[0, pl.ds(0, 3), 0, 0], o2r.at[0])
            own_out(o3, 0)
            own_out(o3, 1)

        rest_in(vx, n)
        vy_in(n)
        first(0, 2, n)
        for c in (0, 1):
            h_cross(c, turn(n), True).start()
            h_side(c, turn(n), True).start()
        return carry

    def first_late(n, carry):
        @pl.when(n == 1)
        def _():
            h_on(0, 1)
            h_on(1, 1)
            pass_on(o3, 0)
            own_out(o3, 2)

        @pl.when(n == 3)
        def _():
            h_on(0, 3)
            h_on(1, 3)

        first(2, 2, n)
        h_cross(2, turn(n), True).start()
        return carry

    rest_in(vx, 0)
    vy_in(0)
    lax.fori_loop(0, NC, first_own, 0)
    lax.fori_loop(1, 4, first_early, 0)
    lax.fori_loop(1, 4, first_late, 0)

    for s in (1, 3, 2):
        h_cross(3, s, True).start()
    pass_on(o3, 1)
    own_out(o3, 3)
    h_on(0, 2)
    h_on(1, 2)
    for s in (1, 3, 2):
        h_side(2, s, True).start()
    rest_in(o3, 0)
    o4(0, True).start()
    pass_on(o3, 2)
    h_on(2, 1)
    rest_in(o3, 1)
    o4(1, True).start()
    h_on(2, 3)
    pass_on(o3, 3)

    whole = pl.ds(0, 256)

    def s_slot(c, at, rows):
        return out.at[pl.ds((lax.rem(at["z"], 2) * 4 + at["x"]) * 8 + c * 2, 2), rows]

    def s_out(c, d, rows, part):
        block = ss.at[c, lax.rem(x + d, 4)]

        def stay():
            pltpu.make_async_copy(block.at[0, :, rows], s_slot(c, p, rows), srr.at[0]).start()
            remote(block.at[1, :, rows], s_slot(c, p, rows), sent.at[SC], srr.at[0], flip(p, "z")).start()

        def leave():
            s_cross(c, d, rows, part).start()
            remote(block.at[0, :, rows], s_slot(c, p, rows), sent.at[SD], srr.at[0], moved(p, x=d)).start()

        if isinstance(d, int):
            leave() if d else stay()
        else:
            pl.when(d == 0)(stay)
            pl.when(d > 0)(leave)

    def s_cross(c, d, rows, part):
        return remote(
            ss.at[c, lax.rem(x + d, 4), 1, :, rows], sz.at[c, d - 1, :, rows], sent.at[SC], zr.at[part, c, d], flip(p, "z")
        )

    def s_on(c, d, rows, part):
        s_cross(c, d, rows, part).wait_recv()
        remote(
            sz.at[c, d - 1, :, rows], s_slot(c, flip(p, "z"), rows), sent.at[SP], srr.at[0], moved(p, x=d)
        ).start()

    def s_on_early(part):
        for i in range(3):
            for c in (0, 1):
                s_on(c, far_first(i), pl.ds(part * 128, 128), part)

    def lined_up(c, q):
        rows = []
        for b in range(16):
            for j in range(4):
                n = (b // 2) * 8 + j * 2 + b % 2
                rows.append(hr[c, q, n // 8, (n % 8) * 32:(n % 8) * 32 + 32, :])
        return jnp.concatenate(rows, axis=0)

    def second(chunks, rows_of):
        lhs = jnp.concatenate(
            [
                jnp.concatenate(
                    [
                        rows_of(got.at[b // 8, (b // 2) % 4, b % 2, zl if e == 0 else 1 - zl]).reshape(256, 128)
                        for b in range(16)
                    ],
                    axis=1,
                )
                for e in (0, 1)
            ],
            axis=0,
        )
        rhs = jnp.concatenate([lined_up(c, q) for c in chunks for q in range(2)], axis=1)
        return jnp.dot(lhs, rhs, preferred_element_type=F32).astype(BF)

    arrived(hr.at[pl.ds(0, 2)], hrr.at[0])

    def second_early(t, carry):
        @pl.when(t == 2)
        def _():
            h_on(2, 2)
            for s in (1, 3, 2):
                h_side(3, s, True).start()
            h_on(3, 1)
            rest_in(o3, 2)
            o4(2, True).start()

        @pl.when(t == 3)
        def _():
            rest_in(o3, 3)
            o4(3, True).start()
            h_on(3, 3)

        o4(t, False).wait_recv()
        r = second((0, 1), lambda ref: ref[:, t])
        rows = pl.ds(pl.multiple_of(t * 64, 64), 64)
        for c in (0, 1):
            for owner in range(4):
                for e in (0, 1):
                    at = e * 256 + owner * 64
                    for q in range(2):
                        ss[c, owner, e, q, rows] = r[at:at + 64, (c * 2 + q) * 128:(c * 2 + q + 1) * 128]

        for part in (0, 1):

            @pl.when(t == part * 2 + 1)
            def _():
                for i in range(4):
                    for c in (0, 1):
                        s_out(c, far_first(i), pl.ds(part * 128, 128), part)

        return carry

    lax.fori_loop(0, 4, second_early, 0)
    h_on(3, 2)

    def second_late(c, carry):
        arrived(hr.at[c], hrr.at[c - 1])

        def tile(i, inner):
            d = far_first(i)
            owner = lax.rem(x + d, 4)
            r = second((c,), lambda ref: ref[owner])
            for e in (0, 1):
                for q in range(2):
                    ss[c, owner, e, q] = r[e * 256:(e + 1) * 256, q * 128:(q + 1) * 128]
            s_out(c, d, whole, 0)
            return inner

        lax.fori_loop(0, 4, tile, 0)
        s_on_early(c - 2)
        return carry

    lax.fori_loop(2, 4, second_late, 0)

    def s_on_late(i, carry):
        s_on(2 + i // 3, far_first(lax.rem(i, 3)), whole, 0)
        return carry

    lax.fori_loop(0, 6, s_on_late, 0)

    arrived(out, srr.at[0])
    arrived(t2.at[:, 0], sent.at[TS])
    for kind, ref in (
        (V1, gst.at[pl.ds(0, 7)]), (O1, gst.at[pl.ds(0, 7)]),
        (V2, got.at[0, pl.ds(0, 3), 0, 0]), (O2, got.at[0, pl.ds(0, 3), 0, 0]),
        (VY, got.at[0, pl.ds(0, 3), :, 0]), (VX, got.at[0, pl.ds(0, 3), :, 0]),
        (O3, got.at[0, pl.ds(0, 3)]), (O4, got.at[0]),
        (HC, got.at[0, pl.ds(0, 2)]), (HD, got.at[0, pl.ds(0, 3), :, 0]), (HP, got.at[0, pl.ds(0, 3), :, 0]),
        (SC, got.at[0, pl.ds(0, 2)]), (SD, got.at[0, pl.ds(0, 3), :, 0]), (SP, got.at[0, pl.ds(0, 3), :, 0]),
    ):
        arrived(ref, sent.at[kind])


def restack(source, out, target, out_sem):
    parts = out_sem.shape[0]
    lams = out.shape[0] // parts

    def store(i):
        some = pl.ds(i * lams, lams)
        return pltpu.make_async_copy(target.at[some], out.at[some], out_sem.at[i])

    to = lax.broadcasted_iota(jnp.int32, (256, 256), 0)
    frm = lax.broadcasted_iota(jnp.int32, (256, 256), 1)
    one_hot = ((to // 16 == lax.rem(frm, 16)) & (lax.rem(to, 16) == frm // 16)).astype(BF)

    def part(i, carry):
        for pair in range(lams // 32):
            for group in range(source.shape[0] // 16):
                ps = slice(group * 16, group * 16 + 16)
                at = [pl.ds(pl.multiple_of(i * lams + pair * 32 + h * 16, 16), 16) for h in range(2)]
                rows = jnp.concatenate([source[ps, at[h], :].reshape(256, 128) for h in range(2)], axis=1)
                moved_rows = jnp.dot(one_hot, rows, preferred_element_type=F32).astype(BF)
                for h in range(2):
                    target[at[h], ps, :] = moved_rows[:, h * 128:(h + 1) * 128].reshape(16, 16, 128)
        store(i).start()
        return carry

    lax.fori_loop(0, parts, part, 0)
    for i in range(parts):
        store(i).wait()


def per_device(three_centre, green_virt, green_occ, pattern, block_sizes, atom_order):
    vmem = pl.BlockSpec(memory_space=pltpu.VMEM)
    anywhere = pl.BlockSpec(memory_space=pl.ANY)
    dma = pltpu.SemaphoreType.DMA
    blocks = pl.pallas_call(
        kernel,
        out_shape=pltpu.VMEM((64, 256, 128), BF),
        in_specs=[vmem, vmem, pl.BlockSpec(memory_space=pltpu.SMEM), vmem, vmem, anywhere],
        out_specs=vmem,
        scratch_shapes=[
            pltpu.VMEM((4, 16, 16, 128), F32),
            pltpu.VMEM((2, 2, 4, 16, 128), BF),
            pltpu.VMEM((2, 4, 2, 4, 4, 2, 32, 128), BF),
            pltpu.VMEM((8, 2, 128, 2048), BF),
            pltpu.VMEM((128, 2048), BF),
            pltpu.VMEM((NC, 8, 2, 256, 128), BF),
            pltpu.VMEM((NC, 3, 2, 256, 128), BF),
            pltpu.VMEM((NC, 2, 8, 256, 128), BF),
            pltpu.VMEM((8, 16, 1024), BF),
            pltpu.VMEM((2, 4, 2, 2, 4, 4, 64, 128), BF),
            pltpu.VMEM((NC, 4, 2, 2, 256, 128), BF),
            pltpu.VMEM((NC, 3, 2, 256, 128), BF),
            dma((NC,)), dma((2,)), dma((15,)), dma((1,)), dma((2,)), dma((2, 4)), dma((4,)), dma((4, 2)),
            dma((1,)), dma((1,)), dma((4, 2)), dma((4,)), dma((NC, 4)), dma((3,)), dma((2, NC, 4)), dma((1,)),
        ],
        compiler_params=pltpu.CompilerParams(
            collective_id=0, has_side_effects=True, vmem_limit_bytes=56 * 2**20
        ),
        name="contract",
    )(green_virt, green_occ, atom_order, block_sizes.reshape(1, -1), pattern, three_centre)
    return pl.pallas_call(
        restack,
        out_shape=jax.ShapeDtypeStruct((256, 64, 128), BF),
        in_specs=[vmem],
        out_specs=anywhere,
        scratch_shapes=[pltpu.VMEM((256, 64, 128), BF), dma((2,))],
        compiler_params=pltpu.CompilerParams(vmem_limit_bytes=40 * 2**20),
        name="restack",
    )(blocks)


def solution(mesh):
    in_specs = (P("row", "col", None), P(("row", "col"), None), P(("row", "col"), None), P(), P(), P())
    return jax.shard_map(
        per_device, mesh=mesh, in_specs=in_specs, out_specs=P("row", None, "col"), check_vma=False
    )
```

```python
import jax
import jax.numpy as jnp
from jax import lax
from jax.experimental import pallas as pl
from jax.experimental.pallas import tpu as pltpu
from jax.sharding import PartitionSpec as P

MESH = pl.DeviceIdType.MESH
BF = jnp.bfloat16
F32 = jnp.float32
NC = 4
ORDERS = ("zyx", "zxy")
TS, V1, V2, VY, VX, O1, O2, O3, O4, HC, HD, HP, SC, SD, SP = 0, 1, 2, 3, 3, 1, 2, 3, 0, 4, 5, 5, 4, 5, 5
FAR_ORDER = (1, 3, 2, 0)


def me():
    r = lax.axis_index("row")
    c = lax.axis_index("col")
    return {
        "x": lax.rem(r, 4),
        "y": c // 4,
        "z": lax.rem(c // 2, 2) * 2 + r // 4,
        "k": lax.rem(c, 2),
    }


def turn(i):
    return i + (i // 2) * (5 - 2 * i)


def far_first(i):
    return (2 + 3 * i + (i // 2) * (7 - 2 * i)) % 4 if isinstance(i, int) else lax.rem(2 + 3 * i + (i // 2) * (7 - 2 * i), 4)


def stage(c):
    return c // 2 + c // 3


def device(p):
    return {"row": lax.rem(p["z"], 2) * 4 + p["x"], "col": (p["y"] * 2 + p["z"] // 2) * 2 + p["k"]}


def moved(p, **by):
    q = dict(p)
    for axis, d in by.items():
        q[axis] = lax.rem(p[axis] + d, 2) if axis == "k" else lax.rem(p[axis] + d + 4, 4)
    return q


def flip(p, axis):
    q = dict(p)
    q[axis] = p[axis] + 1 - 2 * lax.rem(p[axis], 2)
    return q


def partners(p):
    found = [moved(p, k=1)]
    for d in (1, 2, 3):
        for e in (0, 1):
            found.append(moved(p, y=d, k=e))
            found.append(moved(p, z=d, k=e))
        found.append(moved(p, x=d))
    return found


def kernel(gv, go, order, sizes, pattern, t_hbm, out,
           turned, gp, gvb, t2, mask, hs, hz, hr, gst, got, ss, sz,
           t_sem, own_sem, sent, tr, v1r, v2r, vyr, vxr, o1r, o2r, o3r, o4r, hur, hrr, zr, srr):
    p = me()
    x, y, z, k = p["x"], p["y"], p["z"], p["k"]
    zl, zh, yl, yh = lax.rem(z, 2), z // 2, lax.rem(y, 2), y // 2
    row, col = lax.axis_index("row"), lax.axis_index("col")

    def remote(src, dst, send, recv, to):
        return pltpu.make_async_remote_copy(
            src_ref=src, dst_ref=dst, send_sem=send, recv_sem=recv, device_id=device(to), device_id_type=MESH
        )

    def arrived(ref, sem):
        pltpu.make_async_copy(ref, ref, sem).wait()

    def t_load(c):
        two = pl.ds(c * 2, 2)
        return pltpu.make_async_copy(t_hbm.at[two], t2.at[two, k], t_sem.at[c])

    barrier = pltpu.get_barrier_semaphore()
    peers = partners(p)
    for q in peers:
        pl.semaphore_signal(barrier, inc=1, device_id=device(q), device_id_type=MESH)

    for c in range(NC):
        t_load(c).start()

    lane_slot = lax.broadcasted_iota(jnp.int32, (16, 128), 1) // 32
    for b in range(16):
        source = gv[:, b * 128:(b + 1) * 128].astype(F32)
        for t in range(4):
            turned[t, b] = pltpu.roll(source, t * 32, 1) if t else source

    def permute(i, carry):
        part = 1 - i // 8
        core, pair = lax.rem(i, 2), lax.rem(i // 2, 4)
        j = pair * 4 + part * 2 + core
        wanted = jnp.zeros((16, 128), jnp.int32)
        for s in range(4):
            wanted = jnp.where(lane_slot == s, order[4 * j + s], wanted)
        block = jnp.zeros((16, 128), F32)
        for t in range(4):
            first_atom = wanted - lax.rem(lane_slot - t + 4, 4)
            for b in range(16):
                block = jnp.where(first_atom == 4 * b, turned[t, b], block)
        gp[core, part, pair] = block.astype(BF)
        return carry

    lax.fori_loop(0, 8, permute, 0)

    def rows16(core):
        return pl.ds(pl.multiple_of(core * 16, 16), 16)

    def own(part):
        return pltpu.make_async_copy(gp.at[k, part], gvb.at[part, :, zl, x, y, zh, rows16(k)], own_sem.at[part])

    own(1).start()
    own_o = pltpu.make_async_copy(
        go.at[:, pl.ds(pl.multiple_of(k * 1024, 1024), 1024)], gst.at[y * 2 + k], own_sem.at[2]
    )
    own_o.start()

    pl.semaphore_wait(barrier, len(peers))

    def v1(part, d, e):
        to = moved(p, z=d, k=e)
        return remote(
            gp.at[to["k"], part], gvb.at[part, :, zl, x, y, zh, rows16(k)], sent.at[V1], v1r.at[part], to
        )

    v1_targets = [(0, 1)] + [(d, e) for d in (1, 3, 2) for e in (0, 1)]
    for d, e in v1_targets:
        v1(1, d, e).start()
    lax.fori_loop(8, 16, permute, 0)
    own(0).start()
    for d, e in v1_targets:
        v1(0, d, e).start()

    def o1(d, e, mine):
        to = moved(p, y=d, k=e)
        frm = p if mine else moved(p, y=-d, k=e)
        half = pl.ds(pl.multiple_of(to["k"] * 1024, 1024), 1024)
        return remote(go.at[:, half], gst.at[frm["y"] * 2 + frm["k"]], sent.at[O1], o1r.at[0], to)

    group = [(d, e) for d in range(4) for e in (0, 1) if d or e]
    for de in group:
        o1(*de, True).start()

    atom_of_row = lax.broadcasted_iota(jnp.int32, (128, 64), 0) // 32 + col * 4
    pick = (lax.broadcasted_iota(jnp.int32, (128, 64), 1) == atom_of_row).astype(F32)
    spread = (
        lax.broadcasted_iota(jnp.int32, (64, 2048), 1) // 32 == lax.broadcasted_iota(jnp.int32, (64, 2048), 0)
    ).astype(BF)
    size_row = sizes[...].astype(F32)
    own_size = jnp.sum(pick * size_row, axis=1, keepdims=True)
    row_ok = lax.rem(lax.broadcasted_iota(jnp.int32, (128, 1), 0), 32).astype(F32) < own_size
    paired = jnp.dot(pick.astype(BF), pattern[...].astype(F32).astype(BF), preferred_element_type=F32)
    paired = jnp.where(row_ok, paired, 0.0)
    paired = jnp.dot(paired.astype(BF), spread, preferred_element_type=F32)
    all_sizes = jnp.dot(jnp.broadcast_to(size_row, (8, 64)).astype(BF), spread, preferred_element_type=F32)[0:1]
    column_ok = lax.rem(lax.broadcasted_iota(jnp.int32, (1, 2048), 1), 32).astype(F32) < all_sizes
    mask[...] = jnp.where(column_ok, paired, 0.0).astype(BF)

    def t_share(c, mine):
        part = t2.at[pl.ds(c * 2, 2), k if mine else 1 - k]
        return remote(part, part, sent.at[TS], tr.at[0], moved(p, k=1))

    def filter_chunk(c, carry):
        t_load(c).wait()

        def strip(i, inner):
            rows = pl.ds(pl.multiple_of(i * 16, 16), 16)
            m = mask[rows, :]
            for q in range(2):
                t2[c * 2 + q, k, rows, :] = t2[c * 2 + q, k, rows, :] * m
            return inner

        lax.fori_loop(0, 8, strip, 0)
        t_share(c, True).start()
        return carry

    lax.fori_loop(0, NC, filter_chunk, 0)

    def v2(part, j, d, mine):
        axis = ORDERS[part][1]
        at = p if mine else moved(p, **{axis: -d})
        if part == 0:
            slot = gvb.at[0, lax.rem((y + d if mine else y) + turn(j), 4), :, x, at["y"], :]
        else:
            slot = gvb.at[1, lax.rem(y + FAR_ORDER[j], 4), :, at["x"], y, :]
        return remote(slot, slot, sent.at[V2], v2r.at[part, j], moved(p, **{axis: d}))

    def v2_out(part, j):
        for d in (1, 3, 2):
            v2(part, j, d, True).start()

    def v2_in(part, j):
        arrived(gst.at[pl.ds(0, 3)], v2r.at[part, j])

    for part in (1, 0):
        own(part).wait()
        arrived(turned.at[0, pl.ds(0, 14)], v1r.at[part])
        for j in range(3):
            v2_out(part, j)

    own_o.wait()
    arrived(gst.at[pl.ds(0, 7)], o1r.at[0])
    got[zl, x, zh, k] = gst[...].reshape(128, 1024).T.reshape(4, 4, 64, 128)

    def o2(d, mine):
        at = p if mine else moved(p, z=-d)
        slot = got.at[lax.rem(at["z"], 2), x, at["z"] // 2, k]
        return remote(slot, slot, sent.at[O2], o2r.at[0], moved(p, z=d))

    for d in (1, 3, 2):
        o2(d, True).start()

    def vy(s, d, mine):
        pair = lax.rem((y + d if mine else y) + turn(s), 4)
        slot = gvb.at[1, pair, :, :, y if mine else moved(p, y=-d)["y"], :]
        return remote(slot, slot, sent.at[VY], vyr.at[s], moved(p, y=d))

    def along_x(ref_of, send, recv, side, n, mine):
        step = 1 - 2 * side
        origin = (x if n < 2 else moved(p, x=-step)["x"]) if mine else moved(p, x=-step if n < 2 else 2)["x"]
        slot = ref_of(side if n == 2 else n, origin)
        return remote(slot, slot, send, recv.at[0 if n == side else 1], moved(p, x=step))

    def vx(s, side, n, mine):
        pair = lax.rem(y + turn(s), 4)
        return along_x(lambda half, at: gvb.at[0, pair, half, at], sent.at[VX], vxr.at[s], side, n, mine)

    def o3(t, side, n, mine):
        return along_x(lambda half, at: got.at[half, at, :, k, :, t], sent.at[O3], o3r.at[t], side, n, mine)

    def own_out(copy, i):
        for n in (0, 1):
            for side in (0, 1):
                copy(i, side, n if side == 0 else 1 - n, True).start()

    def pass_on(copy, i):
        if copy is vx:
            arrived(hs.at[0, 0], vxr.at[i, 0])
        else:
            arrived(hs.at[0, pl.ds(0, 2)], o3r.at[i, 0])
        for side in (0, 1):
            copy(i, side, 2, True).start()
        if copy is o3:
            o4(i, False)

    def rest_in(copy, i):
        if copy is vx:
            arrived(hs.at[0, pl.ds(0, 2)], vxr.at[i, 1])
        else:
            arrived(hs.at[0, pl.ds(0, 4)], o3r.at[i, 1])
            o4(i, True)

    def vy_in(s):
        arrived(hs.at[0, pl.ds(0, 3)], vyr.at[s])

    def o4(t, last):
        before, after = moved(p, x=-1)["x"], moved(p, x=1)["x"]
        every = slice(None)
        first, second = (0, before), (1, after)
        if last:
            first, second = (1, before), (0, after)
        for half, at in (first, second, (every, moved(p, x=2)["x"] if last else x)):
            slot = got.at[half, at, :, k, :, t]
            remote(slot, slot, sent.at[O4], o4r.at[t], moved(p, k=1)).start()

    def o4_in(t):
        arrived(got.at[:, :, :, 0, :, 0], o4r.at[t])

    v2_in(1, 0)
    vy(0, FAR_ORDER[0], True).start()
    v2_in(0, 0)
    own_out(vx, 0)
    for j in (1, 2):
        v2_in(1, j)
        vy(0, FAR_ORDER[j], True).start()
    v2_out(1, 3)
    v2_out(0, 3)
    vy(1, 1, True).start()
    vy(1, 2, True).start()
    v2_in(0, 1)
    pass_on(vx, 0)
    own_out(vx, 1)
    v2_in(0, 2)
    own_out(vx, 2)
    v2_in(1, 3)
    vy(1, 3, True).start()
    for s in (2, 3):
        for d in (1, 3, 2):
            vy(s, d, True).start()

    arrived(t2.at[:, 0], tr.at[0])

    def h_own(c):
        chip = y * 2 + zh
        return pltpu.make_async_copy(hs.at[c, chip], hr.at[c, :, chip], hrr.at[stage(c)])

    def h_side(c, s, mine):
        source = moved(p, y=0 if mine else -s)["y"] * 2 + zh
        return remote(
            hs.at[c, lax.rem(y + s, 4) * 2 + zh], hr.at[c, :, source], sent.at[HD], hrr.at[stage(c)], moved(p, y=s)
        )

    def h_cross(c, s, mine):
        if isinstance(s, int) and s == 0:
            dst, sem = hr.at[c, :, y * 2 + (zh if mine else 1 - zh)], hrr.at[stage(c)]
        else:
            dst, sem = hz.at[c, s - 1], hur.at[stage(c), s]
        return remote(hs.at[c, lax.rem(y + s, 4) * 2 + 1 - zh], dst, sent.at[HC], sem, moved(p, z=2))

    def h_pass(c, s, mine):
        source = moved(p, y=0 if mine else -s)["y"] * 2 + 1 - zh
        return remote(hz.at[c, s - 1], hr.at[c, :, source], sent.at[HP], hrr.at[stage(c)], moved(p, y=s))

    def h_on(chunks, s):
        arrived(hz.at[0, pl.ds(0, len(chunks))], hur.at[stage(chunks[0]), s])
        for c in chunks:
            h_pass(c, s, True).start()

    def first(c0, chunks, n):
        pair = lax.rem(y + turn(n), 4)
        rhs = jnp.concatenate([gvb[q, pair].reshape(2048, 128) for q in range(2)], axis=1)
        lhs = t2[pl.ds(c0 * 2, chunks * 2)].reshape(chunks * 512, 2048)
        h = jnp.dot(lhs, rhs, preferred_element_type=F32).astype(BF)
        for m in range(chunks):
            for q in range(2):
                hs[c0 + m, pair * 2 + q] = h[m * 512:(m + 1) * 512, q * 128:(q + 1) * 128].reshape(2, 256, 128)

    def first_own(c, carry):
        first(c, 1, 0)
        h_cross(c, 0, True).start()
        h_own(c).start()
        return carry

    def first_early(n, carry):
        @pl.when(n == 1)
        def _():
            pass_on(vx, 1)
            v2_in(0, 3)
            own_out(vx, 3)
            pass_on(vx, 2)

        @pl.when(n == 2)
        def _():
            pass_on(vx, 3)
            arrived(got.at[0, pl.ds(0, 3), 0, 0], o2r.at[0])
            own_out(o3, 0)
            own_out(o3, 1)

        rest_in(vx, n)
        vy_in(n)
        first(0, 2, n)
        for c in (0, 1):
            h_cross(c, turn(n), True).start()
            h_side(c, turn(n), True).start()
        return carry

    def first_late(n, carry):
        @pl.when(n == 1)
        def _():
            h_on((0, 1), 1)
            pass_on(o3, 0)
            own_out(o3, 2)

        @pl.when(n == 3)
        def _():
            h_on((0, 1), 3)

        first(2, 2, n)
        h_cross(2, turn(n), True).start()
        return carry

    rest_in(vx, 0)
    vy_in(0)
    lax.fori_loop(0, NC, first_own, 0)
    lax.fori_loop(1, 4, first_early, 0)
    lax.fori_loop(1, 4, first_late, 0)

    for s in (1, 3, 2):
        h_cross(3, s, True).start()
    pass_on(o3, 1)
    own_out(o3, 3)
    h_on((0, 1), 2)
    for s in (1, 3, 2):
        h_side(2, s, True).start()
    rest_in(o3, 0)
    pass_on(o3, 2)
    h_on((2,), 1)
    rest_in(o3, 1)
    h_on((2,), 3)
    pass_on(o3, 3)

    whole = pl.ds(0, 256)

    def s_slot(c, at, rows):
        return out.at[pl.ds((lax.rem(at["z"], 2) * 4 + at["x"]) * 8 + c * 2, 2), rows]

    def s_straight(c, rows):
        return remote(ss.at[c, x, 1, :, rows], s_slot(c, p, rows), sent.at[SC], srr.at[0], flip(p, "z"))

    def s_out(c, d, rows, part):
        block = ss.at[c, lax.rem(x + d, 4)]

        def stay():
            pltpu.make_async_copy(block.at[0, :, rows], s_slot(c, p, rows), srr.at[0]).start()
            if isinstance(d, int):
                s_straight(c, rows).start()

        def leave():
            s_cross(c, d, rows, part).start()
            remote(block.at[0, :, rows], s_slot(c, p, rows), sent.at[SD], srr.at[0], moved(p, x=d)).start()

        if isinstance(d, int):
            leave() if d else stay()
        else:
            pl.when(d == 0)(stay)
            pl.when(d > 0)(leave)

    def s_cross(c, d, rows, part):
        return remote(
            ss.at[c, lax.rem(x + d, 4), 1, :, rows], sz.at[c, d - 1, :, rows], sent.at[SC], zr.at[part, d], flip(p, "z")
        )

    def s_on(chunks, d, rows, part):
        arrived(sz.at[0, 0], zr.at[part, d])
        for c in chunks:
            remote(
                sz.at[c, d - 1, :, rows], s_slot(c, flip(p, "z"), rows), sent.at[SP], srr.at[0], moved(p, x=d)
            ).start()

    def s_on_early(part):
        for i in range(3):
            s_on((0, 1), far_first(i), pl.ds(part * 128, 128), part)

    def lined_up(c, q):
        rows = []
        for b in range(16):
            for j in range(4):
                n = (b // 2) * 8 + j * 2 + b % 2
                rows.append(hr[c, q, n // 8, (n % 8) * 32:(n % 8) * 32 + 32, :])
        return jnp.concatenate(rows, axis=0)

    def second(chunks, rows_of):
        lhs = jnp.concatenate(
            [
                jnp.concatenate(
                    [
                        rows_of(got.at[b // 8, (b // 2) % 4, b % 2, zl if e == 0 else 1 - zl]).reshape(256, 128)
                        for b in range(16)
                    ],
                    axis=1,
                )
                for e in (0, 1)
            ],
            axis=0,
        )
        rhs = jnp.concatenate([lined_up(c, q) for c in chunks for q in range(2)], axis=1)
        return jnp.dot(lhs, rhs, preferred_element_type=F32).astype(BF)

    arrived(hr.at[pl.ds(0, 2)], hrr.at[0])

    def second_early(t, carry):
        @pl.when(t == 2)
        def _():
            h_on((2,), 2)
            for s in (1, 3, 2):
                h_side(3, s, True).start()
            h_on((3,), 1)
            rest_in(o3, 2)

        @pl.when(t == 3)
        def _():
            rest_in(o3, 3)
            h_on((3,), 3)

        o4_in(t)
        r = second((0, 1), lambda ref: ref[:, t])
        rows = pl.ds(pl.multiple_of(t * 64, 64), 64)
        for c in (0, 1):
            for owner in range(4):
                for e in (0, 1):
                    at = e * 256 + owner * 64
                    for q in range(2):
                        ss[c, owner, e, q, rows] = r[at:at + 64, (c * 2 + q) * 128:(c * 2 + q + 1) * 128]

        for part in (0, 1):

            @pl.when(t == part * 2 + 1)
            def _():
                for i in range(4):
                    for c in (0, 1):
                        s_out(c, far_first(i), pl.ds(part * 128, 128), part)

        return carry

    lax.fori_loop(0, 4, second_early, 0)
    h_on((3,), 2)

    def second_late(c, carry):
        arrived(hr.at[c], hrr.at[c - 1])

        def tile(i, inner):
            d = far_first(i)
            owner = lax.rem(x + d, 4)
            r = second((c,), lambda ref: ref[owner])
            for e in (0, 1):
                for q in range(2):
                    ss[c, owner, e, q] = r[e * 256:(e + 1) * 256, q * 128:(q + 1) * 128]
            s_out(c, d, whole, c)
            return inner

        lax.fori_loop(0, 4, tile, 0)

        @pl.when(c == 3)
        def _():
            s_straight(2, whole).start()
            s_straight(3, whole).start()

        s_on_early(c - 2)
        return carry

    lax.fori_loop(2, 4, second_late, 0)

    def s_on_late(i, carry):
        s_on((2 + i // 3,), far_first(lax.rem(i, 3)), whole, 2 + i // 3)
        return carry

    lax.fori_loop(0, 6, s_on_late, 0)

    arrived(out, srr.at[0])
    for sem, ref in (
        (TS, t2), (V1, t2.at[0, 0, pl.ds(0, 112)]), (V2, t2.at[pl.ds(0, 3), 0]),
        (VX, t2.at[pl.ds(0, 6)]), (HC, t2.at[:, 0]), (HD, t2.at[pl.ds(0, 6)]),
    ):
        arrived(ref, sent.at[sem])


def restack(source, out, target, out_sem):
    parts = out_sem.shape[0]
    lams = out.shape[0] // parts

    def store(i):
        some = pl.ds(i * lams, lams)
        return pltpu.make_async_copy(target.at[some], out.at[some], out_sem.at[i])

    to = lax.broadcasted_iota(jnp.int32, (256, 256), 0)
    frm = lax.broadcasted_iota(jnp.int32, (256, 256), 1)
    one_hot = ((to // 16 == lax.rem(frm, 16)) & (lax.rem(to, 16) == frm // 16)).astype(BF)

    def part(i, carry):
        for pair in range(lams // 32):
            for group in range(source.shape[0] // 16):
                ps = slice(group * 16, group * 16 + 16)
                at = [pl.ds(pl.multiple_of(i * lams + pair * 32 + h * 16, 16), 16) for h in range(2)]
                rows = jnp.concatenate([source[ps, at[h], :].reshape(256, 128) for h in range(2)], axis=1)
                moved_rows = jnp.dot(one_hot, rows, preferred_element_type=F32).astype(BF)
                for h in range(2):
                    target[at[h], ps, :] = moved_rows[:, h * 128:(h + 1) * 128].reshape(16, 16, 128)
        store(i).start()
        return carry

    lax.fori_loop(0, parts, part, 0)
    for i in range(parts):
        store(i).wait()


def per_device(three_centre, green_virt, green_occ, pattern, block_sizes, atom_order):
    vmem = pl.BlockSpec(memory_space=pltpu.VMEM)
    anywhere = pl.BlockSpec(memory_space=pl.ANY)
    dma = pltpu.SemaphoreType.DMA
    blocks = pl.pallas_call(
        kernel,
        out_shape=pltpu.VMEM((64, 256, 128), BF),
        in_specs=[vmem, vmem, pl.BlockSpec(memory_space=pltpu.SMEM), vmem, vmem, anywhere],
        out_specs=vmem,
        scratch_shapes=[
            pltpu.VMEM((4, 16, 16, 128), F32),
            pltpu.VMEM((2, 2, 4, 16, 128), BF),
            pltpu.VMEM((2, 4, 2, 4, 4, 2, 32, 128), BF),
            pltpu.VMEM((8, 2, 128, 2048), BF),
            pltpu.VMEM((128, 2048), BF),
            pltpu.VMEM((NC, 8, 2, 256, 128), BF),
            pltpu.VMEM((NC, 3, 2, 256, 128), BF),
            pltpu.VMEM((NC, 2, 8, 256, 128), BF),
            pltpu.VMEM((8, 16, 1024), BF),
            pltpu.VMEM((2, 4, 2, 2, 4, 4, 64, 128), BF),
            pltpu.VMEM((NC, 4, 2, 2, 256, 128), BF),
            pltpu.VMEM((NC, 3, 2, 256, 128), BF),
            dma((NC,)), dma((3,)), dma((6,)), dma((1,)), dma((2,)), dma((2, 4)), dma((4,)), dma((4, 2)),
            dma((1,)), dma((1,)), dma((4, 2)), dma((4,)), dma((3, 4)), dma((3,)), dma((4, 4)), dma((1,)),
        ],
        compiler_params=pltpu.CompilerParams(
            collective_id=0, has_side_effects=True, vmem_limit_bytes=56 * 2**20
        ),
        name="contract",
    )(green_virt, green_occ, atom_order, block_sizes.reshape(1, -1), pattern, three_centre)
    return pl.pallas_call(
        restack,
        out_shape=jax.ShapeDtypeStruct((256, 64, 128), BF),
        in_specs=[vmem],
        out_specs=anywhere,
        scratch_shapes=[pltpu.VMEM((256, 64, 128), BF), dma((2,))],
        compiler_params=pltpu.CompilerParams(vmem_limit_bytes=40 * 2**20),
        name="restack",
    )(blocks)


def solution(mesh):
    in_specs = (P("row", "col", None), P(("row", "col"), None), P(("row", "col"), None), P(), P(), P())
    return jax.shard_map(
        per_device, mesh=mesh, in_specs=in_specs, out_specs=P("row", None, "col"), check_vma=False
    )
```

```python
import jax
import jax.numpy as jnp
from jax import lax
from jax.experimental import pallas as pl
from jax.experimental.pallas import tpu as pltpu
from jax.sharding import PartitionSpec as P

MESH = pl.DeviceIdType.MESH
BF = jnp.bfloat16
F32 = jnp.float32
NC = 4
ORDERS = ("zyx", "zxy")
TS, V1, V2, VY, VX, O1, O2, O3, O4, HC, HD, HP, SC, SD, SP = 0, 1, 2, 3, 3, 1, 2, 3, 0, 4, 5, 5, 4, 5, 5
EARLY_ROWS = ((0, 128), (128, 64), (192, 64))
FAR_ORDER = (None, None, 2, 0)


def me():
    r = lax.axis_index("row")
    c = lax.axis_index("col")
    return {
        "x": lax.rem(r, 4),
        "y": c // 4,
        "z": lax.rem(c // 2, 2) * 2 + r // 4,
        "k": lax.rem(c, 2),
    }


def turn(i):
    return i + (i // 2) * (5 - 2 * i)


def far_first(i):
    return (2 + 3 * i + (i // 2) * (7 - 2 * i)) % 4 if isinstance(i, int) else lax.rem(2 + 3 * i + (i // 2) * (7 - 2 * i), 4)


def stage(c):
    return c // 2 + c // 3


def device(p):
    return {"row": lax.rem(p["z"], 2) * 4 + p["x"], "col": (p["y"] * 2 + p["z"] // 2) * 2 + p["k"]}


def moved(p, **by):
    q = dict(p)
    for axis, d in by.items():
        q[axis] = lax.rem(p[axis] + d, 2) if axis == "k" else lax.rem(p[axis] + d + 4, 4)
    return q


def flip(p, axis):
    q = dict(p)
    q[axis] = p[axis] + 1 - 2 * lax.rem(p[axis], 2)
    return q


def partners(p):
    found = [moved(p, k=1)]
    for d in (1, 2, 3):
        for e in (0, 1):
            found.append(moved(p, y=d, k=e))
            found.append(moved(p, z=d, k=e))
        found.append(moved(p, x=d))
    return found


def kernel(gv, go, order, sizes, pattern, t_hbm, out,
           turned, gp, gvb, t2, mask, hs, hz, hr, gst, got, ss, sz,
           t_sem, own_sem, sent, tr, v1r, v2r, vyr, vxr, o1r, o2r, o3r, o4r, hur, hrr, zr, srr):
    p = me()
    x, y, z, k = p["x"], p["y"], p["z"], p["k"]
    zl, zh, yl, yh = lax.rem(z, 2), z // 2, lax.rem(y, 2), y // 2
    row, col = lax.axis_index("row"), lax.axis_index("col")

    def remote(src, dst, send, recv, to):
        return pltpu.make_async_remote_copy(
            src_ref=src, dst_ref=dst, send_sem=send, recv_sem=recv, device_id=device(to), device_id_type=MESH
        )

    def arrived(ref, sem):
        pltpu.make_async_copy(ref, ref, sem).wait()

    def t_load(c):
        two = pl.ds(c * 2, 2)
        return pltpu.make_async_copy(t_hbm.at[two], t2.at[two, k], t_sem.at[c])

    barrier = pltpu.get_barrier_semaphore()
    peers = partners(p)
    for q in peers:
        pl.semaphore_signal(barrier, inc=1, device_id=device(q), device_id_type=MESH)

    for c in range(NC):
        t_load(c).start()

    lane_slot = lax.broadcasted_iota(jnp.int32, (16, 128), 1) // 32
    for b in range(16):
        source = gv[:, b * 128:(b + 1) * 128].astype(F32)
        for t in range(4):
            turned[t, b] = pltpu.roll(source, t * 32, 1) if t else source

    def permute(i, carry):
        part = 1 - i // 8
        core, pair = lax.rem(i, 2), lax.rem(i // 2, 4)
        j = pair * 4 + part * 2 + core
        wanted = jnp.zeros((16, 128), jnp.int32)
        for s in range(4):
            wanted = jnp.where(lane_slot == s, order[4 * j + s], wanted)
        block = jnp.zeros((16, 128), F32)
        for t in range(4):
            first_atom = wanted - lax.rem(lane_slot - t + 4, 4)
            for b in range(16):
                block = jnp.where(first_atom == 4 * b, turned[t, b], block)
        gp[core, part, pair] = block.astype(BF)
        return carry

    lax.fori_loop(0, 8, permute, 0)

    def rows16(core):
        return pl.ds(pl.multiple_of(core * 16, 16), 16)

    def own(part):
        return pltpu.make_async_copy(gp.at[k, part], gvb.at[part, :, zl, x, y, zh, rows16(k)], own_sem.at[part])

    own(1).start()
    own_o = pltpu.make_async_copy(
        go.at[:, pl.ds(pl.multiple_of(k * 1024, 1024), 1024)], gst.at[y * 2 + k], own_sem.at[2]
    )
    own_o.start()

    pl.semaphore_wait(barrier, len(peers))

    def v1(part, d, e):
        to = moved(p, z=d, k=e)
        return remote(
            gp.at[to["k"], part], gvb.at[part, :, zl, x, y, zh, rows16(k)], sent.at[V1], v1r.at[part], to
        )

    v1_targets = [(0, 1)] + [(d, e) for d in (1, 3, 2) for e in (0, 1)]
    for d, e in v1_targets:
        v1(1, d, e).start()
    lax.fori_loop(8, 16, permute, 0)
    own(0).start()
    for d, e in v1_targets:
        v1(0, d, e).start()

    def o1(d, e, mine):
        to = moved(p, y=d, k=e)
        frm = p if mine else moved(p, y=-d, k=e)
        half = pl.ds(pl.multiple_of(to["k"] * 1024, 1024), 1024)
        return remote(go.at[:, half], gst.at[frm["y"] * 2 + frm["k"]], sent.at[O1], o1r.at[0], to)

    group = [(d, e) for d in range(4) for e in (0, 1) if d or e]
    for de in group:
        o1(*de, True).start()

    atom_of_row = lax.broadcasted_iota(jnp.int32, (128, 64), 0) // 32 + col * 4
    pick = (lax.broadcasted_iota(jnp.int32, (128, 64), 1) == atom_of_row).astype(F32)
    spread = (
        lax.broadcasted_iota(jnp.int32, (64, 2048), 1) // 32 == lax.broadcasted_iota(jnp.int32, (64, 2048), 0)
    ).astype(BF)
    size_row = sizes[...].astype(F32)
    own_size = jnp.sum(pick * size_row, axis=1, keepdims=True)
    row_ok = lax.rem(lax.broadcasted_iota(jnp.int32, (128, 1), 0), 32).astype(F32) < own_size
    paired = jnp.dot(pick.astype(BF), pattern[...].astype(F32).astype(BF), preferred_element_type=F32)
    paired = jnp.where(row_ok, paired, 0.0)
    paired = jnp.dot(paired.astype(BF), spread, preferred_element_type=F32)
    all_sizes = jnp.dot(jnp.broadcast_to(size_row, (8, 64)).astype(BF), spread, preferred_element_type=F32)[0:1]
    column_ok = lax.rem(lax.broadcasted_iota(jnp.int32, (1, 2048), 1), 32).astype(F32) < all_sizes
    mask[...] = jnp.where(column_ok, paired, 0.0).astype(BF)

    def t_share(c, mine):
        part = t2.at[pl.ds(c * 2, 2), k if mine else 1 - k]
        return remote(part, part, sent.at[TS], tr.at[0], moved(p, k=1))

    def filter_chunk(c, carry):
        t_load(c).wait()

        def strip(i, inner):
            rows = pl.ds(pl.multiple_of(i * 16, 16), 16)
            m = mask[rows, :]
            for q in range(2):
                t2[c * 2 + q, k, rows, :] = t2[c * 2 + q, k, rows, :] * m
            return inner

        lax.fori_loop(0, 8, strip, 0)
        t_share(c, True).start()
        return carry

    lax.fori_loop(0, NC, filter_chunk, 0)

    def v2(part, j, d):
        axis = ORDERS[part][1]
        if part == 0:
            slots = [gvb.at[0, lax.rem(y + d + turn(j), 4), :, x, y, :]]
        elif j < 2:
            slots = [gvb.at[1, lax.rem(y + near, 4), j, x, y, :] for near in (1, 3)]
        else:
            slots = [gvb.at[1, lax.rem(y + FAR_ORDER[j], 4), :, x, y, :]]
        to = moved(p, **{axis: d})
        return [remote(slot, slot, sent.at[V2], v2r.at[part, j], to) for slot in slots]

    def v2_out(part, j):
        for d in (1, 3, 2):
            for copy in v2(part, j, d):
                copy.start()

    def v2_in(part, j):
        arrived(gst.at[pl.ds(0, 3)], v2r.at[part, j])

    for part in (1, 0):
        own(part).wait()
        arrived(turned.at[0, pl.ds(0, 14)], v1r.at[part])
        for j in range(3):
            v2_out(part, j)

    own_o.wait()
    arrived(gst.at[pl.ds(0, 7)], o1r.at[0])
    got[zl, x, zh, k] = gst[...].reshape(128, 1024).T.reshape(4, 4, 64, 128)

    def o2(d, mine):
        at = p if mine else moved(p, z=-d)
        slot = got.at[lax.rem(at["z"], 2), x, at["z"] // 2, k]
        return remote(slot, slot, sent.at[O2], o2r.at[0], moved(p, z=d))

    for d in (1, 3, 2):
        o2(d, True).start()

    def vy(s, d, half=slice(None)):
        slot = gvb.at[1, lax.rem(y + d + turn(s), 4), half, :, y, :]
        return remote(slot, slot, sent.at[VY], vyr.at[s], moved(p, y=d))

    def along_x(ref_of, send, recv, side, n, mine):
        step = 1 - 2 * side
        origin = (x if n < 2 else moved(p, x=-step)["x"]) if mine else moved(p, x=-step if n < 2 else 2)["x"]
        slot = ref_of(side if n == 2 else n, origin)
        return remote(slot, slot, send, recv[0 if n == side else 1], moved(p, x=step))

    def vx(s, side, n, mine):
        pair = lax.rem(y + turn(s), 4)
        return along_x(
            lambda half, at: gvb.at[0, pair, half, at], sent.at[VX], (vxr.at[s, 0], vxr.at[s, 1]), side, n, mine
        )

    def vx_first(q, side, n):
        return along_x(
            lambda half, at: gvb.at[0, y, half, at, pl.ds(q * 2, 2)],
            sent.at[VX], (vxr.at[4, q], vxr.at[0, 1]), side, n, True,
        )

    def o3(t, side, n, mine):
        return along_x(lambda half, at: got.at[half, at, :, k, :, t], sent.at[O3], (o3r.at[t, 0], o3r.at[t, 1]), side, n, mine)

    def own_out(copy, i):
        for n in (0, 1):
            for side in (0, 1):
                copy(i, side, n if side == 0 else 1 - n, True).start()

    def pass_on(copy, i):
        if copy is vx:
            arrived(hs.at[0, 0], vxr.at[i, 0])
        else:
            arrived(hs.at[0, pl.ds(0, 2)], o3r.at[i, 0])
        for side in (0, 1):
            copy(i, side, 2, True).start()
        if copy is o3:
            o4(i, False)

    def rest_in(copy, i):
        if copy is vx:
            arrived(hs.at[0, pl.ds(0, 2)], vxr.at[i, 1])
        else:
            arrived(hs.at[0, pl.ds(0, 4)], o3r.at[i, 1])
            o4(i, True)

    def vy_in(s):
        arrived(hs.at[0, pl.ds(0, 3)], vyr.at[s])

    def o4(t, last):
        before, after = moved(p, x=-1)["x"], moved(p, x=1)["x"]
        every = slice(None)
        first, second = (0, before), (1, after)
        if last:
            first, second = (1, before), (0, after)
        for half, at in (first, second, (every, moved(p, x=2)["x"] if last else x)):
            slot = got.at[half, at, :, k, :, t]
            remote(slot, slot, sent.at[O4], o4r.at[t], moved(p, k=1)).start()

    def o4_in(t):
        arrived(got.at[:, :, :, 0, :, 0], o4r.at[t])

    v2_in(1, 0)
    for d in (1, 3):
        vy(0, d, 0).start()
    v2_in(0, 0)
    for other in (0, 1):
        for q in (0, 1):
            for side in (0, 1):
                vx_first(q, side, 1 - side if other else side).start()
    v2_in(1, 1)
    for d in (1, 3):
        vy(0, d, 1).start()
    v2_in(1, 2)
    vy(0, 2).start()
    v2_out(1, 3)
    v2_out(0, 3)
    vy(1, 1).start()
    vy(1, 2).start()
    v2_in(0, 1)
    for q in (0, 1):
        arrived(hs.at[0, 0, 0], vxr.at[4, q])
        for side in (0, 1):
            vx_first(q, side, 2).start()
    own_out(vx, 1)
    v2_in(0, 2)
    own_out(vx, 2)
    v2_in(1, 3)
    vy(1, 3).start()
    for s in (2, 3):
        for d in (1, 3, 2):
            vy(s, d).start()

    arrived(t2.at[:, 0], tr.at[0])

    def h_own(c):
        chip = y * 2 + zh
        return pltpu.make_async_copy(hs.at[c, chip], hr.at[c, :, chip], hrr.at[stage(c)])

    def h_side(c, s, mine):
        source = moved(p, y=0 if mine else -s)["y"] * 2 + zh
        return remote(
            hs.at[c, lax.rem(y + s, 4) * 2 + zh], hr.at[c, :, source], sent.at[HD], hrr.at[stage(c)], moved(p, y=s)
        )

    def h_cross(c, s, mine):
        if isinstance(s, int) and s == 0:
            dst, sem = hr.at[c, :, y * 2 + (zh if mine else 1 - zh)], hrr.at[stage(c)]
        else:
            dst, sem = hz.at[c, s - 1], hur.at[stage(c), s]
        return remote(hs.at[c, lax.rem(y + s, 4) * 2 + 1 - zh], dst, sent.at[HC], sem, moved(p, z=2))

    def h_pass(c, s, mine):
        source = moved(p, y=0 if mine else -s)["y"] * 2 + 1 - zh
        return remote(hz.at[c, s - 1], hr.at[c, :, source], sent.at[HP], hrr.at[stage(c)], moved(p, y=s))

    def h_on(chunks, s):
        arrived(hz.at[0, pl.ds(0, len(chunks))], hur.at[stage(chunks[0]), s])
        for c in chunks:
            h_pass(c, s, True).start()

    def first(c0, chunks, n):
        pair = lax.rem(y + turn(n), 4)
        rhs = jnp.concatenate([gvb[q, pair].reshape(2048, 128) for q in range(2)], axis=1)
        lhs = t2[pl.ds(c0 * 2, chunks * 2)].reshape(chunks * 512, 2048)
        h = jnp.dot(lhs, rhs, preferred_element_type=F32).astype(BF)
        for m in range(chunks):
            for q in range(2):
                hs[c0 + m, pair * 2 + q] = h[m * 512:(m + 1) * 512, q * 128:(q + 1) * 128].reshape(2, 256, 128)

    def first_own(c, carry):
        @pl.when(c == 2)
        def _():
            pass_on(vx, 1)
            v2_in(0, 3)
            own_out(vx, 3)

        first(c, 1, 0)
        h_cross(c, 0, True).start()
        h_own(c).start()
        return carry

    def first_early(n, carry):
        @pl.when(n == 1)
        def _():
            pass_on(vx, 2)

        @pl.when(n == 2)
        def _():
            pass_on(vx, 3)
            arrived(got.at[0, pl.ds(0, 3), 0, 0], o2r.at[0])
            own_out(o3, 0)
            own_out(o3, 1)

        rest_in(vx, n)
        vy_in(n)
        first(0, 2, n)
        for c in (0, 1):
            h_cross(c, turn(n), True).start()
            h_side(c, turn(n), True).start()
        return carry

    def first_late(n, carry):
        @pl.when(n == 1)
        def _():
            h_on((0, 1), 1)
            pass_on(o3, 0)
            own_out(o3, 2)

        @pl.when(n == 3)
        def _():
            h_on((0, 1), 3)

        first(2, 2, n)
        h_cross(2, turn(n), True).start()
        return carry

    rest_in(vx, 0)
    vy_in(0)
    lax.fori_loop(0, NC, first_own, 0)
    lax.fori_loop(1, 4, first_early, 0)
    lax.fori_loop(1, 4, first_late, 0)

    for s in (1, 3, 2):
        h_cross(3, s, True).start()
    pass_on(o3, 1)
    own_out(o3, 3)
    h_on((0, 1), 2)
    for s in (1, 3, 2):
        h_side(2, s, True).start()
    rest_in(o3, 0)
    pass_on(o3, 2)
    h_on((2,), 1)
    rest_in(o3, 1)
    h_on((2,), 3)
    pass_on(o3, 3)

    whole = pl.ds(0, 256)

    def s_slot(c, at, rows):
        return out.at[pl.ds((lax.rem(at["z"], 2) * 4 + at["x"]) * 8 + c * 2, 2), rows]

    def s_straight(c, rows):
        return remote(ss.at[c, x, 1, :, rows], s_slot(c, p, rows), sent.at[SC], srr.at[0], flip(p, "z"))

    def s_out(c, d, rows, part):
        block = ss.at[c, lax.rem(x + d, 4)]

        def stay():
            pltpu.make_async_copy(block.at[0, :, rows], s_slot(c, p, rows), srr.at[0]).start()
            if isinstance(d, int):
                s_straight(c, rows).start()

        def leave():
            s_cross(c, d, rows, part).start()
            remote(block.at[0, :, rows], s_slot(c, p, rows), sent.at[SD], srr.at[0], moved(p, x=d)).start()

        if isinstance(d, int):
            leave() if d else stay()
        else:
            pl.when(d == 0)(stay)
            pl.when(d > 0)(leave)

    def s_cross(c, d, rows, part):
        return remote(
            ss.at[c, lax.rem(x + d, 4), 1, :, rows], sz.at[c, d - 1, :, rows], sent.at[SC], zr.at[part, d], flip(p, "z")
        )

    def s_on(chunks, d, rows, part):
        arrived(sz.at[pl.ds(0, len(chunks)), 0, :, rows], zr.at[part, d])
        for c in chunks:
            remote(
                sz.at[c, d - 1, :, rows], s_slot(c, flip(p, "z"), rows), sent.at[SP], srr.at[0], moved(p, x=d)
            ).start()

    def s_on_early(part):
        for i in range(3):
            s_on((0, 1), far_first(i), pl.ds(*EARLY_ROWS[part]), part)

    def lined_up(c, q):
        rows = []
        for b in range(16):
            for j in range(4):
                n = (b // 2) * 8 + j * 2 + b % 2
                rows.append(hr[c, q, n // 8, (n % 8) * 32:(n % 8) * 32 + 32, :])
        return jnp.concatenate(rows, axis=0)

    def second(chunks, rows_of):
        lhs = jnp.concatenate(
            [
                jnp.concatenate(
                    [
                        rows_of(got.at[b // 8, (b // 2) % 4, b % 2, zl if e == 0 else 1 - zl]).reshape(256, 128)
                        for b in range(16)
                    ],
                    axis=1,
                )
                for e in (0, 1)
            ],
            axis=0,
        )
        rhs = jnp.concatenate([lined_up(c, q) for c in chunks for q in range(2)], axis=1)
        return jnp.dot(lhs, rhs, preferred_element_type=F32).astype(BF)

    arrived(hr.at[pl.ds(0, 2)], hrr.at[0])

    def second_early(t, carry):
        @pl.when(t == 2)
        def _():
            h_on((2,), 2)
            for s in (1, 3, 2):
                h_side(3, s, True).start()
            h_on((3,), 1)
            rest_in(o3, 2)

        @pl.when(t == 3)
        def _():
            rest_in(o3, 3)
            h_on((3,), 3)

        o4_in(t)
        r = second((0, 1), lambda ref: ref[:, t])
        rows = pl.ds(pl.multiple_of(t * 64, 64), 64)
        for c in (0, 1):
            for owner in range(4):
                for e in (0, 1):
                    at = e * 256 + owner * 64
                    for q in range(2):
                        ss[c, owner, e, q, rows] = r[at:at + 64, (c * 2 + q) * 128:(c * 2 + q + 1) * 128]

        for part, (start, size) in enumerate(EARLY_ROWS):

            @pl.when(t == part + 1)
            def _():
                for i in range(4):
                    for c in (0, 1):
                        s_out(c, far_first(i), pl.ds(start, size), part)

        return carry

    lax.fori_loop(0, 4, second_early, 0)
    h_on((3,), 2)

    def second_late(c, carry):
        arrived(hr.at[c], hrr.at[c - 1])

        def tile(i, inner):
            d = far_first(i)
            owner = lax.rem(x + d, 4)
            r = second((c,), lambda ref: ref[owner])
            for e in (0, 1):
                for q in range(2):
                    ss[c, owner, e, q] = r[e * 256:(e + 1) * 256, q * 128:(q + 1) * 128]
            s_out(c, d, whole, c + 1)
            return inner

        lax.fori_loop(0, 4, tile, 0)

        @pl.when(c == 3)
        def _():
            s_straight(2, whole).start()
            s_straight(3, whole).start()

        @pl.when(c == 2)
        def _():
            s_on_early(0)

        @pl.when(c == 3)
        def _():
            s_on_early(1)
            s_on_early(2)

        return carry

    lax.fori_loop(2, 4, second_late, 0)

    def s_on_late(i, carry):
        s_on((2 + i // 3,), far_first(lax.rem(i, 3)), whole, 3 + i // 3)
        return carry

    lax.fori_loop(0, 6, s_on_late, 0)

    arrived(out, srr.at[0])
    for sem, ref in (
        (TS, t2), (V1, t2.at[0, 0, pl.ds(0, 112)]), (V2, t2.at[pl.ds(0, 3), 0]),
        (VX, t2.at[pl.ds(0, 6)]), (HC, t2.at[:, 0]), (HD, t2.at[pl.ds(0, 6)]),
    ):
        arrived(ref, sent.at[sem])


def restack(source, out, target, out_sem):
    parts = out_sem.shape[0]
    lams = out.shape[0] // parts
    to = lax.broadcasted_iota(jnp.int32, (256, 256), 0)
    frm = lax.broadcasted_iota(jnp.int32, (256, 256), 1)
    one_hot = ((to // 16 == lax.rem(frm, 16)) & (lax.rem(to, 16) == frm // 16)).astype(BF)
    stores = []
    for i in range(parts):
        for base in range(i * lams, (i + 1) * lams, 32):
            at = [slice(base + h * 16, base + h * 16 + 16) for h in range(2)]
            for group in range(source.shape[0] // 16):
                ps = slice(group * 16, group * 16 + 16)
                rows = jnp.concatenate([source[ps, at[h], :].reshape(256, 128) for h in range(2)], axis=1)
                moved_rows = jnp.dot(one_hot, rows, preferred_element_type=F32).astype(BF)
                for h in range(2):
                    target[at[h], ps, :] = moved_rows[:, h * 128:(h + 1) * 128].reshape(16, 16, 128)
        some = pl.ds(i * lams, lams)
        stores.append(pltpu.make_async_copy(target.at[some], out.at[some], out_sem.at[i]))
        stores[-1].start()
    for store in stores:
        store.wait()


def per_device(three_centre, green_virt, green_occ, pattern, block_sizes, atom_order):
    vmem = pl.BlockSpec(memory_space=pltpu.VMEM)
    anywhere = pl.BlockSpec(memory_space=pl.ANY)
    dma = pltpu.SemaphoreType.DMA
    blocks = pl.pallas_call(
        kernel,
        out_shape=pltpu.VMEM((64, 256, 128), BF),
        in_specs=[vmem, vmem, pl.BlockSpec(memory_space=pltpu.SMEM), vmem, vmem, anywhere],
        out_specs=vmem,
        scratch_shapes=[
            pltpu.VMEM((4, 16, 16, 128), F32),
            pltpu.VMEM((2, 2, 4, 16, 128), BF),
            pltpu.VMEM((2, 4, 2, 4, 4, 2, 32, 128), BF),
            pltpu.VMEM((8, 2, 128, 2048), BF),
            pltpu.VMEM((128, 2048), BF),
            pltpu.VMEM((NC, 8, 2, 256, 128), BF),
            pltpu.VMEM((NC, 3, 2, 256, 128), BF),
            pltpu.VMEM((NC, 2, 8, 256, 128), BF),
            pltpu.VMEM((8, 16, 1024), BF),
            pltpu.VMEM((2, 4, 2, 2, 4, 4, 64, 128), BF),
            pltpu.VMEM((NC, 4, 2, 2, 256, 128), BF),
            pltpu.VMEM((NC, 3, 2, 256, 128), BF),
            dma((NC,)), dma((3,)), dma((6,)), dma((1,)), dma((2,)), dma((2, 4)), dma((4,)), dma((5, 2)),
            dma((1,)), dma((1,)), dma((4, 2)), dma((4,)), dma((3, 4)), dma((3,)), dma((5, 4)), dma((1,)),
        ],
        compiler_params=pltpu.CompilerParams(
            collective_id=0, has_side_effects=True, vmem_limit_bytes=56 * 2**20
        ),
        name="contract",
    )(green_virt, green_occ, atom_order, block_sizes.reshape(1, -1), pattern, three_centre)
    return pl.pallas_call(
        restack,
        out_shape=jax.ShapeDtypeStruct((256, 64, 128), BF),
        in_specs=[vmem],
        out_specs=anywhere,
        scratch_shapes=[pltpu.VMEM((256, 64, 128), BF), dma((4,))],
        compiler_params=pltpu.CompilerParams(vmem_limit_bytes=40 * 2**20),
        name="restack",
    )(blocks)


def solution(mesh):
    in_specs = (P("row", "col", None), P(("row", "col"), None), P(("row", "col"), None), P(), P(), P())
    return jax.shard_map(
        per_device, mesh=mesh, in_specs=in_specs, out_specs=P("row", None, "col"), check_vma=False
    )
```

```python
import jax
import jax.numpy as jnp
from jax import lax
from jax.experimental import pallas as pl
from jax.experimental.pallas import tpu as pltpu
from jax.sharding import PartitionSpec as P

MESH = pl.DeviceIdType.MESH
BF = jnp.bfloat16
F32 = jnp.float32
NC = 4
ORDERS = ("zyx", "zxy")
TS, V1, V2, VY, VX, O1, O2, O3, O4, HC, HD, HP, SC, SD, SP = 0, 1, 2, 3, 3, 1, 2, 3, 0, 4, 5, 5, 4, 5, 5
EARLY_ROWS = ((0, 128), (128, 64), (192, 64))
FAR_ORDER = (None, None, 2, 0)


def me():
    r = lax.axis_index("row")
    c = lax.axis_index("col")
    return {
        "x": lax.rem(r, 4),
        "y": c // 4,
        "z": lax.rem(c // 2, 2) * 2 + r // 4,
        "k": lax.rem(c, 2),
    }


def turn(i):
    return i + (i // 2) * (5 - 2 * i)


def far_first(i):
    return (2 + 3 * i + (i // 2) * (7 - 2 * i)) % 4 if isinstance(i, int) else lax.rem(2 + 3 * i + (i // 2) * (7 - 2 * i), 4)


def stage(c):
    return c // 2 + c // 3


def device(p):
    return {"row": lax.rem(p["z"], 2) * 4 + p["x"], "col": (p["y"] * 2 + p["z"] // 2) * 2 + p["k"]}


def moved(p, **by):
    q = dict(p)
    for axis, d in by.items():
        q[axis] = lax.rem(p[axis] + d, 2) if axis == "k" else lax.rem(p[axis] + d + 4, 4)
    return q


def flip(p, axis):
    q = dict(p)
    q[axis] = p[axis] + 1 - 2 * lax.rem(p[axis], 2)
    return q


def partners(p):
    found = [moved(p, k=1)]
    for d in (1, 2, 3):
        for e in (0, 1):
            found.append(moved(p, y=d, k=e))
            found.append(moved(p, z=d, k=e))
        found.append(moved(p, x=d))
    return found


def kernel(gv, go, order, sizes, pattern, t_hbm, out,
           turned, gp, gvb, t2, mask, hs, hz, hr, gst, got, ss, sz,
           t_sem, own_sem, sent, tr, v1r, v2r, vyr, vxr, o1r, o2r, o3r, o4r, hur, hrr, zr, srr):
    p = me()
    x, y, z, k = p["x"], p["y"], p["z"], p["k"]
    zl, zh, yl, yh = lax.rem(z, 2), z // 2, lax.rem(y, 2), y // 2
    row, col = lax.axis_index("row"), lax.axis_index("col")

    def remote(src, dst, send, recv, to):
        return pltpu.make_async_remote_copy(
            src_ref=src, dst_ref=dst, send_sem=send, recv_sem=recv, device_id=device(to), device_id_type=MESH
        )

    def arrived(ref, sem):
        pltpu.make_async_copy(ref, ref, sem).wait()

    def t_load(c):
        two = pl.ds(c * 2, 2)
        return pltpu.make_async_copy(t_hbm.at[two], t2.at[two, k], t_sem.at[c])

    barrier = pltpu.get_barrier_semaphore()
    peers = partners(p)
    for q in peers:
        pl.semaphore_signal(barrier, inc=1, device_id=device(q), device_id_type=MESH)

    for c in range(NC):
        t_load(c).start()

    lane_slot = lax.broadcasted_iota(jnp.int32, (16, 128), 1) // 32
    for b in range(16):
        source = gv[:, b * 128:(b + 1) * 128].astype(F32)
        for t in range(4):
            turned[t, b] = pltpu.roll(source, t * 32, 1) if t else source

    def permute(i, carry):
        part = 1 - i // 8
        core, pair = lax.rem(i, 2), lax.rem(i // 2, 4)
        j = pair * 4 + part * 2 + core
        wanted = jnp.zeros((16, 128), jnp.int32)
        for s in range(4):
            wanted = jnp.where(lane_slot == s, order[4 * j + s], wanted)
        block = jnp.zeros((16, 128), F32)
        for t in range(4):
            first_atom = wanted - lax.rem(lane_slot - t + 4, 4)
            for b in range(16):
                block = jnp.where(first_atom == 4 * b, turned[t, b], block)
        gp[core, part, pair] = block.astype(BF)
        return carry

    lax.fori_loop(0, 8, permute, 0)

    def rows16(core):
        return pl.ds(pl.multiple_of(core * 16, 16), 16)

    def own(part):
        return pltpu.make_async_copy(gp.at[k, part], gvb.at[part, :, zl, x, y, zh, rows16(k)], own_sem.at[part])

    own(1).start()
    own_o = pltpu.make_async_copy(
        go.at[:, pl.ds(pl.multiple_of(k * 1024, 1024), 1024)], gst.at[y * 2 + k], own_sem.at[2]
    )
    own_o.start()

    pl.semaphore_wait(barrier, len(peers))

    def v1(part, d, e):
        to = moved(p, z=d, k=e)
        return remote(
            gp.at[to["k"], part], gvb.at[part, :, zl, x, y, zh, rows16(k)], sent.at[V1], v1r.at[part], to
        )

    v1_targets = [(0, 1)] + [(d, e) for d in (1, 3, 2) for e in (0, 1)]
    for d, e in v1_targets:
        v1(1, d, e).start()
    lax.fori_loop(8, 16, permute, 0)
    own(0).start()
    for d, e in v1_targets:
        v1(0, d, e).start()

    def o1(d, e, mine):
        to = moved(p, y=d, k=e)
        frm = p if mine else moved(p, y=-d, k=e)
        half = pl.ds(pl.multiple_of(to["k"] * 1024, 1024), 1024)
        return remote(go.at[:, half], gst.at[frm["y"] * 2 + frm["k"]], sent.at[O1], o1r.at[0], to)

    group = [(d, e) for d in range(4) for e in (0, 1) if d or e]
    for de in group:
        o1(*de, True).start()

    atom_of_row = lax.broadcasted_iota(jnp.int32, (128, 64), 0) // 32 + col * 4
    pick = (lax.broadcasted_iota(jnp.int32, (128, 64), 1) == atom_of_row).astype(F32)
    spread = (
        lax.broadcasted_iota(jnp.int32, (64, 2048), 1) // 32 == lax.broadcasted_iota(jnp.int32, (64, 2048), 0)
    ).astype(BF)
    size_row = sizes[...].astype(F32)
    own_size = jnp.sum(pick * size_row, axis=1, keepdims=True)
    row_ok = lax.rem(lax.broadcasted_iota(jnp.int32, (128, 1), 0), 32).astype(F32) < own_size
    paired = jnp.dot(pick.astype(BF), pattern[...].astype(F32).astype(BF), preferred_element_type=F32)
    paired = jnp.where(row_ok, paired, 0.0)
    paired = jnp.dot(paired.astype(BF), spread, preferred_element_type=F32)
    all_sizes = jnp.dot(jnp.broadcast_to(size_row, (8, 64)).astype(BF), spread, preferred_element_type=F32)[0:1]
    column_ok = lax.rem(lax.broadcasted_iota(jnp.int32, (1, 2048), 1), 32).astype(F32) < all_sizes
    mask[...] = jnp.where(column_ok, paired, 0.0).astype(BF)

    def t_share(c, mine):
        part = t2.at[pl.ds(c * 2, 2), k if mine else 1 - k]
        return remote(part, part, sent.at[TS], tr.at[0], moved(p, k=1))

    def filter_chunk(c, carry):
        t_load(c).wait()

        def strip(i, inner):
            rows = pl.ds(pl.multiple_of(i * 16, 16), 16)
            m = mask[rows, :]
            for q in range(2):
                t2[c * 2 + q, k, rows, :] = t2[c * 2 + q, k, rows, :] * m
            return inner

        lax.fori_loop(0, 8, strip, 0)
        t_share(c, True).start()
        return carry

    lax.fori_loop(0, NC, filter_chunk, 0)

    def v2(part, j, d):
        axis = ORDERS[part][1]
        if part == 0:
            slots = [gvb.at[0, lax.rem(y + d + turn(j), 4), :, x, y, :]]
        elif j < 2:
            slots = [gvb.at[1, lax.rem(y + near, 4), j, x, y, :] for near in (1, 3)]
        else:
            slots = [gvb.at[1, lax.rem(y + FAR_ORDER[j], 4), :, x, y, :]]
        to = moved(p, **{axis: d})
        return [remote(slot, slot, sent.at[V2], v2r.at[part, j], to) for slot in slots]

    def v2_out(part, j):
        for d in (1, 3, 2):
            for copy in v2(part, j, d):
                copy.start()

    def v2_in(part, j):
        arrived(gst.at[pl.ds(0, 3)], v2r.at[part, j])

    for part in (1, 0):
        own(part).wait()
        arrived(turned.at[0, pl.ds(0, 14)], v1r.at[part])
        for j in range(3):
            v2_out(part, j)

    own_o.wait()
    arrived(gst.at[pl.ds(0, 7)], o1r.at[0])
    got[zl, x, zh, k] = gst[...].reshape(128, 1024).T.reshape(4, 4, 64, 128)

    def o2(d, mine):
        at = p if mine else moved(p, z=-d)
        slot = got.at[lax.rem(at["z"], 2), x, at["z"] // 2, k]
        return remote(slot, slot, sent.at[O2], o2r.at[0], moved(p, z=d))

    for d in (2, 1, 3):
        o2(d, True).start()

    def vy(s, d, half=slice(None)):
        slot = gvb.at[1, lax.rem(y + d + turn(s), 4), half, :, y, :]
        return remote(slot, slot, sent.at[VY], vyr.at[s], moved(p, y=d))

    def along_x(ref_of, send, recv, side, n, mine):
        step = 1 - 2 * side
        origin = (x if n < 2 else moved(p, x=-step)["x"]) if mine else moved(p, x=-step if n < 2 else 2)["x"]
        slot = ref_of(side if n == 2 else n, origin)
        return remote(slot, slot, send, recv[0 if n == side else 1], moved(p, x=step))

    def vx(s, side, n, mine):
        pair = lax.rem(y + turn(s), 4)
        return along_x(
            lambda half, at: gvb.at[0, pair, half, at], sent.at[VX], (vxr.at[s, 0], vxr.at[s, 1]), side, n, mine
        )

    def vx_first(q, side, n):
        return along_x(
            lambda half, at: gvb.at[0, y, half, at, pl.ds(q * 2, 2)],
            sent.at[VX], (vxr.at[4, q], vxr.at[0, 1]), side, n, True,
        )

    def o3(t, side, n, mine):
        return along_x(lambda half, at: got.at[half, at, :, k, :, t], sent.at[O3], (o3r.at[t, 0], o3r.at[t, 1]), side, n, mine)

    def own_out(copy, i):
        for n in (0, 1):
            for side in (0, 1):
                copy(i, side, n if side == 0 else 1 - n, True).start()

    def pass_on(copy, i):
        if copy is vx:
            arrived(hs.at[0, 0], vxr.at[i, 0])
        else:
            arrived(hs.at[0, pl.ds(0, 2)], o3r.at[i, 0])
        for side in (0, 1):
            copy(i, side, 2, True).start()
        if copy is o3:
            o4(i, False)

    def rest_in(copy, i):
        if copy is vx:
            arrived(hs.at[0, pl.ds(0, 2)], vxr.at[i, 1])
        else:
            arrived(hs.at[0, pl.ds(0, 4)], o3r.at[i, 1])
            o4(i, True)

    def vy_in(s):
        arrived(hs.at[0, pl.ds(0, 3)], vyr.at[s])

    def o4(t, last):
        before, after = moved(p, x=-1)["x"], moved(p, x=1)["x"]
        every = slice(None)
        first, second = (0, before), (1, after)
        if last:
            first, second = (1, before), (0, after)
        for half, at in (first, second, (every, moved(p, x=2)["x"] if last else x)):
            slot = got.at[half, at, :, k, :, t]
            remote(slot, slot, sent.at[O4], o4r.at[t], moved(p, k=1)).start()

    def o4_in(t):
        arrived(got.at[:, :, :, 0, :, 0], o4r.at[t])

    v2_in(1, 0)
    for d in (1, 3):
        vy(0, d, 0).start()
    v2_in(0, 0)
    for other in (0, 1):
        for q in (0, 1):
            for side in (0, 1):
                vx_first(q, side, 1 - side if other else side).start()
    v2_in(1, 1)
    for d in (1, 3):
        vy(0, d, 1).start()
    v2_in(1, 2)
    vy(0, 2).start()
    v2_out(1, 3)
    v2_out(0, 3)
    vy(1, 1).start()
    vy(1, 2).start()
    v2_in(0, 1)
    for q in (0, 1):
        arrived(hs.at[0, 0, 0], vxr.at[4, q])
        for side in (0, 1):
            vx_first(q, side, 2).start()
    own_out(vx, 1)
    v2_in(0, 2)
    own_out(vx, 2)
    v2_in(1, 3)
    vy(1, 3).start()
    for s in (2, 3):
        for d in (1, 3, 2):
            vy(s, d).start()

    arrived(t2.at[:, 0], tr.at[0])

    def h_own(c):
        chip = y * 2 + zh
        return pltpu.make_async_copy(hs.at[c, chip], hr.at[c, :, chip], hrr.at[stage(c)])

    def h_side(c, s, mine):
        source = moved(p, y=0 if mine else -s)["y"] * 2 + zh
        return remote(
            hs.at[c, lax.rem(y + s, 4) * 2 + zh], hr.at[c, :, source], sent.at[HD], hrr.at[stage(c)], moved(p, y=s)
        )

    def h_cross(c, s, mine):
        if isinstance(s, int) and s == 0:
            dst, sem = hr.at[c, :, y * 2 + (zh if mine else 1 - zh)], hrr.at[stage(c)]
        else:
            dst, sem = hz.at[c, s - 1], hur.at[stage(c), s]
        return remote(hs.at[c, lax.rem(y + s, 4) * 2 + 1 - zh], dst, sent.at[HC], sem, moved(p, z=2))

    def h_pass(c, s, mine):
        source = moved(p, y=0 if mine else -s)["y"] * 2 + 1 - zh
        return remote(hz.at[c, s - 1], hr.at[c, :, source], sent.at[HP], hrr.at[stage(c)], moved(p, y=s))

    def h_on(chunks, s):
        arrived(hz.at[0, pl.ds(0, len(chunks))], hur.at[stage(chunks[0]), s])
        for c in chunks:
            h_pass(c, s, True).start()

    def first(c0, chunks, n):
        pair = lax.rem(y + turn(n), 4)
        rhs = jnp.concatenate([gvb[q, pair].reshape(2048, 128) for q in range(2)], axis=1)
        lhs = t2[pl.ds(c0 * 2, chunks * 2)].reshape(chunks * 512, 2048)
        h = jnp.dot(lhs, rhs, preferred_element_type=F32).astype(BF)
        for m in range(chunks):
            for q in range(2):
                hs[c0 + m, pair * 2 + q] = h[m * 512:(m + 1) * 512, q * 128:(q + 1) * 128].reshape(2, 256, 128)

    def first_own(c, carry):
        @pl.when(c == 2)
        def _():
            pass_on(vx, 1)
            v2_in(0, 3)
            own_out(vx, 3)

        first(c, 1, 0)
        h_cross(c, 0, True).start()
        h_own(c).start()
        return carry

    def first_early(n, carry):
        @pl.when(n == 1)
        def _():
            pass_on(vx, 2)

        @pl.when(n == 2)
        def _():
            pass_on(vx, 3)
            arrived(got.at[0, pl.ds(0, 3), 0, 0], o2r.at[0])
            own_out(o3, 0)
            own_out(o3, 1)

        rest_in(vx, n)
        vy_in(n)
        first(0, 2, n)
        for c in (0, 1):
            h_cross(c, turn(n), True).start()
            h_side(c, turn(n), True).start()
        return carry

    def first_late(n, carry):
        @pl.when(n == 1)
        def _():
            h_on((0, 1), 1)
            pass_on(o3, 0)
            own_out(o3, 2)

        @pl.when(n == 3)
        def _():
            h_on((0, 1), 3)

        first(2, 2, n)
        h_cross(2, turn(n), True).start()
        return carry

    rest_in(vx, 0)
    vy_in(0)
    lax.fori_loop(0, NC, first_own, 0)
    lax.fori_loop(1, 4, first_early, 0)
    lax.fori_loop(1, 4, first_late, 0)

    for s in (1, 3, 2):
        h_cross(3, s, True).start()
    pass_on(o3, 1)
    own_out(o3, 3)
    h_on((0, 1), 2)
    for s in (1, 3, 2):
        h_side(2, s, True).start()
    rest_in(o3, 0)
    pass_on(o3, 2)
    h_on((2,), 1)
    rest_in(o3, 1)
    h_on((2,), 3)
    pass_on(o3, 3)

    whole = pl.ds(0, 256)

    def s_slot(c, at, rows):
        return out.at[pl.ds((lax.rem(at["z"], 2) * 4 + at["x"]) * 8 + c * 2, 2), rows]

    def s_straight(c, rows):
        return remote(ss.at[c, x, 1, :, rows], s_slot(c, p, rows), sent.at[SC], srr.at[0], flip(p, "z"))

    def s_out(c, d, rows, part):
        block = ss.at[c, lax.rem(x + d, 4)]

        def stay():
            pltpu.make_async_copy(block.at[0, :, rows], s_slot(c, p, rows), srr.at[0]).start()
            if isinstance(d, int):
                s_straight(c, rows).start()

        def leave():
            s_cross(c, d, rows, part).start()
            remote(block.at[0, :, rows], s_slot(c, p, rows), sent.at[SD], srr.at[0], moved(p, x=d)).start()

        if isinstance(d, int):
            leave() if d else stay()
        else:
            pl.when(d == 0)(stay)
            pl.when(d > 0)(leave)

    def s_cross(c, d, rows, part):
        return remote(
            ss.at[c, lax.rem(x + d, 4), 1, :, rows], sz.at[c, d - 1, :, rows], sent.at[SC], zr.at[part, d], flip(p, "z")
        )

    def s_on(chunks, d, rows, part):
        arrived(sz.at[pl.ds(0, len(chunks)), 0, :, rows], zr.at[part, d])
        for c in chunks:
            remote(
                sz.at[c, d - 1, :, rows], s_slot(c, flip(p, "z"), rows), sent.at[SP], srr.at[0], moved(p, x=d)
            ).start()

    def s_on_early(part):
        for i in range(3):
            s_on((0, 1), far_first(i), pl.ds(*EARLY_ROWS[part]), part)

    def lined_up(c, q):
        rows = []
        for b in range(16):
            for j in range(4):
                n = (b // 2) * 8 + j * 2 + b % 2
                rows.append(hr[c, q, n // 8, (n % 8) * 32:(n % 8) * 32 + 32, :])
        return jnp.concatenate(rows, axis=0)

    def second(chunks, rows_of):
        lhs = jnp.concatenate(
            [
                jnp.concatenate(
                    [
                        rows_of(got.at[b // 8, (b // 2) % 4, b % 2, zl if e == 0 else 1 - zl]).reshape(256, 128)
                        for b in range(16)
                    ],
                    axis=1,
                )
                for e in (0, 1)
            ],
            axis=0,
        )
        rhs = jnp.concatenate([lined_up(c, q) for c in chunks for q in range(2)], axis=1)
        return jnp.dot(lhs, rhs, preferred_element_type=F32).astype(BF)

    arrived(hr.at[pl.ds(0, 2)], hrr.at[0])

    def second_early(t, carry):
        @pl.when(t == 2)
        def _():
            h_on((2,), 2)
            for s in (1, 3, 2):
                h_side(3, s, True).start()
            h_on((3,), 1)
            rest_in(o3, 2)

        @pl.when(t == 3)
        def _():
            rest_in(o3, 3)
            h_on((3,), 3)

        o4_in(t)
        r = second((0, 1), lambda ref: ref[:, t])
        rows = pl.ds(pl.multiple_of(t * 64, 64), 64)
        for c in (0, 1):
            for owner in range(4):
                for e in (0, 1):
                    at = e * 256 + owner * 64
                    for q in range(2):
                        ss[c, owner, e, q, rows] = r[at:at + 64, (c * 2 + q) * 128:(c * 2 + q + 1) * 128]

        for part, (start, size) in enumerate(EARLY_ROWS):

            @pl.when(t == part + 1)
            def _():
                for i in range(4):
                    for c in (0, 1):
                        s_out(c, far_first(i), pl.ds(start, size), part)

        return carry

    lax.fori_loop(0, 4, second_early, 0)
    h_on((3,), 2)

    def second_late(c, carry):
        arrived(hr.at[c], hrr.at[c - 1])

        def tile(i, inner):
            d = far_first(i)
            owner = lax.rem(x + d, 4)
            r = second((c,), lambda ref: ref[owner])
            for e in (0, 1):
                for q in range(2):
                    ss[c, owner, e, q] = r[e * 256:(e + 1) * 256, q * 128:(q + 1) * 128]
            s_out(c, d, whole, c + 1)
            return inner

        lax.fori_loop(0, 4, tile, 0)

        @pl.when(c == 3)
        def _():
            s_straight(2, whole).start()
            s_straight(3, whole).start()

        @pl.when(c == 2)
        def _():
            s_on_early(0)

        @pl.when(c == 3)
        def _():
            s_on_early(1)
            s_on_early(2)

        return carry

    lax.fori_loop(2, 4, second_late, 0)

    def s_on_late(i, carry):
        s_on((2 + i // 3,), far_first(lax.rem(i, 3)), whole, 3 + i // 3)
        return carry

    lax.fori_loop(0, 6, s_on_late, 0)

    arrived(out, srr.at[0])
    for sem, ref in (
        (TS, t2), (V1, t2.at[0, 0, pl.ds(0, 112)]), (V2, t2.at[pl.ds(0, 3), 0]),
        (VX, t2.at[pl.ds(0, 6)]), (HC, t2.at[:, 0]), (HD, t2.at[pl.ds(0, 6)]),
    ):
        arrived(ref, sent.at[sem])


def restack(source, out, target, out_sem):
    parts = out_sem.shape[0]
    lams = out.shape[0] // parts
    to = lax.broadcasted_iota(jnp.int32, (256, 256), 0)
    frm = lax.broadcasted_iota(jnp.int32, (256, 256), 1)
    one_hot = ((to // 16 == lax.rem(frm, 16)) & (lax.rem(to, 16) == frm // 16)).astype(BF)
    stores = []
    for i in range(parts):
        for base in range(i * lams, (i + 1) * lams, 32):
            at = [slice(base + h * 16, base + h * 16 + 16) for h in range(2)]
            for group in range(source.shape[0] // 16):
                ps = slice(group * 16, group * 16 + 16)
                rows = jnp.concatenate([source[ps, at[h], :].reshape(256, 128) for h in range(2)], axis=1)
                moved_rows = jnp.dot(one_hot, rows, preferred_element_type=F32).astype(BF)
                for h in range(2):
                    target[at[h], ps, :] = moved_rows[:, h * 128:(h + 1) * 128].reshape(16, 16, 128)
        some = pl.ds(i * lams, lams)
        stores.append(pltpu.make_async_copy(target.at[some], out.at[some], out_sem.at[i]))
        stores[-1].start()
    for store in stores:
        store.wait()


def per_device(three_centre, green_virt, green_occ, pattern, block_sizes, atom_order):
    vmem = pl.BlockSpec(memory_space=pltpu.VMEM)
    anywhere = pl.BlockSpec(memory_space=pl.ANY)
    dma = pltpu.SemaphoreType.DMA
    blocks = pl.pallas_call(
        kernel,
        out_shape=pltpu.VMEM((64, 256, 128), BF),
        in_specs=[vmem, vmem, pl.BlockSpec(memory_space=pltpu.SMEM), vmem, vmem, anywhere],
        out_specs=vmem,
        scratch_shapes=[
            pltpu.VMEM((4, 16, 16, 128), F32),
            pltpu.VMEM((2, 2, 4, 16, 128), BF),
            pltpu.VMEM((2, 4, 2, 4, 4, 2, 32, 128), BF),
            pltpu.VMEM((8, 2, 128, 2048), BF),
            pltpu.VMEM((128, 2048), BF),
            pltpu.VMEM((NC, 8, 2, 256, 128), BF),
            pltpu.VMEM((NC, 3, 2, 256, 128), BF),
            pltpu.VMEM((NC, 2, 8, 256, 128), BF),
            pltpu.VMEM((8, 16, 1024), BF),
            pltpu.VMEM((2, 4, 2, 2, 4, 4, 64, 128), BF),
            pltpu.VMEM((NC, 4, 2, 2, 256, 128), BF),
            pltpu.VMEM((NC, 3, 2, 256, 128), BF),
            dma((NC,)), dma((3,)), dma((6,)), dma((1,)), dma((2,)), dma((2, 4)), dma((4,)), dma((5, 2)),
            dma((1,)), dma((1,)), dma((4, 2)), dma((4,)), dma((3, 4)), dma((3,)), dma((5, 4)), dma((1,)),
        ],
        compiler_params=pltpu.CompilerParams(
            collective_id=0, has_side_effects=True, vmem_limit_bytes=56 * 2**20
        ),
        name="contract",
    )(green_virt, green_occ, atom_order, block_sizes.reshape(1, -1), pattern, three_centre)
    return pl.pallas_call(
        restack,
        out_shape=jax.ShapeDtypeStruct((256, 64, 128), BF),
        in_specs=[vmem],
        out_specs=anywhere,
        scratch_shapes=[pltpu.VMEM((256, 64, 128), BF), dma((4,))],
        compiler_params=pltpu.CompilerParams(vmem_limit_bytes=40 * 2**20),
        name="restack",
    )(blocks)


def solution(mesh):
    in_specs = (P("row", "col", None), P(("row", "col"), None), P(("row", "col"), None), P(), P(), P())
    return jax.shard_map(
        per_device, mesh=mesh, in_specs=in_specs, out_specs=P("row", None, "col"), check_vma=False
    )
```
